32 devices in a mesh: fsdp: 8 (over y, x, core), seq: 4 (over z).
Axes of the slice: x: 2, y: 2, z: 4, core: 2. Of those that a mesh axis runs over, the one named last changes fastest.
Arguments:
- frames: bfloat16 [16, 1500, 768], P('fsdp', 'seq'), may hold values from -6 to 6
- cotangent: bfloat16 [16, 1500, 768], P('fsdp', 'seq'), may hold values from -6 to 6
- valid_slots: int32 [16], P('fsdp'), may hold values 0 or 1
- first_gain: bfloat16 [768], P('fsdp'), may hold values from 0.25 to 1.75
- first_shift: bfloat16 [768], P('fsdp'), may hold values from -3 to 3
- query_weight: bfloat16 [768, 768], P('fsdp'), may hold values from -0.21875 to 0.21875
- query_bias: bfloat16 [768], P('fsdp'), may hold values from -3 to 3
- key_weight: bfloat16 [768, 768], P('fsdp'), may hold values from -0.21875 to 0.21875
- value_weight: bfloat16 [768, 768], P('fsdp'), may hold values from -0.21875 to 0.21875
- value_bias: bfloat16 [768], P('fsdp'), may hold values from -3 to 3
- output_weight: bfloat16 [768, 768], P('fsdp'), may hold values from -6 to 6
- output_bias: bfloat16 [768], P('fsdp'), may hold values from -3 to 3
- second_gain: bfloat16 [768], P('fsdp'), may hold values from 0.25 to 1.75
- second_shift: bfloat16 [768], P('fsdp'), may hold values from -3 to 3
- inner_weight: bfloat16 [768, 3072], P('fsdp'), may hold values from -0.21875 to 0.21875
- inner_bias: bfloat16 [3072], P('fsdp'), may hold values from -3 to 3
- outer_weight: bfloat16 [3072, 768], P('fsdp'), may hold values from -0.21875 to 0.21875
- outer_bias: bfloat16 [768], P('fsdp'), may hold values from -3 to 3
Outputs:
- outputs: bfloat16 [16, 1500, 768], P('fsdp', 'seq')
- input_grad: bfloat16 [16, 1500, 768], P('fsdp', 'seq')
- grad_first_gain: float32 [768], P('fsdp')
- grad_first_shift: float32 [768], P('fsdp')
- grad_query_weight: float32 [768, 768], P('fsdp')
- grad_query_bias: float32 [768], P('fsdp')
- grad_key_weight: float32 [768, 768], P('fsdp')
- grad_value_weight: float32 [768, 768], P('fsdp')
- grad_value_bias: float32 [768], P('fsdp')
- grad_output_weight: float32 [768, 768], P('fsdp')
- grad_output_bias: float32 [768], P('fsdp')
- grad_second_gain: float32 [768], P('fsdp')
- grad_second_shift: float32 [768], P('fsdp')
- grad_inner_weight: float32 [768, 3072], P('fsdp')
- grad_inner_bias: float32 [3072], P('fsdp')
- grad_outer_weight: float32 [3072, 768], P('fsdp')
- grad_outer_bias: float32 [768], P('fsdp')
The draws below stay inside these ranges and needn't reach their ends.
All inputs are finite; a program needn't handle non-finite values. No bound on the sum of `valid_slots` on one device may be relied on, other than what follows from the above.
Results may differ from the reference program's by a relative error of at most 0.012.
The reference program's roundings to bfloat16 on the way count: a program that leaves them out, or rounds other values in their place, can miss the bound.
Values may be sent and summed in bfloat16 or wider, within the bound.
A program may use at most 256 MiB of HBM per device.

```python
import jax
import jax.numpy as jnp
from jax import lax

D = 768
H = 12
HD = 64
FF = 3072
L = 1500
SLOTS = 16


def touch_ends(array, own_key, low, largest):
    place = [jax.random.randint(jax.random.fold_in(own_key, axis), (), 0, length) for axis, length in enumerate(array.shape)]
    main_axis = array.shape.index(max(array.shape))
    neighbour = place[:main_axis] + [(place[main_axis] + 1) % array.shape[main_axis]] + place[main_axis + 1:]
    return array.at[tuple(place)].set(low).at[tuple(neighbour)].set(largest)


def strengthened(array, rng, source, target, shards_of, factor):
    owner, partner = [(jnp.arange(array.shape[axis_at]) // (array.shape[axis_at] // shards_of)).reshape([-1 if axis == axis_at else 1 for axis in range(array.ndim)]) for axis_at in (source, target)]
    chosen = jax.random.permutation(rng, shards_of)[partner]
    strong = (owner == chosen) | (owner == (partner + shards_of // 2) % shards_of)
    return jnp.where(strong, factor * array, array)


def block_scale(key, dims, pieces, smallest, top_value):
    def one(axis_at, shards_of):
        steps = jax.random.uniform(jax.random.fold_in(jax.random.fold_in(key, 6), axis_at), (shards_of,), jnp.float32, smallest / len(pieces), top_value / len(pieces))
        return jnp.repeat(jnp.exp(steps), dims[axis_at] // shards_of).reshape((-1,) + (1,) * (len(dims) - axis_at - 1))

    level = one(*pieces[0])
    for cut in pieces[1:]:
        level = level * one(*cut)
    return level


def scatter_about(key, dims, deviation, reach, split=(), kind=jnp.bfloat16):
    array = deviation * jax.random.normal(key, dims, jnp.float32)
    if split:
        array = array * block_scale(key, dims, split, -0.22, 0.18)
    return jnp.clip(array, -reach, reach).astype(kind)


def gaussian_with(own_key, extent, spread, limit, split, heavy, dtype=jnp.bfloat16):
    entries = spread * jax.random.normal(own_key, extent, jnp.float32)
    if split:
        entries = entries * block_scale(own_key, extent, split, -0.22, 0.18)
    return jnp.clip(strengthened(entries, jax.random.fold_in(own_key, 3), *heavy), -limit, limit).astype(dtype)


def setup_inputs(seed: int = 0) -> dict:
    key_of = jax.random.split(jax.random.key(seed), 19)
    frames = gaussian_with(key_of[0], (SLOTS, L, D), 1.0, 6.0, ((0, 8), (1, 4)), (0, 2, 8, 2.0))
    cotangent = scatter_about(key_of[1], (SLOTS, L, D), 1.0, 6.0, ((0, 8), (1, 4)))
    valid_slots = touch_ends((jax.random.randint(key_of[2], (SLOTS,), 0, 3) < 2).astype(jnp.int32), jax.random.fold_in(key_of[2], 1), 0, 1)
    first_gain = jnp.clip(1.0 + 0.15 * jax.random.normal(key_of[3], (D,), jnp.float32), 0.25, 1.75).astype(jnp.bfloat16)
    first_shift = scatter_about(key_of[4], (D,), 0.5, 3.0, ((0, 8),))
    query_weight = scatter_about(key_of[5], (D, D), D ** -0.5, 0.21875, ((0, 8),))
    query_bias = scatter_about(key_of[6], (D,), 0.5, 3.0, ((0, 8),))
    key_weight = scatter_about(key_of[7], (D, D), D ** -0.5, 0.21875, ((0, 8),))
    value_weight = scatter_about(key_of[8], (D, D), D ** -0.5, 0.21875, ((0, 8),))
    value_bias = scatter_about(key_of[9], (D,), 0.5, 3.0, ((0, 8),))
    output_weight = scatter_about(key_of[10], (D, D), (max(1, D // L)) ** -0.5, 6.0, ((0, 8),))
    output_bias = scatter_about(key_of[11], (D,), 0.5, 3.0, ((0, 8),))
    second_gain = jnp.clip(1.0 + 0.15 * jax.random.normal(key_of[12], (D,), jnp.float32), 0.25, 1.75).astype(jnp.bfloat16)
    second_shift = scatter_about(key_of[13], (D,), 0.5, 3.0, ((0, 8),))
    inner_weight = scatter_about(key_of[14], (D, FF), D ** -0.5, 0.21875, ((0, 8),))
    inner_bias = scatter_about(key_of[15], (FF,), 0.5, 3.0, ((0, 8),))
    outer_weight = scatter_about(key_of[16], (FF, D), (FF // 4) ** -0.5, 0.21875, ((0, 8),))
    outer_bias = scatter_about(key_of[17], (D,), 0.5, 3.0, ((0, 8),))
    return dict(frames=frames, cotangent=cotangent, valid_slots=valid_slots, first_gain=first_gain, first_shift=first_shift, query_weight=query_weight, query_bias=query_bias, key_weight=key_weight, value_weight=value_weight, value_bias=value_bias, output_weight=output_weight, output_bias=output_bias, second_gain=second_gain, second_shift=second_shift, inner_weight=inner_weight, inner_bias=inner_bias, outer_weight=outer_weight, outer_bias=outer_bias)


@jax.custom_vjp
def low(v):
    return lax.optimization_barrier(v.astype(jnp.bfloat16)).astype(jnp.float32)

@jax.custom_vjp
def low_back(v):
    return v

def low_keep(v):
    return (low(v), None)

def low_pass(kept, grad):
    return (grad,)

def back_keep(v):
    return (v, None)

def back_low(kept, grad):
    return (low(grad),)
low.defvjp(low_keep, low_pass)
low_back.defvjp(back_keep, back_low)

def product(left, right):
    return jnp.matmul(left, right, precision=lax.Precision.HIGHEST)

def rounded_both(value):
    return low(low_back(value))

def layer_norm(rows, gain, shift):
    center = rows - lax.optimization_barrier(jnp.mean(rows, -1, keepdims=True))
    variance = lax.optimization_barrier(jnp.mean(center * center, -1, keepdims=True))
    return center * lax.rsqrt(variance + 1e-05) * gain + shift

def slot_forward(params, clip, keep):
    first_gain, first_shift, query_weight, query_bias, key_weight, value_weight, value_bias, output_weight, output_bias, second_gain, second_shift, inner_weight, inner_bias, outer_weight, outer_bias = params
    length = clip.shape[0]
    normed1 = low(layer_norm(clip, first_gain, first_shift))
    query = rounded_both(product(normed1, query_weight) + query_bias).reshape(length, H, HD)
    keys = rounded_both(product(normed1, key_weight)).reshape(length, H, HD)
    values = rounded_both(product(normed1, value_weight) + value_bias).reshape(length, H, HD)
    scores = low_back(jnp.einsum('qhd,khd->hqk', query, keys, precision=lax.Precision.HIGHEST) * HD ** (-0.5))
    probs = low(jax.nn.softmax(scores, axis=-1))
    mixed = jnp.einsum('hqk,khd->qhd', probs, values, precision=lax.Precision.HIGHEST).reshape(length, H * HD)
    mixed = rounded_both(mixed)
    branch = low_back(product(mixed, output_weight) + output_bias)
    resid = clip + branch
    normed2 = low(layer_norm(resid, second_gain, second_shift))
    inner = low_back(product(normed2, inner_weight) + inner_bias)
    active = low(jax.nn.gelu(inner, approximate=False))
    return (resid + product(active, outer_weight) + outer_bias) * keep

def reference(frames, cotangent, valid_slots, first_gain, first_shift, query_weight, query_bias, key_weight, value_weight, value_bias, output_weight, output_bias, second_gain, second_shift, inner_weight, inner_bias, outer_weight, outer_bias):
    params = tuple((p.astype(jnp.float32) for p in (first_gain, first_shift, query_weight, query_bias, key_weight, value_weight, value_bias, output_weight, output_bias, second_gain, second_shift, inner_weight, inner_bias, outer_weight, outer_bias)))
    keep = valid_slots.astype(jnp.float32)
    inputs = frames.astype(jnp.float32)
    step_fn = jax.checkpoint(slot_forward)

    def whole(params_now, inputs_now):

        def one(carry, item):
            return (carry, step_fn(params_now, item[0], item[1]))
        _, results = lax.scan(one, jnp.zeros((), jnp.float32), (inputs_now, keep))
        return results
    results, pull = jax.vjp(whole, params, inputs)
    grad_params, grad_inputs = pull(cotangent.astype(jnp.float32))
    return (results.astype(jnp.bfloat16), grad_inputs.astype(jnp.bfloat16), grad_params[0], grad_params[1], grad_params[2], grad_params[3], grad_params[4], grad_params[5], grad_params[6], grad_params[7], grad_params[8], grad_params[9], grad_params[10], grad_params[11], grad_params[12], grad_params[13], grad_params[14])
```

```python
import math

import jax
import jax.numpy as jnp
from jax import lax
from jax.experimental import pallas as pl
from jax.experimental.pallas import tpu as pltpu
from jax.sharding import PartitionSpec as P

H = 12
HD = 64
EPS = 1e-05
MESH = pl.DeviceIdType.MESH
F32 = jnp.float32
BF16 = jnp.bfloat16
ANY = pl.BlockSpec(memory_space=pl.ANY)
VMEM = pl.BlockSpec(memory_space=pltpu.VMEM)
LIMIT = 60 << 20
QB = 256


def nn(a, b):
    return lax.dot_general(a, b, (((1,), (0,)), ((), ())), preferred_element_type=F32)


def nt(a, b):
    return lax.dot_general(a, b, (((1,), (1,)), ((), ())), preferred_element_type=F32)


def tn(a, b):
    return lax.dot_general(a, b, (((0,), (0,)), ((), ())), preferred_element_type=F32)


def normalize(rows):
    center = rows - jnp.mean(rows, -1, keepdims=True)
    inv = lax.rsqrt(jnp.mean(center * center, -1, keepdims=True) + EPS)
    return center * inv, inv


def norm_back(grad, gain, hat, inv):
    tilted = grad * gain
    first = jnp.mean(tilted, -1, keepdims=True)
    cross = jnp.mean(tilted * hat, -1, keepdims=True)
    return inv * (tilted - first - hat * cross)


def where_am_i():
    f = lax.axis_index("fsdp")
    z = lax.axis_index("seq")
    return f, z, f // 2, f % 2


def meet(peers):
    barrier = pltpu.get_barrier_semaphore()
    for peer in peers:
        pl.semaphore_signal(barrier, inc=1, device_id=peer, device_id_type=MESH)
    pl.semaphore_wait(barrier, len(peers))


def column_peers(seq):
    f, z, m, c = where_am_i()
    peers = []
    for dc in range(2):
        for dz in range(seq):
            if dc or dz:
                peers.append((m * 2 + (c + dc) % 2, (z + dz) % seq))
    return peers


class Ship:
    def __init__(self, src, dst, send, recv, target):
        f, z, _, _ = where_am_i()
        self.here = jnp.logical_and(target[0] == f, target[1] == z)
        self.local = pltpu.make_async_copy(src, dst, recv)
        self.remote = pltpu.make_async_remote_copy(
            src, dst, send, recv, device_id=target, device_id_type=MESH
        )

    def start(self):
        pl.when(self.here)(self.local.start)
        pl.when(jnp.logical_not(self.here))(self.remote.start)

    def wait_send(self):
        pl.when(jnp.logical_not(self.here))(self.remote.wait_send)


def remote(src, dst, send, recv, target):
    return pltpu.make_async_remote_copy(
        src, dst, send, recv, device_id=target, device_id_type=MESH
    )


class Gather:
    def __init__(self, send_ref, full_ref, send_sem, recv_sem, pass_send, pass_recv, seq):
        f, z, m, c = where_am_i()
        self.ships = []
        for i in range(2):
            for h in range(2):
                slot = 2 * c + i
                self.ships.append(
                    Ship(
                        send_ref.at[i, h],
                        full_ref.at[z, h],
                        send_sem.at[i, h],
                        recv_sem.at[z],
                        (m * 2 + h, slot),
                    )
                )
        other = (m * 2 + 1 - c, z)
        self.arrivals = [
            remote(send_ref.at[0, 0], full_ref.at[k, c], send_sem.at[0, 0], recv_sem.at[k], other)
            for k in range(seq)
        ]
        self.passes = [
            remote(full_ref.at[k, c], full_ref.at[k, c], pass_send.at[k], pass_recv.at[k], other)
            for k in range(seq)
        ]
        self.handed = [
            remote(
                full_ref.at[k, c], full_ref.at[k, 1 - c], pass_send.at[k], pass_recv.at[k], other
            )
            for k in range(seq)
        ]

    def start(self):
        for ship in self.ships:
            ship.start()

    def hand_on(self, k):
        self.arrivals[k].wait_recv()
        self.passes[k].start()

    def ready(self, k):
        self.handed[k].wait_recv()

    def finish(self):
        for ship in self.ships:
            ship.wait_send()
        for item in self.passes:
            item.wait_send()


GATHER_SEMS = lambda seq: [
    pltpu.SemaphoreType.DMA((2, 2)),
    pltpu.SemaphoreType.DMA((seq,)),
    pltpu.SemaphoreType.DMA((seq,)),
    pltpu.SemaphoreType.DMA((seq,)),
]


class Return:
    def __init__(self, own_ref, back_ref, send_sem, recv_sem, seq):
        f, z, m, c = where_am_i()
        home = z // 2
        self.ships = [
            Ship(
                own_ref.at[k],
                back_ref.at[z % 2, c],
                send_sem.at[k],
                recv_sem.at[z % 2, c],
                (m * 2 + home, k),
            )
            for k in range(seq)
        ]
        self.arrivals = [
            remote(
                own_ref.at[0],
                back_ref.at[i, h],
                send_sem.at[0],
                recv_sem.at[i, h],
                (m * 2 + 1 - c, z),
            )
            for i in range(2)
            for h in range(2)
        ]

    def start(self):
        for ship in self.ships:
            ship.start()

    def finish(self):
        for ship in self.ships:
            ship.wait_send()
        for item in self.arrivals:
            item.wait_recv()


RETURN_SEMS = lambda seq: [pltpu.SemaphoreType.DMA((seq,)), pltpu.SemaphoreType.DMA((2, 2))]


def own_lanes(parity):
    lane = lax.broadcasted_iota(jnp.int32, (1, 128), 1)
    return (lane // HD) == parity, lane == HD * (1 - parity)


def project_kernel(
    seq, x_send, wqkv, vecs, x_full, n1_out, q_out, k_out, v_out, ssem, rsem, psend, precv, xv, lsem
):
    f, z, m, c = where_am_i()
    meet(column_peers(seq))
    gather = Gather(x_send, x_full, ssem, rsem, psend, precv, seq)
    gather.start()
    half = xv.shape[1]
    width = q_out.shape[1]
    for k in range(seq):
        gather.hand_on(k)
    gain = vecs[0:1, :]
    shift = vecs[1:2, :]
    cols = pl.ds(pl.multiple_of(c * width, 128), width)
    qb = vecs[2:3, cols]
    vb = vecs[3:4, cols]

    for k in range(seq):
        gather.ready(k)
        copy = pltpu.make_async_copy(x_full.at[k], xv, lsem)
        copy.start()
        copy.wait()
        rows = pl.ds(k * 2 * half, 2 * half)
        hat, _ = normalize(xv[...].reshape(2 * half, -1).astype(F32))
        normed = (hat * gain + shift).astype(BF16)
        n1_out[rows, :] = normed
        qkv = nn(normed, wqkv[...])
        q_out[rows, :] = (qkv[:, :width] + qb).astype(BF16)
        k_out[rows, :] = qkv[:, width : 2 * width].astype(BF16)
        v_out[rows, :] = (qkv[:, 2 * width :] + vb).astype(BF16)
    gather.finish()


def project(x_send, wqkv, vecs, seq):
    _, _, half, width = x_send.shape
    rows = seq * 2 * half
    mine = wqkv.shape[1] // 3
    return pl.pallas_call(
        lambda *refs: project_kernel(seq, *refs),
        in_specs=[ANY, VMEM, VMEM],
        out_specs=[ANY, VMEM, VMEM, VMEM, VMEM],
        out_shape=[
            jax.ShapeDtypeStruct((seq, 2, half, width), BF16),
            jax.ShapeDtypeStruct((rows, width), BF16),
        ]
        + [jax.ShapeDtypeStruct((rows, mine), BF16)] * 3,
        scratch_shapes=GATHER_SEMS(seq)
        + [pltpu.VMEM((2, half, width), BF16), pltpu.SemaphoreType.DMA],
        compiler_params=pltpu.CompilerParams(
            collective_id=0, has_side_effects=True, vmem_limit_bytes=LIMIT
        ),
        name="project",
    )(x_send, wqkv, vecs)


def attend_kernel(
    seq, local, heads, cot_send, q, k, v, e_out, o_out, linv_out, mixed_out, cot_full,
    ssem, rsem, psend, precv, stage, ka, va, msend, mrecv, mlocal,
):
    f, z, m, c = where_am_i()
    h = pl.program_id(0)
    pair = h // 2
    parity = h % 2
    rows = q.shape[0]
    gather = Gather(cot_send, cot_full, ssem, rsem, psend, precv, seq)
    other = (m * 2 + 1 - c, z)

    @pl.when(h == 0)
    def _():
        meet(column_peers(seq))
        gather.start()

    mine, first = own_lanes(parity)
    place = lax.broadcasted_iota(jnp.int32, (rows, 1), 0) % (rows // seq)
    bar = jnp.where(place < local, 0.0, -1e38).astype(F32)
    ka[...] = jnp.where(mine, k[...].astype(F32), jnp.where(first, bar, 0.0)).astype(BF16)
    va[...] = jnp.where(mine, v[...].astype(F32), jnp.where(first, 1.0, 0.0)).astype(BF16)
    factor = HD ** (-0.5) * math.log2(math.e)
    for i in range(rows // QB):
        sl = slice(i * QB, (i + 1) * QB)
        qa = jnp.where(mine, q[sl, :].astype(F32), jnp.where(first, 1.0, 0.0)).astype(BF16)
        scores = nt(qa, ka[...])
        peak = jnp.max(scores, -1, keepdims=True)
        expo = jnp.exp2((scores - peak) * factor).astype(BF16)
        e_out[0, sl, :] = expo
        raw = nn(expo, va[...])
        total = jnp.sum(jnp.where(first, raw, 0.0), -1, keepdims=True)
        inv = 1.0 / total
        res = raw * inv

        @pl.when(parity == 0)
        def _():
            o_out[sl, :] = res
            linv_out[sl, :] = jnp.broadcast_to(inv, res.shape)

        @pl.when(parity == 1)
        def _():
            both = jnp.where(mine, res, o_out[sl, :])
            o_out[sl, :] = both
            linv_out[sl, :] = jnp.where(mine, inv, linv_out[sl, :])
            stage[pair, sl, :] = both.astype(BF16)

    def mixed_copies(p):
        return (
            pltpu.make_async_copy(stage.at[p], mixed_out.at[c, p], mlocal.at[p]),
            remote(stage.at[p], mixed_out.at[c, p], msend.at[p], mrecv.at[p], other),
            remote(stage.at[p], mixed_out.at[1 - c, p], msend.at[p], mrecv.at[p], other),
        )

    @pl.when(parity == 1)
    def _():
        here, there, _ = mixed_copies(pair)
        here.start()
        there.start()

    @pl.when(h == heads - 2)
    def _():
        for item in range(seq):
            gather.hand_on(item)

    @pl.when(h == heads - 1)
    def _():
        for item in range(seq):
            gather.ready(item)
        gather.finish()
        for p in range(heads // 2):
            here, there, back = mixed_copies(p)
            here.wait()
            there.wait_send()
            back.wait_recv()


def attend(cot_send, q, k, v, local, seq):
    rows, mine = q.shape
    heads = mine // HD
    _, _, half, width = cot_send.shape
    pairs = heads // 2
    by_pair = pl.BlockSpec((rows, 128), lambda h: (0, h // 2))
    return pl.pallas_call(
        lambda *refs: attend_kernel(seq, local, heads, *refs),
        grid=(heads,),
        in_specs=[ANY, by_pair, by_pair, by_pair],
        out_specs=[
            pl.BlockSpec((1, rows, rows), lambda h: (h, 0, 0)),
            by_pair,
            by_pair,
            ANY,
            ANY,
        ],
        out_shape=[
            jax.ShapeDtypeStruct((heads, rows, rows), BF16),
            jax.ShapeDtypeStruct((rows, mine), F32),
            jax.ShapeDtypeStruct((rows, mine), F32),
            jax.ShapeDtypeStruct((2, pairs, rows, 128), BF16),
            jax.ShapeDtypeStruct((seq, 2, half, width), BF16),
        ],
        scratch_shapes=GATHER_SEMS(seq)
        + [
            pltpu.VMEM((pairs, rows, 128), BF16),
            pltpu.VMEM((rows, 128), BF16),
            pltpu.VMEM((rows, 128), BF16),
            pltpu.SemaphoreType.DMA((pairs,)),
            pltpu.SemaphoreType.DMA((pairs,)),
            pltpu.SemaphoreType.DMA((pairs,)),
        ],
        compiler_params=pltpu.CompilerParams(
            collective_id=1, has_side_effects=True, vmem_limit_bytes=LIMIT
        ),
        name="attend",
    )(cot_send, q, k, v)


def gelu_parts(u):
    x = jnp.abs(u) * (1.0 / math.sqrt(2.0))
    t = 1.0 / (1.0 + 0.3275911 * x)
    poly = t * (
        0.254829592
        + t * (-0.284496736 + t * (1.421413741 + t * (-1.453152027 + t * 1.061405429)))
    )
    expo = jnp.exp(-x * x)
    tail = 0.5 * poly * expo
    phi = jnp.where(u >= 0, 1.0 - tail, tail)
    return phi, u * expo * (1.0 / math.sqrt(2.0 * math.pi))


def dense_kernel(
    seq, x, mixed, cot, wo, wi, wu, vecs, ibias,
    out_own, gres_own, gm_out, gwo_out, gwi_out, gwu_out, gvec_out, gib_out,
    n2, hat2, inv2, keep, gown, pstage, precv, gstage, grecv, psem, prsem, gsem, grsem,
):
    f, z, m, c = where_am_i()
    other = (m * 2 + 1 - c, z)
    meet([other])
    half = x.shape[2]
    chunk = 2 * half
    width = x.shape[3]
    mine = gm_out.shape[1]
    obias, gain, shift, ubias = vecs[4:5, :], vecs[5:6, :], vecs[6:7, :], vecs[7:8, :]
    gvec_out[...] = jnp.zeros_like(gvec_out)
    gib_out[...] = jnp.zeros_like(gib_out)
    gwo_out[...] = jnp.zeros_like(gwo_out)
    gwi_out[...] = jnp.zeros_like(gwi_out)
    gwu_out[...] = jnp.zeros_like(gwu_out)

    def p_copy(i):
        return remote(pstage.at[i], precv.at[i], psem.at[i], prsem.at[i], other)

    def g_copy(i):
        return remote(gstage.at[i], grecv.at[i], gsem.at[i], grsem.at[i], other)

    def mixed_rows(i):
        rows = pl.ds(i * chunk, chunk)
        return jnp.concatenate(
            [mixed[a, p, rows, :] for a in range(2) for p in range(mixed.shape[1])], axis=1
        )

    def first(i, _):
        rows = pl.ds(i * chunk, chunk)
        resid = (
            x[i].reshape(chunk, width).astype(F32) + nn(mixed_rows(i), wo[...]) + obias
        )
        hat, inv = normalize(resid)
        normed = (hat * gain + shift).astype(BF16)
        n2[rows, :] = normed
        hat2[rows, :] = hat
        inv2[rows, :] = jnp.broadcast_to(inv, (chunk, 128))
        inner = nn(normed, wi[...]) + ibias[...]
        phi, bump = gelu_parts(inner)
        active = (inner * phi).astype(BF16)
        slope = phi + bump
        pout = nn(active, wu[...])
        full = resid + ubias

        @pl.when(c == 0)
        def _():
            keep[i] = full[:half] + pout[:half]
            pstage[i] = pout[half:]

        @pl.when(c == 1)
        def _():
            keep[i] = full[half:] + pout[half:]
            pstage[i] = pout[:half]

        p_copy(i).start()
        g = cot[i].reshape(chunk, width)
        gi = (nt(g, wu[...]) * slope).astype(BF16)
        gn2 = nt(gi, wi[...])
        gown[i] = gn2
        gstage[i] = gn2.astype(gstage.dtype)
        g_copy(i).start()
        gwu_out[...] += tn(active, g)
        gwi_out[...] += tn(normed, gi)
        gib_out[...] += jnp.sum(gi.astype(F32), 0, keepdims=True)
        gvec_out[0:1, :] += jnp.sum(g.astype(F32), 0, keepdims=True)
        return 0

    def second(i, _):
        rows = pl.ds(i * chunk, chunk)
        g_copy(i).wait_recv()
        gn2 = gown[i] + grecv[i].astype(F32)
        hat = hat2[rows, :]
        gvec_out[1:2, :] += jnp.sum(gn2 * hat, 0, keepdims=True)
        gvec_out[2:3, :] += jnp.sum(gn2, 0, keepdims=True)
        g = cot[i].reshape(chunk, width).astype(F32)
        gres = g + norm_back(gn2, gain, hat, inv2[rows, 0:1])
        branch = gres.astype(BF16)
        gvec_out[3:4, :] += jnp.sum(branch.astype(F32), 0, keepdims=True)
        wrows = pl.ds(pl.multiple_of(c * mine, 128), mine)
        gm_out[rows, :] = nt(branch, wo[wrows, :]).astype(BF16)
        mix = mixed_rows(i)

        @pl.when(c == 0)
        def _():
            gres_own[i] = gres[:half]
            gwo_out[...] += tn(mix, branch[:, :mine])

        @pl.when(c == 1)
        def _():
            gres_own[i] = gres[half:]
            gwo_out[...] += tn(mix, branch[:, mine:])

        p_copy(i).wait_recv()
        out_own[i] = (keep[i] + precv[i]).astype(BF16)
        return 0

    lax.fori_loop(0, seq, first, 0)
    lax.fori_loop(0, seq, second, 0)

    def last(i, _):
        p_copy(i).wait_send()
        g_copy(i).wait_send()
        return 0

    lax.fori_loop(0, seq, last, 0)


def dense(x, mixed, cot, wo, wi, wu, vecs, ibias):
    seq, _, half, width = x.shape
    rows = seq * 2 * half
    hidden = wi.shape[1]
    mine = width // 2
    return pl.pallas_call(
        lambda *refs: dense_kernel(seq, *refs),
        in_specs=[VMEM] * 8,
        out_specs=[VMEM] * 8,
        out_shape=[
            jax.ShapeDtypeStruct((seq, half, width), BF16),
            jax.ShapeDtypeStruct((seq, half, width), F32),
            jax.ShapeDtypeStruct((rows, mine), BF16),
            jax.ShapeDtypeStruct((width, mine), F32),
            jax.ShapeDtypeStruct((width, hidden), F32),
            jax.ShapeDtypeStruct((hidden, width), F32),
            jax.ShapeDtypeStruct((8, width), F32),
            jax.ShapeDtypeStruct((1, hidden), F32),
        ],
        scratch_shapes=[
            pltpu.VMEM((rows, width), BF16),
            pltpu.VMEM((rows, width), F32),
            pltpu.VMEM((rows, 128), F32),
            pltpu.VMEM((seq, half, width), F32),
            pltpu.VMEM((seq, 2 * half, width), F32),
            pltpu.VMEM((seq, half, width), F32),
            pltpu.VMEM((seq, half, width), F32),
            pltpu.VMEM((seq, 2 * half, width), BF16),
            pltpu.VMEM((seq, 2 * half, width), BF16),
            pltpu.SemaphoreType.DMA((seq,)),
            pltpu.SemaphoreType.DMA((seq,)),
            pltpu.SemaphoreType.DMA((seq,)),
            pltpu.SemaphoreType.DMA((seq,)),
        ],
        compiler_params=pltpu.CompilerParams(
            collective_id=2, has_side_effects=True, vmem_limit_bytes=LIMIT
        ),
        name="dense",
    )(x, mixed, cot, wo, wi, wu, vecs, ibias)


def attend_back_kernel(
    seq, heads, out_own, q, k, v, gm, o, linv, e, gq_out, gk_out, gv_out, out_back,
    ssem, rsem, do, dot_, qt, va, km, dqs, dvt, dkt,
):
    h = pl.program_id(0)
    parity = h % 2
    rows = q.shape[0]
    back = Return(out_own, out_back, ssem, rsem, seq)

    @pl.when(h == 0)
    def _():
        meet(column_peers(seq))
        back.start()

    mine, first = own_lanes(parity)
    third = HD ** (-0.5)
    scaled = (gm[...].astype(F32) * linv[...]).astype(BF16).astype(F32)
    scaled = jnp.where(mine, scaled, 0.0)
    delta = jnp.sum(scaled * o[...], -1, keepdims=True)
    high = delta.astype(BF16).astype(F32)
    middle = (delta - high).astype(BF16).astype(F32)
    low = delta - high - middle
    lane = lax.broadcasted_iota(jnp.int32, (1, 128), 1)
    base = HD * (1 - parity)
    do[...] = (
        scaled
        - jnp.where(lane == base, high, 0.0)
        - jnp.where(lane == base + 1, middle, 0.0)
        - jnp.where(lane == base + 2, low, 0.0)
    ).astype(BF16)
    ones = jnp.logical_and(lane >= base, lane < base + 3)
    va[...] = jnp.where(mine, v[...].astype(F32), jnp.where(ones, 1.0, 0.0)).astype(BF16)
    km[...] = jnp.where(mine, k[...].astype(F32), 0.0).astype(BF16)
    dot_[...] = do[...].T
    qt[...] = q[...].T
    sub = pl.ds(pl.multiple_of(parity * HD, HD), HD)
    for i in range(rows // QB):
        sl = slice(i * QB, (i + 1) * QB)
        p = e[0, sl, :]
        dp = nt(do[sl, :], va[...])
        ds = (p.astype(F32) * dp).astype(BF16)
        dq = nn(ds, km[...])

        @pl.when(parity == 0)
        def _():
            dqs[sl, :] = dq

        @pl.when(parity == 1)
        def _():
            gq_out[sl, :] = ((dqs[sl, :] + dq) * third).astype(BF16)

        a = nn(dot_[sub, sl], p)
        b = nn(qt[sub, sl], ds)
        if i == 0:
            dvt[sub, :] = a
            dkt[sub, :] = b
        else:
            dvt[sub, :] += a
            dkt[sub, :] += b

    @pl.when(parity == 1)
    def _():
        gv_out[...] = dvt[...].T.astype(BF16)
        gk_out[...] = (dkt[...] * third).T.astype(BF16)

    @pl.when(h == heads - 1)
    def _():
        back.finish()


def attend_back(out_own, q, k, v, gm, o, linv, e):
    rows, mine = q.shape
    heads = mine // HD
    seq, half, width = out_own.shape
    by_pair = pl.BlockSpec((rows, 128), lambda h: (0, h // 2))
    return pl.pallas_call(
        lambda *refs: attend_back_kernel(seq, heads, *refs),
        grid=(heads,),
        in_specs=[ANY] + [by_pair] * 6 + [pl.BlockSpec((1, rows, rows), lambda h: (h, 0, 0))],
        out_specs=[by_pair] * 3 + [ANY],
        out_shape=[jax.ShapeDtypeStruct((rows, mine), BF16)] * 3
        + [jax.ShapeDtypeStruct((2, 2, half, width), BF16)],
        scratch_shapes=RETURN_SEMS(seq)
        + [
            pltpu.VMEM((rows, 128), BF16),
            pltpu.VMEM((128, rows), BF16),
            pltpu.VMEM((128, rows), BF16),
            pltpu.VMEM((rows, 128), BF16),
            pltpu.VMEM((rows, 128), BF16),
            pltpu.VMEM((rows, 128), F32),
            pltpu.VMEM((128, rows), F32),
            pltpu.VMEM((128, rows), F32),
        ],
        compiler_params=pltpu.CompilerParams(
            collective_id=3, has_side_effects=True, vmem_limit_bytes=LIMIT
        ),
        name="attend_back",
    )(out_own, q, k, v, gm, o, linv, e)


def project_back_kernel(
    seq, x, n1, gq, gk, gv, gres, wqkv, vecs, gw_out, gvec_out, ig_back,
    gown, gstage, grecv, ig_own, gsem, grsem, ssem, rsem,
):
    f, z, m, c = where_am_i()
    other = (m * 2 + 1 - c, z)
    meet(column_peers(seq))
    half = x.shape[2]
    chunk = 2 * half
    width = x.shape[3]
    mine = gq.shape[1]
    gain = vecs[0:1, :]

    def g_copy(i):
        return remote(gstage.at[i], grecv.at[i], gsem.at[i], grsem.at[i], other)

    def grads(i):
        rows = pl.ds(i * chunk, chunk)
        return jnp.concatenate([gq[rows, :], gk[rows, :], gv[rows, :]], axis=1)

    gw_out[...] = jnp.zeros_like(gw_out)
    gvec_out[...] = jnp.zeros_like(gvec_out)

    def first(i, _):
        gn1 = nt(grads(i), wqkv[...])

        @pl.when(c == 0)
        def _():
            gown[i] = gn1[:half]
            gstage[i] = gn1[half:]

        @pl.when(c == 1)
        def _():
            gown[i] = gn1[half:]
            gstage[i] = gn1[:half]

        g_copy(i).start()
        return 0

    def second(i, _):
        g_copy(i).wait_recv()
        gn1 = gown[i] + grecv[i]
        hat, inv = normalize(x[i, c].astype(F32))
        gvec_out[0:1, :] += jnp.sum(gn1 * hat, 0, keepdims=True)
        gvec_out[1:2, :] += jnp.sum(gn1, 0, keepdims=True)
        ig_own[i] = (gres[i] + norm_back(gn1, gain, hat, inv)).astype(BF16)
        return 0

    lax.fori_loop(0, seq, first, 0)
    lax.fori_loop(0, seq, second, 0)
    back = Return(ig_own, ig_back, ssem, rsem, seq)
    back.start()

    def third(i, _):
        rows = pl.ds(i * chunk, chunk)
        g = grads(i)
        gw_out[...] += tn(n1[rows, :], g)
        gvec_out[2:3, :mine] += jnp.sum(g[:, :mine].astype(F32), 0, keepdims=True)
        gvec_out[3:4, :mine] += jnp.sum(g[:, 2 * mine :].astype(F32), 0, keepdims=True)
        return 0

    lax.fori_loop(0, seq, third, 0)

    def last(i, _):
        g_copy(i).wait_send()
        return 0

    lax.fori_loop(0, seq, last, 0)
    back.finish()


def project_back(x, n1, gq, gk, gv, gres, wqkv, vecs):
    seq, _, half, width = x.shape
    return pl.pallas_call(
        lambda *refs: project_back_kernel(seq, *refs),
        in_specs=[VMEM] * 8,
        out_specs=[VMEM, VMEM, ANY],
        out_shape=[
            jax.ShapeDtypeStruct(wqkv.shape, F32),
            jax.ShapeDtypeStruct((8, width), F32),
            jax.ShapeDtypeStruct((2, 2, half, width), BF16),
        ],
        scratch_shapes=[
            pltpu.VMEM((seq, half, width), F32),
            pltpu.VMEM((seq, half, width), F32),
            pltpu.VMEM((seq, half, width), F32),
            pltpu.VMEM((seq, half, width), BF16),
            pltpu.SemaphoreType.DMA((seq,)),
            pltpu.SemaphoreType.DMA((seq,)),
        ]
        + RETURN_SEMS(seq),
        compiler_params=pltpu.CompilerParams(
            collective_id=4, has_side_effects=True, vmem_limit_bytes=LIMIT
        ),
        name="project_back",
    )(x, n1, gq, gk, gv, gres, wqkv, vecs)


def per_device(
    frames,
    cotangent,
    valid_slots,
    first_gain,
    first_shift,
    query_weight,
    query_bias,
    key_weight,
    value_weight,
    value_bias,
    output_weight,
    output_bias,
    second_gain,
    second_shift,
    inner_weight,
    inner_bias,
    outer_weight,
    outer_bias,
):
    seq = lax.axis_size("seq")
    n_f = lax.axis_size("fsdp")
    f = lax.axis_index("fsdp")
    c = f % 2
    slots, local, width = frames.shape
    chunk = -(-local // 128) * 128
    half = chunk // 2
    mine = width // 2
    hidden = n_f * inner_bias.shape[0]
    piece = hidden // n_f

    def gathered(value):
        return lax.all_gather(value, "fsdp", axis=0, tiled=True)

    def my_columns(value):
        return lax.dynamic_slice_in_dim(value, c * mine, mine, axis=1)

    keep = valid_slots.astype(BF16)[:, None, None]
    pad = ((0, 0), (0, chunk - local), (0, 0))
    x_send = jnp.pad(frames, pad).reshape(slots, 2, half, width)
    cot_send = jnp.pad(cotangent * keep, pad).reshape(slots, 2, half, width)
    wqkv = jnp.concatenate(
        [my_columns(gathered(w)) for w in (query_weight, key_weight, value_weight)], axis=1
    )
    wo = gathered(output_weight)
    wi = gathered(inner_weight).reshape(width, n_f // 2, 2, piece)
    wi = lax.dynamic_index_in_dim(wi, c, 2, keepdims=False).reshape(width, hidden // 2)
    wu = gathered(outer_weight).reshape(n_f // 2, 2, piece, width)
    wu = lax.dynamic_index_in_dim(wu, c, 1, keepdims=False).reshape(hidden // 2, width)
    small = jnp.stack(
        [
            first_gain,
            first_shift,
            query_bias,
            value_bias,
            output_bias,
            second_gain,
            second_shift,
            outer_bias,
        ]
    )
    vecs = lax.all_gather(small, "fsdp", axis=1, tiled=True).astype(F32)
    ibias = gathered(inner_bias).astype(F32).reshape(n_f // 2, 2, piece)
    ibias = lax.dynamic_index_in_dim(ibias, c, 1, keepdims=False).reshape(1, hidden // 2)

    x, n1, q, k, v = project(x_send, wqkv, vecs, seq)
    e, o, linv, mixed, cot = attend(cot_send, q, k, v, local, seq)
    out_own, gres, gm, gwo, gwi, gwu, gvec_b, gib = dense(x, mixed, cot, wo, wi, wu, vecs, ibias)
    gq, gk, gv, out_back = attend_back(out_own, q, k, v, gm, o, linv, e)
    gw, gvec_a, ig_back = project_back(x, n1, gq, gk, gv, gres, wqkv, vecs)

    keep32 = valid_slots.astype(F32)[:, None, None]
    outputs = (out_back.reshape(slots, chunk, width)[:, :local].astype(F32) * keep32).astype(BF16)
    input_grad = ig_back.reshape(slots, chunk, width)[:, :local]

    def both_columns(value):
        wide = jnp.zeros((value.shape[0], 2 * mine), F32)
        return lax.dynamic_update_slice_in_dim(wide, value, c * mine, axis=1)

    def both_blocks(value, axis):
        shape = list(value.shape)
        shape[axis : axis + 1] = [n_f // 2, 1, piece]
        full = list(shape)
        full[axis + 1] = 2
        wide = jnp.zeros(full, F32)
        wide = lax.dynamic_update_slice_in_dim(wide, value.reshape(shape), c, axis=axis + 1)
        shape = list(value.shape)
        shape[axis] = hidden
        return wide.reshape(shape)

    def reduced(value):
        return lax.psum_scatter(
            lax.psum(value, "seq"), "fsdp", scatter_dimension=0, tiled=True
        )

    grads = dict(
        first_gain=gvec_a[0],
        first_shift=gvec_a[1],
        query_weight=both_columns(gw[:, :mine]),
        query_bias=both_columns(gvec_a[2:3, :mine])[0],
        key_weight=both_columns(gw[:, mine : 2 * mine]),
        value_weight=both_columns(gw[:, 2 * mine :]),
        value_bias=both_columns(gvec_a[3:4, :mine])[0],
        output_weight=both_columns(gwo),
        output_bias=0.5 * gvec_b[3],
        second_gain=0.5 * gvec_b[1],
        second_shift=0.5 * gvec_b[2],
        inner_weight=both_blocks(gwi, 1),
        inner_bias=both_blocks(gib, 1)[0],
        outer_weight=both_blocks(gwu, 0),
        outer_bias=0.5 * gvec_b[0],
    )
    return (outputs, input_grad) + tuple(reduced(value) for value in grads.values())


def solution(mesh):
    rows = P("fsdp", "seq", None)
    vector, matrix = P("fsdp"), P("fsdp", None)
    weights = (
        vector,
        vector,
        matrix,
        vector,
        matrix,
        matrix,
        vector,
        matrix,
        vector,
        vector,
        vector,
        matrix,
        vector,
        matrix,
        vector,
    )
    return jax.shard_map(
        per_device,
        mesh=mesh,
        in_specs=(rows, rows, vector) + weights,
        out_specs=(rows, rows) + weights,
        check_vma=False,
    )
```

```python
import math

import jax
import jax.numpy as jnp
from jax import lax
from jax.experimental import pallas as pl
from jax.experimental.pallas import tpu as pltpu
from jax.sharding import PartitionSpec as P

H = 12
HD = 64
EPS = 1e-05
MESH = pl.DeviceIdType.MESH
F32 = jnp.float32
BF16 = jnp.bfloat16
ANY = pl.BlockSpec(memory_space=pl.ANY)
VMEM = pl.BlockSpec(memory_space=pltpu.VMEM)
LIMIT = 62 << 20
QB = 256


def nn(a, b):
    return lax.dot_general(a, b, (((1,), (0,)), ((), ())), preferred_element_type=F32)


def nt(a, b):
    return lax.dot_general(a, b, (((1,), (1,)), ((), ())), preferred_element_type=F32)


def tn(a, b):
    return lax.dot_general(a, b, (((0,), (0,)), ((), ())), preferred_element_type=F32)


def normalize(rows):
    center = rows - jnp.mean(rows, -1, keepdims=True)
    inv = lax.rsqrt(jnp.mean(center * center, -1, keepdims=True) + EPS)
    return center * inv, inv


def norm_back(grad, gain, hat, inv):
    tilted = grad * gain
    first = jnp.mean(tilted, -1, keepdims=True)
    cross = jnp.mean(tilted * hat, -1, keepdims=True)
    return inv * (tilted - first - hat * cross)


def where_am_i():
    f = lax.axis_index("fsdp")
    z = lax.axis_index("seq")
    return f, z, f // 2, f % 2


def meet(peers):
    barrier = pltpu.get_barrier_semaphore()
    for peer in peers:
        pl.semaphore_signal(barrier, inc=1, device_id=peer, device_id_type=MESH)
    pl.semaphore_wait(barrier, len(peers))


def column_peers(seq):
    f, z, m, c = where_am_i()
    peers = []
    for dc in range(2):
        for dz in range(seq):
            if dc or dz:
                peers.append((m * 2 + (c + dc) % 2, (z + dz) % seq))
    return peers


class Ship:
    def __init__(self, src, dst, send, recv, target):
        f, z, _, _ = where_am_i()
        self.here = jnp.logical_and(target[0] == f, target[1] == z)
        self.local = pltpu.make_async_copy(src, dst, recv)
        self.remote = pltpu.make_async_remote_copy(
            src, dst, send, recv, device_id=target, device_id_type=MESH
        )

    def start(self):
        pl.when(self.here)(self.local.start)
        pl.when(jnp.logical_not(self.here))(self.remote.start)

    def wait_send(self):
        pl.when(jnp.logical_not(self.here))(self.remote.wait_send)


def remote(src, dst, send, recv, target):
    return pltpu.make_async_remote_copy(
        src, dst, send, recv, device_id=target, device_id_type=MESH
    )


class Gather:
    def __init__(self, send_ref, full_ref, send_sem, recv_sem, pass_send, pass_recv, seq):
        f, z, m, c = where_am_i()
        self.ships = []
        for i in range(2):
            for h in range(2):
                slot = 2 * c + i
                self.ships.append(
                    Ship(
                        send_ref.at[i, h],
                        full_ref.at[z, h],
                        send_sem.at[i, h],
                        recv_sem.at[z],
                        (m * 2 + h, slot),
                    )
                )
        other = (m * 2 + 1 - c, z)
        self.arrivals = [
            remote(send_ref.at[0, 0], full_ref.at[k, c], send_sem.at[0, 0], recv_sem.at[k], other)
            for k in range(seq)
        ]
        self.passes = [
            remote(full_ref.at[k, c], full_ref.at[k, c], pass_send.at[k], pass_recv.at[k], other)
            for k in range(seq)
        ]
        self.handed = [
            remote(
                full_ref.at[k, c], full_ref.at[k, 1 - c], pass_send.at[k], pass_recv.at[k], other
            )
            for k in range(seq)
        ]

    def start(self):
        for ship in self.ships:
            ship.start()

    def hand_on(self, k):
        self.arrivals[k].wait_recv()
        self.passes[k].start()

    def ready(self, k):
        self.handed[k].wait_recv()

    def finish(self):
        for ship in self.ships:
            ship.wait_send()
        for item in self.passes:
            item.wait_send()


GATHER_SEMS = lambda seq: [
    pltpu.SemaphoreType.DMA((2, 2)),
    pltpu.SemaphoreType.DMA((seq,)),
    pltpu.SemaphoreType.DMA((seq,)),
    pltpu.SemaphoreType.DMA((seq,)),
]


class Return:
    def __init__(self, own_ref, back_ref, send_sem, recv_sem, seq):
        f, z, m, c = where_am_i()
        home = z // 2
        self.ships = [
            Ship(
                own_ref.at[k],
                back_ref.at[z % 2, c],
                send_sem.at[k],
                recv_sem.at[z % 2, c],
                (m * 2 + home, k),
            )
            for k in range(seq)
        ]
        self.arrivals = [
            remote(
                own_ref.at[0],
                back_ref.at[i, h],
                send_sem.at[0],
                recv_sem.at[i, h],
                (m * 2 + 1 - c, z),
            )
            for i in range(2)
            for h in range(2)
        ]

    def start(self):
        for ship in self.ships:
            ship.start()

    def finish(self):
        for ship in self.ships:
            ship.wait_send()
        for item in self.arrivals:
            item.wait_recv()


RETURN_SEMS = lambda seq: [pltpu.SemaphoreType.DMA((seq,)), pltpu.SemaphoreType.DMA((2, 2))]


class Spread:
    def __init__(self, source, full_ref, send_sem, recv_sem, local_sem, stride):
        f, z, m, c = where_am_i()
        n_f = lax.axis_size("fsdp")
        steps = n_f // stride
        slot = f if stride == 1 else m
        self.local = pltpu.make_async_copy(source(f), full_ref.at[slot], local_sem)
        self.sends = []
        self.arrivals = []
        for d in range(1, steps):
            to = (f + d * stride) % n_f
            back = (f + n_f - d * stride) % n_f
            self.sends.append(
                remote(source(to), full_ref.at[slot], send_sem.at[d], recv_sem.at[d], (to, z))
            )
            place = back if stride == 1 else back // 2
            self.arrivals.append(
                remote(source(f), full_ref.at[place], send_sem.at[d], recv_sem.at[d], (to, z))
            )

    def start(self):
        self.local.start()
        for item in self.sends:
            item.start()

    def ready(self):
        self.local.wait()
        for item in self.arrivals:
            item.wait_recv()

    def finish(self):
        for item in self.sends:
            item.wait_send()


def spread_sems(steps):
    return [
        pltpu.SemaphoreType.DMA((steps,)),
        pltpu.SemaphoreType.DMA((steps,)),
        pltpu.SemaphoreType.DMA,
    ]


def fsdp_peers():
    f, z, _, _ = where_am_i()
    n_f = lax.axis_size("fsdp")
    return [((f + d) % n_f, z) for d in range(1, n_f)]


def all_peers(seq):
    f, z, m, c = where_am_i()
    other = m * 2 + 1 - c
    peers = fsdp_peers()
    for d in range(1, seq):
        peers.append((f, (z + d) % seq))
        peers.append((other, (z + d) % seq))
    return peers


class Scatter:
    def __init__(self, parts_ref, got_ref, send_sem, recv_sem):
        f, z, m, c = where_am_i()
        n_m = lax.axis_size("fsdp") // 2
        self.copies = []
        for d in range(1, n_m):
            to = (m + d) % n_m
            self.copies.append(
                remote(
                    parts_ref.at[to],
                    got_ref.at[d - 1],
                    send_sem.at[d],
                    recv_sem.at[d],
                    (to * 2 + c, z),
                )
            )

    def start(self):
        for item in self.copies:
            item.start()

    def ready(self):
        for item in self.copies:
            item.wait_recv()

    def finish(self):
        for item in self.copies:
            item.wait_send()


def scatter_sems():
    n_m = lax.axis_size("fsdp") // 2
    return [pltpu.SemaphoreType.DMA((n_m,)), pltpu.SemaphoreType.DMA((n_m,))]


class Across:
    def __init__(self, own_ref, mate_ref, end_ref, sems):
        f, z, _, _ = where_am_i()
        self.own, self.mate, self.end = own_ref, mate_ref, end_ref
        self.edge = jnp.logical_or(z == 0, z == 3)
        self.inner = jnp.logical_not(self.edge)
        beside = jnp.where(z < 2, 1 - z, 5 - z)
        across = 3 - z
        self.up = remote(own_ref, end_ref, sems.at[0], sems.at[1], (f, beside))
        self.swap = remote(own_ref, mate_ref, sems.at[2], sems.at[3], (f, across))
        self.down = remote(own_ref, mate_ref, sems.at[4], sems.at[5], (f, beside))

    def rise(self):
        pl.when(self.edge)(self.up.start)

    def exchange(self):
        @pl.when(self.inner)
        def _():
            self.up.wait_recv()
            total = self.own[...].astype(F32) + self.end[...].astype(F32)
            self.own[...] = total.astype(self.own.dtype)
            self.swap.start()

    def settle(self):
        @pl.when(self.inner)
        def _():
            self.swap.wait()
            total = self.own[...].astype(F32) + self.mate[...].astype(F32)
            self.own[...] = total.astype(self.own.dtype)
            self.down.start()

    def ready(self):
        @pl.when(self.edge)
        def _():
            self.up.wait_send()
            self.down.wait_recv()
            self.own[...] = self.mate[...]

        @pl.when(self.inner)
        def _():
            self.down.wait_send()


ACROSS_SEMS = pltpu.SemaphoreType.DMA((6,))


def own_lanes(parity):
    lane = lax.broadcasted_iota(jnp.int32, (1, 128), 1)
    return (lane // HD) == parity, lane == HD * (1 - parity)


def project_kernel(
    seq, x_send, wqkv_send, wo_send,
    first_gain, first_shift, query_bias, value_bias, output_bias, second_gain, second_shift,
    outer_bias, inner_bias,
    x_full, n1_out, q_out, k_out, v_out, wqkv_out, wo_out, vecs_out, ibias_out,
    ssem, rsem, psend, precv,
    qsend, qrecv, qlocal, osend, orecv, olocal, vsend, vrecv, vlocal,
    xv, wqkv, small, smalls, lsem, wsem,
):
    f, z, m, c = where_am_i()
    n_f = lax.axis_size("fsdp")
    share = first_gain.shape[1]
    piece = inner_bias.shape[1]
    small[...] = jnp.zeros_like(small)
    for r, ref in enumerate(
        (
            first_gain,
            first_shift,
            query_bias,
            value_bias,
            output_bias,
            second_gain,
            second_shift,
            outer_bias,
        )
    ):
        small[r : r + 1, :share] = ref[...].astype(F32)
    small[8:9, :piece] = inner_bias[...].astype(F32)
    meet(all_peers(seq))
    gather = Gather(x_send, x_full, ssem, rsem, psend, precv, seq)
    vectors = Spread(lambda to: small, smalls, vsend, vrecv, vlocal, 1)
    weights = Spread(lambda to: wqkv_send.at[to % 2], wqkv, qsend, qrecv, qlocal, 1)
    later = Spread(lambda to: wo_send, wo_out, osend, orecv, olocal, 1)
    vectors.start()
    gather.start()
    weights.start()
    half = xv.shape[2]
    mine = q_out.shape[1]
    width = n1_out.shape[1]

    vectors.ready()
    row = lax.broadcasted_iota(jnp.int32, (128, width), 0)
    col = lax.broadcasted_iota(jnp.int32, (128, width), 1)
    vecs = jnp.zeros((16, width), F32)
    for k in range(n_f):
        spot = jnp.logical_and(col - k * share == row, row < share)
        vecs = vecs + nn(
            smalls[k, :, :128].astype(BF16), jnp.where(spot, 1.0, 0.0).astype(BF16)
        )
    vecs_out[...] = vecs[:8]
    for k in range(n_f // 2):
        ibias_out[0:1, k * piece : (k + 1) * piece] = smalls[2 * k + c, 8:9, :piece]
    weights.ready()
    later.start()
    keep_weights = pltpu.make_async_copy(wqkv, wqkv_out, wsem)
    keep_weights.start()
    for k in range(seq):
        gather.hand_on(k)
    gain = vecs_out[0:1, :]
    shift = vecs_out[1:2, :]
    cols = pl.ds(pl.multiple_of(c * mine, 128), mine)
    qb = vecs_out[2:3, cols]
    vb = vecs_out[3:4, cols]

    for k in range(seq):
        gather.ready(k)
        copy = pltpu.make_async_copy(x_full.at[k], xv.at[k], lsem.at[k])
        copy.start()
        copy.wait()
        rows = pl.ds(k * 2 * half, 2 * half)
        hat, _ = normalize(xv[k].reshape(2 * half, width).astype(F32))
        normed = (hat * gain + shift).astype(BF16)
        n1_out[rows, :] = normed
        qkv = nn(normed, wqkv[...].reshape(width, 3 * mine))
        q_out[rows, :] = (qkv[:, :mine] + qb).astype(BF16)
        k_out[rows, :] = qkv[:, mine : 2 * mine].astype(BF16)
        v_out[rows, :] = (qkv[:, 2 * mine :] + vb).astype(BF16)
    gather.finish()
    later.ready()
    vectors.finish()
    weights.finish()
    later.finish()
    keep_weights.wait()


def project(x_send, wqkv_send, wo_send, vectors, seq):
    _, _, half, width = x_send.shape
    n_f = lax.axis_size("fsdp")
    rows = seq * 2 * half
    share = wo_send.shape[0]
    mine = wqkv_send.shape[2] // 3
    piece = vectors[-1].shape[1]
    lanes = max(128, piece)
    return pl.pallas_call(
        lambda *refs: project_kernel(seq, *refs),
        in_specs=[ANY] * 3 + [VMEM] * 9,
        out_specs=[ANY, VMEM, VMEM, VMEM, VMEM, ANY, ANY, VMEM, VMEM],
        out_shape=[
            jax.ShapeDtypeStruct((seq, 2, half, width), BF16),
            jax.ShapeDtypeStruct((rows, width), BF16),
        ]
        + [jax.ShapeDtypeStruct((rows, mine), BF16)] * 3
        + [
            jax.ShapeDtypeStruct((n_f, share, 3 * mine), BF16),
            jax.ShapeDtypeStruct((n_f, share, width), BF16),
            jax.ShapeDtypeStruct((8, width), F32),
            jax.ShapeDtypeStruct((1, piece * n_f // 2), F32),
        ],
        scratch_shapes=GATHER_SEMS(seq)
        + spread_sems(n_f)
        + spread_sems(n_f)
        + spread_sems(n_f)
        + [
            pltpu.VMEM((seq, 2, half, width), BF16),
            pltpu.VMEM((n_f, share, 3 * mine), BF16),
            pltpu.VMEM((16, lanes), F32),
            pltpu.VMEM((n_f, 16, lanes), F32),
            pltpu.SemaphoreType.DMA((seq,)),
            pltpu.SemaphoreType.DMA,
        ],
        compiler_params=pltpu.CompilerParams(
            collective_id=0, has_side_effects=True, vmem_limit_bytes=LIMIT
        ),
        name="project",
    )(x_send, wqkv_send, wo_send, *vectors)


def project_plain_kernel(seq, x_send, wqkv, vecs, x_full, n1_out, q_out, k_out, v_out,
                         ssem, rsem, psend, precv, xv, lsem):
    f, z, m, c = where_am_i()
    meet(column_peers(seq))
    gather = Gather(x_send, x_full, ssem, rsem, psend, precv, seq)
    gather.start()
    half = xv.shape[1]
    mine = q_out.shape[1]
    for k in range(seq):
        gather.hand_on(k)
    gain = vecs[0:1, :]
    shift = vecs[1:2, :]
    cols = pl.ds(pl.multiple_of(c * mine, 128), mine)
    qb = vecs[2:3, cols]
    vb = vecs[3:4, cols]
    for k in range(seq):
        gather.ready(k)
        copy = pltpu.make_async_copy(x_full.at[k], xv, lsem)
        copy.start()
        copy.wait()
        rows = pl.ds(k * 2 * half, 2 * half)
        hat, _ = normalize(xv[...].reshape(2 * half, -1).astype(F32))
        normed = (hat * gain + shift).astype(BF16)
        n1_out[rows, :] = normed
        qkv = nn(normed, wqkv[...])
        q_out[rows, :] = (qkv[:, :mine] + qb).astype(BF16)
        k_out[rows, :] = qkv[:, mine : 2 * mine].astype(BF16)
        v_out[rows, :] = (qkv[:, 2 * mine :] + vb).astype(BF16)
    gather.finish()


def project_plain(x_send, wqkv, vecs, seq):
    _, _, half, width = x_send.shape
    rows = seq * 2 * half
    mine = wqkv.shape[1] // 3
    return pl.pallas_call(
        lambda *refs: project_plain_kernel(seq, *refs),
        in_specs=[ANY, VMEM, VMEM],
        out_specs=[ANY, VMEM, VMEM, VMEM, VMEM],
        out_shape=[
            jax.ShapeDtypeStruct((seq, 2, half, width), BF16),
            jax.ShapeDtypeStruct((rows, width), BF16),
        ]
        + [jax.ShapeDtypeStruct((rows, mine), BF16)] * 3,
        scratch_shapes=GATHER_SEMS(seq)
        + [pltpu.VMEM((2, half, width), BF16), pltpu.SemaphoreType.DMA],
        compiler_params=pltpu.CompilerParams(
            collective_id=5, has_side_effects=True, vmem_limit_bytes=LIMIT
        ),
        name="project_plain",
    )(x_send, wqkv, vecs)


def attend_kernel(
    seq, local, heads, cot_send, wi_send, wu_send, q, k, v,
    e_out, o_out, linv_out, mixed_out, cot_full, wi_out, wu_out,
    ssem, rsem, psend, precv, isend, irecv, ilocal, usend, urecv, ulocal,
    stage, ka, va, msend, mrecv, mlocal,
):
    f, z, m, c = where_am_i()
    h = pl.program_id(0)
    pair = h // 2
    parity = h % 2
    rows = q.shape[0]
    gather = Gather(cot_send, cot_full, ssem, rsem, psend, precv, seq)
    weights = [
        Spread(lambda to: wi_send.at[to % 2], wi_out, isend, irecv, ilocal, 1),
        Spread(lambda to: wu_send, wu_out, usend, urecv, ulocal, 2),
    ]
    other = (m * 2 + 1 - c, z)

    @pl.when(h == 0)
    def _():
        meet(all_peers(seq))
        gather.start()
        for item in weights:
            item.start()

    mine, first = own_lanes(parity)
    place = lax.broadcasted_iota(jnp.int32, (rows, 1), 0) % (rows // seq)
    bar = jnp.where(place < local, 0.0, -1e38).astype(F32)
    ka[...] = jnp.where(mine, k[...].astype(F32), jnp.where(first, bar, 0.0)).astype(BF16)
    va[...] = jnp.where(mine, v[...].astype(F32), jnp.where(first, 1.0, 0.0)).astype(BF16)
    factor = HD ** (-0.5) * math.log2(math.e)
    for i in range(rows // QB):
        sl = slice(i * QB, (i + 1) * QB)
        qa = jnp.where(mine, q[sl, :].astype(F32), jnp.where(first, 1.0, 0.0)).astype(BF16)
        scores = nt(qa, ka[...])
        peak = jnp.max(scores, -1, keepdims=True)
        expo = jnp.exp2((scores - peak) * factor).astype(BF16)
        e_out[0, sl, :] = expo
        raw = nn(expo, va[...])
        total = jnp.sum(jnp.where(first, raw, 0.0), -1, keepdims=True)
        inv = 1.0 / total
        res = raw * inv

        @pl.when(parity == 0)
        def _():
            o_out[sl, :] = res
            linv_out[sl, :] = jnp.broadcast_to(inv, res.shape)

        @pl.when(parity == 1)
        def _():
            both = jnp.where(mine, res, o_out[sl, :])
            o_out[sl, :] = both
            linv_out[sl, :] = jnp.where(mine, inv, linv_out[sl, :])
            stage[pair, sl, :] = both.astype(BF16)

    def mixed_copies(p):
        return (
            pltpu.make_async_copy(stage.at[p], mixed_out.at[c, p], mlocal.at[p]),
            remote(stage.at[p], mixed_out.at[c, p], msend.at[p], mrecv.at[p], other),
            remote(stage.at[p], mixed_out.at[1 - c, p], msend.at[p], mrecv.at[p], other),
        )

    @pl.when(parity == 1)
    def _():
        here, there, _ = mixed_copies(pair)
        here.start()
        there.start()

    @pl.when(h == heads - 2)
    def _():
        for item in range(seq):
            gather.hand_on(item)

    @pl.when(h == heads - 1)
    def _():
        for item in range(seq):
            gather.ready(item)
        gather.finish()
        for item in weights:
            item.ready()
            item.finish()
        for p in range(heads // 2):
            here, there, back = mixed_copies(p)
            here.wait()
            there.wait_send()
            back.wait_recv()


def attend(cot_send, wi_send, wu_send, q, k, v, local, seq):
    rows, mine = q.shape
    n_f = lax.axis_size("fsdp")
    heads = mine // HD
    _, _, half, width = cot_send.shape
    pairs = heads // 2
    by_pair = pl.BlockSpec((rows, 128), lambda h: (0, h // 2))
    return pl.pallas_call(
        lambda *refs: attend_kernel(seq, local, heads, *refs),
        grid=(heads,),
        in_specs=[ANY, ANY, ANY, by_pair, by_pair, by_pair],
        out_specs=[
            pl.BlockSpec((1, rows, rows), lambda h: (h, 0, 0)),
            by_pair,
            by_pair,
            ANY,
            ANY,
            ANY,
            ANY,
        ],
        out_shape=[
            jax.ShapeDtypeStruct((heads, rows, rows), BF16),
            jax.ShapeDtypeStruct((rows, mine), F32),
            jax.ShapeDtypeStruct((rows, mine), F32),
            jax.ShapeDtypeStruct((2, pairs, rows, 128), BF16),
            jax.ShapeDtypeStruct((seq, 2, half, width), BF16),
            jax.ShapeDtypeStruct((n_f,) + wi_send.shape[1:], BF16),
            jax.ShapeDtypeStruct((n_f // 2,) + wu_send.shape, BF16),
        ],
        scratch_shapes=GATHER_SEMS(seq)
        + spread_sems(n_f)
        + spread_sems(n_f // 2)
        + [
            pltpu.VMEM((pairs, rows, 128), BF16),
            pltpu.VMEM((rows, 128), BF16),
            pltpu.VMEM((rows, 128), BF16),
            pltpu.SemaphoreType.DMA((pairs,)),
            pltpu.SemaphoreType.DMA((pairs,)),
            pltpu.SemaphoreType.DMA((pairs,)),
        ],
        compiler_params=pltpu.CompilerParams(
            collective_id=1, has_side_effects=True, vmem_limit_bytes=LIMIT
        ),
        name="attend",
    )(cot_send, wi_send, wu_send, q, k, v)


def gelu_parts(u):
    x = jnp.abs(u) * (1.0 / math.sqrt(2.0))
    t = 1.0 / (1.0 + 0.3275911 * x)
    poly = t * (
        0.254829592
        + t * (-0.284496736 + t * (1.421413741 + t * (-1.453152027 + t * 1.061405429)))
    )
    expo = jnp.exp(-x * x)
    tail = 0.5 * poly * expo
    phi = jnp.where(u >= 0, 1.0 - tail, tail)
    return phi, u * expo * (1.0 / math.sqrt(2.0 * math.pi))


def dense_kernel(
    seq, x, mixed, cot, wo, wi, wu, vecs, ibias,
    out_back, gres_own, gm_out, gwo_out, gwi_out, ru_out, gvec_out, gib_out,
    n2, hat2, inv2, keep, slope, out_own, pstage, precv, gstage, grecv,
    gwo, gwi, shared, ugot, upart,
    psem, prsem, gsem, grsem, bsend, brecv, usend, urecv,
):
    f, z, m, c = where_am_i()
    other = (m * 2 + 1 - c, z)
    meet(all_peers(seq))
    half = x.shape[2]
    chunk = 2 * half
    width = x.shape[3]
    mine = gm_out.shape[1]
    hidden = wi.shape[1]
    n_m = gwi_out.shape[0]
    share = gwi_out.shape[2]
    piece = upart.shape[1]
    obias, gain, shift, ubias = vecs[4:5, :], vecs[5:6, :], vecs[6:7, :], vecs[7:8, :]
    gvec_out[...] = jnp.zeros_like(gvec_out)
    gib_out[...] = jnp.zeros_like(gib_out)
    gwo[...] = jnp.zeros_like(gwo)
    gwi[...] = jnp.zeros_like(gwi)
    gwu = shared.at[:hidden]
    gown = shared.at[: seq * chunk]
    gwu[...] = jnp.zeros_like(gwu)
    back = Return(out_own, out_back, bsend, brecv, seq)
    outer = Scatter(upart, ugot, usend, urecv)

    def p_copy(i):
        return remote(pstage.at[i], precv.at[i], psem.at[i], prsem.at[i], other)

    def g_copy(i):
        return remote(gstage.at[i], grecv.at[i], gsem.at[i], grsem.at[i], other)

    def mixed_rows(i):
        rows = pl.ds(i * chunk, chunk)
        return jnp.concatenate(
            [mixed[a, p, rows, :] for a in range(2) for p in range(mixed.shape[1])], axis=1
        )

    def forward(i, _):
        rows = pl.ds(i * chunk, chunk)
        resid = (
            x[i].reshape(chunk, width).astype(F32) + nn(mixed_rows(i), wo[...]) + obias
        )
        hat, inv = normalize(resid)
        normed = (hat * gain + shift).astype(BF16)
        n2[rows, :] = normed
        hat2[rows, :] = hat
        inv2[rows, :] = jnp.broadcast_to(inv, (chunk, 128))
        inner = nn(normed, wi[...]) + ibias[...]
        phi, bump = gelu_parts(inner)
        active = (inner * phi).astype(BF16)
        slope[rows, :] = (phi + bump).astype(slope.dtype)
        pout = nn(active, wu[...])
        full = resid + ubias

        @pl.when(c == 0)
        def _():
            keep[i] = full[:half] + pout[:half]
            pstage[i] = pout[half:].astype(pstage.dtype)

        @pl.when(c == 1)
        def _():
            keep[i] = full[half:] + pout[half:]
            pstage[i] = pout[:half].astype(pstage.dtype)

        p_copy(i).start()
        g = cot[i].reshape(chunk, width)
        gwu[...] += tn(active, g)
        gvec_out[0:1, :] += jnp.sum(g.astype(F32), 0, keepdims=True)
        return 0

    def middle(i, _):
        rows = pl.ds(i * chunk, chunk)
        g = cot[i].reshape(chunk, width)
        gi = (nt(g, wu[...]) * slope[rows, :].astype(F32)).astype(BF16)
        gn2 = nt(gi, wi[...])
        gown[rows, :] = gn2
        gstage[i] = gn2.astype(gstage.dtype)
        g_copy(i).start()
        gwi[...] += tn(n2[rows, :], gi)
        gib_out[...] += jnp.sum(gi.astype(F32), 0, keepdims=True)
        return 0

    def backward(i, _):
        rows = pl.ds(i * chunk, chunk)
        g_copy(i).wait_recv()
        gn2 = gown[rows, :] + grecv[i].astype(F32)
        hat = hat2[rows, :]
        gvec_out[1:2, :] += jnp.sum(gn2 * hat, 0, keepdims=True)
        gvec_out[2:3, :] += jnp.sum(gn2, 0, keepdims=True)
        g = cot[i].reshape(chunk, width).astype(F32)
        gres = g + norm_back(gn2, gain, hat, inv2[rows, 0:1])
        branch = gres.astype(BF16)
        gvec_out[3:4, :] += jnp.sum(branch.astype(F32), 0, keepdims=True)
        wrows = pl.ds(pl.multiple_of(c * mine, 128), mine)
        gm_out[rows, :] = nt(branch, wo[wrows, :]).astype(BF16)
        mix = mixed_rows(i)

        @pl.when(c == 0)
        def _():
            gres_own[i] = gres[:half]
            gwo[...] += tn(mix, branch[:, :mine])

        @pl.when(c == 1)
        def _():
            gres_own[i] = gres[half:]
            gwo[...] += tn(mix, branch[:, mine:])

        return 0

    lax.fori_loop(0, seq, forward, 0)
    for k in range(n_m):
        upart[k] = gwu[k * piece : (k + 1) * piece, :].astype(BF16)
    outer.start()
    for k in range(seq):
        p_copy(k).wait_recv()
        out_own[k] = (keep[k] + precv[k].astype(F32)).astype(BF16)
    back.start()
    lax.fori_loop(0, seq, middle, 0)
    for k in range(n_m):
        for j in range(2):
            at = (2 * k + j) * share
            gwi_out[k, j] = gwi[at : at + share, :].astype(BF16)
    lax.fori_loop(0, seq, backward, 0)
    for k in range(n_m):
        for j in range(2):
            at = (2 * k + j) * share
            gwo_out[k, j] = gwo[at : at + share, :].astype(BF16)

    def last(i, _):
        p_copy(i).wait_send()
        g_copy(i).wait_send()
        return 0

    lax.fori_loop(0, seq, last, 0)
    outer.ready()
    total = upart[m].astype(F32)
    for k in range(n_m - 1):
        total = total + ugot[k].astype(F32)
    ru_out[...] = total.astype(BF16)
    outer.finish()
    back.finish()


def dense(x, mixed, cot, wo, wi, wu, vecs, ibias):
    seq, _, half, width = x.shape
    rows = seq * 2 * half
    hidden = wi.shape[1]
    mine = width // 2
    n_f = lax.axis_size("fsdp")
    n_m = n_f // 2
    share = width // n_f
    piece = hidden // n_m
    return pl.pallas_call(
        lambda *refs: dense_kernel(seq, *refs),
        in_specs=[VMEM] * 8,
        out_specs=[ANY] + [VMEM] * 7,
        out_shape=[
            jax.ShapeDtypeStruct((2, 2, half, width), BF16),
            jax.ShapeDtypeStruct((seq, half, width), F32),
            jax.ShapeDtypeStruct((rows, mine), BF16),
            jax.ShapeDtypeStruct((n_m, 2, share, mine), BF16),
            jax.ShapeDtypeStruct((n_m, 2, share, hidden), BF16),
            jax.ShapeDtypeStruct((piece, width), BF16),
            jax.ShapeDtypeStruct((8, width), F32),
            jax.ShapeDtypeStruct((1, hidden), F32),
        ],
        scratch_shapes=[
            pltpu.VMEM((rows, width), BF16),
            pltpu.VMEM((rows, width), F32),
            pltpu.VMEM((rows, 128), F32),
            pltpu.VMEM((seq, half, width), F32),
            pltpu.VMEM((rows, hidden), BF16),
            pltpu.VMEM((seq, half, width), BF16),
            pltpu.VMEM((seq, half, width), BF16),
            pltpu.VMEM((seq, half, width), BF16),
            pltpu.VMEM((seq, 2 * half, width), BF16),
            pltpu.VMEM((seq, 2 * half, width), BF16),
            pltpu.VMEM((width, mine), F32),
            pltpu.VMEM((width, hidden), F32),
            pltpu.VMEM((max(rows, hidden), width), F32),
            pltpu.VMEM((n_m - 1, piece, width), BF16),
            pltpu.VMEM((n_m, piece, width), BF16),
            pltpu.SemaphoreType.DMA((seq,)),
            pltpu.SemaphoreType.DMA((seq,)),
            pltpu.SemaphoreType.DMA((seq,)),
            pltpu.SemaphoreType.DMA((seq,)),
        ]
        + RETURN_SEMS(seq)
        + scatter_sems(),
        compiler_params=pltpu.CompilerParams(
            collective_id=2, has_side_effects=True, vmem_limit_bytes=LIMIT
        ),
        name="dense",
    )(x, mixed, cot, wo, wi, wu, vecs, ibias)


def attend_back_kernel(
    seq, heads, gwi, gwo, ru, q, k, v, gm, o, linv, e,
    gq_out, gk_out, gv_out, igot, ogot, gwu_out,
    isend, irecv, osend, orecv, zsems, zown, zmate, zend, lsem,
    do, dot_, qt, va, km, dqs, dvt, dkt,
):
    h = pl.program_id(0)
    parity = h % 2
    rows = q.shape[0]
    scatters = [Scatter(gwi, igot, isend, irecv), Scatter(gwo, ogot, osend, orecv)]
    outer = Across(zown, zmate, zend, zsems)

    @pl.when(h == 0)
    def _():
        load = pltpu.make_async_copy(ru, zown, lsem)
        load.start()
        meet(all_peers(seq))
        for item in scatters:
            item.start()
        load.wait()
        outer.rise()

    mine, first = own_lanes(parity)
    third = HD ** (-0.5)
    scaled = (gm[...].astype(F32) * linv[...]).astype(BF16).astype(F32)
    scaled = jnp.where(mine, scaled, 0.0)
    delta = jnp.sum(scaled * o[...], -1, keepdims=True)
    high = delta.astype(BF16).astype(F32)
    middle = (delta - high).astype(BF16).astype(F32)
    low = delta - high - middle
    lane = lax.broadcasted_iota(jnp.int32, (1, 128), 1)
    base = HD * (1 - parity)
    do[...] = (
        scaled
        - jnp.where(lane == base, high, 0.0)
        - jnp.where(lane == base + 1, middle, 0.0)
        - jnp.where(lane == base + 2, low, 0.0)
    ).astype(BF16)
    ones = jnp.logical_and(lane >= base, lane < base + 3)
    va[...] = jnp.where(mine, v[...].astype(F32), jnp.where(ones, 1.0, 0.0)).astype(BF16)
    km[...] = jnp.where(mine, k[...].astype(F32), 0.0).astype(BF16)
    dot_[...] = do[...].T
    qt[...] = q[...].T
    sub = pl.ds(pl.multiple_of(parity * HD, HD), HD)
    for i in range(rows // QB):
        sl = slice(i * QB, (i + 1) * QB)
        p = e[0, sl, :]
        dp = nt(do[sl, :], va[...])
        ds = (p.astype(F32) * dp).astype(BF16)
        dq = nn(ds, km[...])

        @pl.when(parity == 0)
        def _():
            dqs[sl, :] = dq

        @pl.when(parity == 1)
        def _():
            gq_out[sl, :] = ((dqs[sl, :] + dq) * third).astype(BF16)

        a = nn(dot_[sub, sl], p)
        b = nn(qt[sub, sl], ds)
        if i == 0:
            dvt[sub, :] = a
            dkt[sub, :] = b
        else:
            dvt[sub, :] += a
            dkt[sub, :] += b

    @pl.when(parity == 1)
    def _():
        gv_out[...] = dvt[...].T.astype(BF16)
        gk_out[...] = (dkt[...] * third).T.astype(BF16)

    pl.when(h == 1)(outer.exchange)
    pl.when(h == 3)(outer.settle)

    @pl.when(h == heads - 1)
    def _():
        outer.ready()
        gwu_out[...] = zown[...].astype(F32)
        for item in scatters:
            item.ready()
            item.finish()


def attend_back(gwi, gwo, ru, q, k, v, gm, o, linv, e, seq):
    rows, mine = q.shape
    heads = mine // HD
    n_m = gwi.shape[0]
    piece, width = ru.shape
    by_pair = pl.BlockSpec((rows, 128), lambda h: (0, h // 2))
    return pl.pallas_call(
        lambda *refs: attend_back_kernel(seq, heads, *refs),
        grid=(heads,),
        in_specs=[ANY] * 3
        + [by_pair] * 6
        + [pl.BlockSpec((1, rows, rows), lambda h: (h, 0, 0))],
        out_specs=[by_pair] * 3
        + [ANY, ANY, pl.BlockSpec((piece, width), lambda h: (0, 0))],
        out_shape=[jax.ShapeDtypeStruct((rows, mine), BF16)] * 3
        + [
            jax.ShapeDtypeStruct((n_m - 1,) + gwi.shape[1:], BF16),
            jax.ShapeDtypeStruct((n_m - 1,) + gwo.shape[1:], BF16),
            jax.ShapeDtypeStruct((piece, width), F32),
        ],
        scratch_shapes=scatter_sems()
        + scatter_sems()
        + [ACROSS_SEMS]
        + [pltpu.VMEM((piece, width), BF16)] * 3
        + [
            pltpu.SemaphoreType.DMA,
            pltpu.VMEM((rows, 128), BF16),
            pltpu.VMEM((128, rows), BF16),
            pltpu.VMEM((128, rows), BF16),
            pltpu.VMEM((rows, 128), BF16),
            pltpu.VMEM((rows, 128), BF16),
            pltpu.VMEM((rows, 128), F32),
            pltpu.VMEM((128, rows), F32),
            pltpu.VMEM((128, rows), F32),
        ],
        compiler_params=pltpu.CompilerParams(
            collective_id=3, has_side_effects=True, vmem_limit_bytes=LIMIT
        ),
        name="attend_back",
    )(gwi, gwo, ru, q, k, v, gm, o, linv, e)


def project_back_kernel(
    seq, x, n1, gq, gk, gv, gres, wqkv, vecs, vpart, gwi, igot, gwo, ogot,
    gwq_out, gwk_out, gwv_out, gwo_out, gwi_out, vec_out, ig_back,
    gown, gstage, grecv, ig_own, gw, qpart, qgot, vgot,
    ri, imate, iend, ito, ra, amate, aend, ato, vown, vmate, vend, vto,
    gsem, grsem, bsend, brecv, qsend, qrecv, vsend, vrecv, zi, za, zv, pair_sems,
):
    f, z, m, c = where_am_i()
    other = (m * 2 + 1 - c, z)
    meet(all_peers(seq))
    half = x.shape[2]
    chunk = 2 * half
    width = x.shape[3]
    mine = gq.shape[1]
    n_m = gwi.shape[0]
    share = gwi.shape[2]
    gain = vecs[0:1, :]
    inner = Across(ri, imate, iend, zi)
    parts = [Across(ra.at[k], amate.at[k], aend.at[k], za.at[k]) for k in range(4)]
    vectors = Across(vown, vmate, vend, zv)
    queries = [
        Scatter(qpart.at[k], qgot.at[k], qsend.at[k], qrecv.at[k]) for k in range(3)
    ]
    vspread = [
        remote(
            vown,
            vgot.at[d - 1],
            vsend.at[d],
            vrecv.at[d],
            (((m + d) % n_m) * 2 + c, z),
        )
        for d in range(1, n_m)
    ]
    back = Return(ig_own, ig_back, bsend, brecv, seq)

    def g_copy(i):
        return remote(gstage.at[i], grecv.at[i], gsem.at[i], grsem.at[i], other)

    def cross(k, src, dst):
        return remote(src, dst, pair_sems.at[0, k], pair_sems.at[1, k], other)

    total = gwi[m].astype(F32)
    for k in range(n_m - 1):
        total = total + igot[k].astype(F32)
    ri[...] = total.astype(BF16)
    inner.rise()
    total = gwo[m].astype(F32)
    for k in range(n_m - 1):
        total = total + ogot[k].astype(F32)
    ra[3] = total.astype(BF16)
    parts[3].rise()

    def first(i, _):
        rows = pl.ds(i * chunk, chunk)
        grads = jnp.concatenate([gq[rows, :], gk[rows, :], gv[rows, :]], axis=1)
        gn1 = nt(grads, wqkv[...])

        @pl.when(c == 0)
        def _():
            gown[i] = gn1[:half]
            gstage[i] = gn1[half:]

        @pl.when(c == 1)
        def _():
            gown[i] = gn1[half:]
            gstage[i] = gn1[:half]

        g_copy(i).start()
        return 0

    lax.fori_loop(0, seq, first, 0)
    for k, ref in enumerate((gq, gk, gv)):
        gw[...] = tn(n1[...], ref[...])
        for j in range(n_m):
            for b in range(2):
                at = (2 * j + b) * share
                qpart[k, j, b] = gw[at : at + share, :].astype(BF16)
        queries[k].start()
        if k == 0:
            inner.exchange()
            parts[3].exchange()
    for k in range(seq):
        g_copy(k).wait_recv()
        gn1 = gown[k] + grecv[k]
        hat, inv = normalize(x[k, c].astype(F32))
        line = jnp.sum(gn1 * hat, 0, keepdims=True)
        flat = jnp.sum(gn1, 0, keepdims=True)
        if k == 0:
            gain_sum, shift_sum = line, flat
        else:
            gain_sum, shift_sum = gain_sum + line, shift_sum + flat
        ig_own[k] = (gres[k] + norm_back(gn1, gain, hat, inv)).astype(BF16)
    back.start()
    inner.settle()
    parts[3].settle()
    vown[...] = vpart[...]
    vown[0:1, :] = gain_sum
    vown[1:2, :] = shift_sum
    cols = pl.ds(pl.multiple_of(c * mine, 128), mine)
    vown[2:3, cols] = jnp.sum(gq[...].astype(F32), 0, keepdims=True)
    vown[3:4, cols] = jnp.sum(gv[...].astype(F32), 0, keepdims=True)
    for item in vspread:
        item.start()
    for item in vspread:
        item.wait()
    total = vown[...]
    for k in range(n_m - 1):
        total = total + vgot[k]
    vown[...] = total
    vectors.rise()
    for k in range(3):
        queries[k].ready()
        total = qpart[k, m].astype(F32)
        for j in range(n_m - 1):
            total = total + qgot[k, j].astype(F32)
        ra[k] = total.astype(BF16)
        parts[k].rise()
    vectors.exchange()
    for k in range(3):
        parts[k].exchange()
    vectors.settle()
    for k in range(3):
        parts[k].settle()
    inner.ready()
    icross = cross(0, ri.at[1 - c], ito)
    icross.start()
    vectors.ready()
    vcross = cross(5, vown, vto)
    vcross.start()
    crosses = []
    for k in (3, 0, 1, 2):
        parts[k].ready()
        crosses.append(cross(1 + k, ra.at[k, 1 - c], ato.at[k]))
        crosses[-1].start()
    outs = {0: gwq_out, 1: gwk_out, 2: gwv_out, 3: gwo_out}
    here = pl.ds(pl.multiple_of(c * mine, 128), mine)
    there = pl.ds(pl.multiple_of((1 - c) * mine, 128), mine)
    icross.wait()
    gwi_out[c] = ri[c].astype(F32)
    gwi_out[1 - c] = ito[...].astype(F32)
    vcross.wait()
    vec_out[...] = vown[...] + vto[...]
    for k, item in zip((3, 0, 1, 2), crosses):
        item.wait()
        outs[k][:, here] = ra[k, c].astype(F32)
        outs[k][:, there] = ato[k].astype(F32)
    for k in range(seq):
        g_copy(k).wait_send()
    for k in range(3):
        queries[k].finish()
    back.finish()


def project_back(x, n1, gq, gk, gv, gres, wqkv, vecs, vpart, gwi, igot, gwo, ogot):
    seq, _, half, width = x.shape
    n_m, _, share, hidden = gwi.shape
    mine = gq.shape[1]
    square = jax.ShapeDtypeStruct((share, width), F32)
    block = (2, share, mine)
    return pl.pallas_call(
        lambda *refs: project_back_kernel(seq, *refs),
        in_specs=[VMEM] * 13,
        out_specs=[VMEM] * 6 + [ANY],
        out_shape=[square] * 4
        + [
            jax.ShapeDtypeStruct((2, share, hidden), F32),
            jax.ShapeDtypeStruct((16, width), F32),
            jax.ShapeDtypeStruct((2, 2, half, width), BF16),
        ],
        scratch_shapes=[
            pltpu.VMEM((seq, half, width), F32),
            pltpu.VMEM((seq, half, width), F32),
            pltpu.VMEM((seq, half, width), F32),
            pltpu.VMEM((seq, half, width), BF16),
            pltpu.VMEM((width, mine), F32),
            pltpu.VMEM((3, n_m) + block, BF16),
            pltpu.VMEM((3, n_m - 1) + block, BF16),
            pltpu.VMEM((n_m - 1, 16, width), F32),
            pltpu.VMEM((2, share, hidden), BF16),
            pltpu.VMEM((2, share, hidden), BF16),
            pltpu.VMEM((2, share, hidden), BF16),
            pltpu.VMEM((share, hidden), BF16),
            pltpu.VMEM((4,) + block, BF16),
            pltpu.VMEM((4,) + block, BF16),
            pltpu.VMEM((4,) + block, BF16),
            pltpu.VMEM((4, share, mine), BF16),
            pltpu.VMEM((16, width), F32),
            pltpu.VMEM((16, width), F32),
            pltpu.VMEM((16, width), F32),
            pltpu.VMEM((16, width), F32),
            pltpu.SemaphoreType.DMA((seq,)),
            pltpu.SemaphoreType.DMA((seq,)),
        ]
        + RETURN_SEMS(seq)
        + [
            pltpu.SemaphoreType.DMA((3, n_m)),
            pltpu.SemaphoreType.DMA((3, n_m)),
            pltpu.SemaphoreType.DMA((n_m,)),
            pltpu.SemaphoreType.DMA((n_m,)),
            ACROSS_SEMS,
            pltpu.SemaphoreType.DMA((4, 6)),
            ACROSS_SEMS,
            pltpu.SemaphoreType.DMA((2, 6)),
        ],
        compiler_params=pltpu.CompilerParams(
            collective_id=4, has_side_effects=True, vmem_limit_bytes=LIMIT
        ),
        name="project_back",
    )(x, n1, gq, gk, gv, gres, wqkv, vecs, vpart, gwi, igot, gwo, ogot)


def per_device(
    frames,
    cotangent,
    valid_slots,
    first_gain,
    first_shift,
    query_weight,
    query_bias,
    key_weight,
    value_weight,
    value_bias,
    output_weight,
    output_bias,
    second_gain,
    second_shift,
    inner_weight,
    inner_bias,
    outer_weight,
    outer_bias,
):
    seq = lax.axis_size("seq")
    n_f = lax.axis_size("fsdp")
    f = lax.axis_index("fsdp")
    m, c = f // 2, f % 2
    slots, local, width = frames.shape
    chunk = -(-local // 128) * 128
    half = chunk // 2
    mine = width // 2
    share = width // n_f
    piece = inner_bias.shape[0]
    hidden = piece * n_f // 2

    keep = valid_slots.astype(BF16)[:, None, None]
    pad = ((0, 0), (0, chunk - local), (0, 0))
    x_send = jnp.pad(frames, pad).reshape(slots, 2, half, width)
    cot_send = jnp.pad(cotangent * keep, pad).reshape(slots, 2, half, width)
    wi_send = inner_weight.reshape(share, n_f // 2, 2, piece).transpose(2, 0, 1, 3)
    wi_send = wi_send.reshape(2, share, hidden)
    vectors = (
        first_gain,
        first_shift,
        query_bias,
        value_bias,
        output_bias,
        second_gain,
        second_shift,
        outer_bias,
    )
    if share % 16 == 0 and piece % 128 == 0:
        wqkv_send = jnp.concatenate(
            [
                w.reshape(share, 2, mine).transpose(1, 0, 2)
                for w in (query_weight, key_weight, value_weight)
            ],
            axis=-1,
        )
        x, n1, q, k, v, wqkv, wo, vecs, ibias = project(
            x_send,
            wqkv_send,
            output_weight,
            [value[None] for value in vectors] + [inner_bias[None]],
            seq,
        )
        wqkv = wqkv.reshape(width, 3 * mine)
        wo = wo.reshape(width, width)
    else:

        def gathered(value, axis=0):
            return lax.all_gather(value, "fsdp", axis=axis, tiled=True)

        def my_columns(value):
            return lax.dynamic_slice_in_dim(value, c * mine, mine, axis=1)

        wqkv = jnp.concatenate(
            [my_columns(gathered(w)) for w in (query_weight, key_weight, value_weight)], axis=1
        )
        wo = gathered(output_weight)
        vecs = gathered(jnp.stack(vectors), 1).astype(F32)
        ibias = gathered(inner_bias).astype(F32).reshape(n_f // 2, 2, piece)
        ibias = lax.dynamic_index_in_dim(ibias, c, 1, keepdims=False).reshape(1, hidden)
        x, n1, q, k, v = project_plain(x_send, wqkv, vecs, seq)

    e, o, linv, mixed, cot, wi, wu = attend(
        cot_send, wi_send, outer_weight, q, k, v, local, seq
    )
    wi = wi.reshape(width, hidden)
    wu = wu.reshape(hidden, width)
    out_back, gres, gm, gwo, gwi, ru, gvec, gib = dense(x, mixed, cot, wo, wi, wu, vecs, ibias)
    gq, gk, gv, igot, ogot, gwu = attend_back(gwi, gwo, ru, q, k, v, gm, o, linv, e, seq)
    vpart = jnp.zeros((16, width), F32)
    vpart = vpart.at[4:8].set(0.5 * gvec[jnp.array([3, 1, 2, 0])])
    bias_rows = hidden // width
    vpart = lax.dynamic_update_slice(
        vpart, gib.reshape(bias_rows, width), (8 + c * bias_rows, 0)
    )
    gwq, gwk, gwv, gwo, gwi, vec, ig_back = project_back(
        x, n1, gq, gk, gv, gres, wqkv, vecs, vpart, gwi, igot, gwo, ogot
    )
    keep32 = valid_slots.astype(F32)[:, None, None]
    outputs = (out_back.reshape(slots, chunk, width)[:, :local].astype(F32) * keep32).astype(BF16)
    input_grad = ig_back.reshape(slots, chunk, width)[:, :local]
    gwi = gwi.reshape(2, share, n_f // 2, piece).transpose(1, 2, 0, 3).reshape(share, 2 * hidden)
    own = lax.dynamic_slice(vec, (0, f * share), (8, share))
    biases = vec[8 : 8 + 2 * bias_rows].reshape(2, n_f // 2, piece)
    gib = lax.dynamic_slice(biases, (c, m, 0), (1, 1, piece)).reshape(piece)
    return (
        outputs,
        input_grad,
        own[0],
        own[1],
        gwq,
        own[2],
        gwk,
        gwv,
        own[3],
        gwo,
        own[4],
        own[5],
        own[6],
        gwi,
        gib,
        gwu,
        own[7],
    )


def solution(mesh):
    rows = P("fsdp", "seq", None)
    vector, matrix = P("fsdp"), P("fsdp", None)
    weights = (
        vector,
        vector,
        matrix,
        vector,
        matrix,
        matrix,
        vector,
        matrix,
        vector,
        vector,
        vector,
        matrix,
        vector,
        matrix,
        vector,
    )
    return jax.shard_map(
        per_device,
        mesh=mesh,
        in_specs=(rows, rows, vector) + weights,
        out_specs=(rows, rows) + weights,
        check_vma=False,
    )
```

```python
import math

import jax
import jax.numpy as jnp
from jax import lax
from jax.experimental import pallas as pl
from jax.experimental.pallas import tpu as pltpu
from jax.sharding import PartitionSpec as P

H = 12
HD = 64
EPS = 1e-05
MESH = pl.DeviceIdType.MESH
F32 = jnp.float32
BF16 = jnp.bfloat16
ANY = pl.BlockSpec(memory_space=pl.ANY)
VMEM = pl.BlockSpec(memory_space=pltpu.VMEM)
LIMIT = 62 << 20
QB = 256


def nn(a, b):
    return lax.dot_general(a, b, (((1,), (0,)), ((), ())), preferred_element_type=F32)


def nt(a, b):
    return lax.dot_general(a, b, (((1,), (1,)), ((), ())), preferred_element_type=F32)


def tn(a, b):
    return lax.dot_general(a, b, (((0,), (0,)), ((), ())), preferred_element_type=F32)


def normalize(rows):
    center = rows - jnp.mean(rows, -1, keepdims=True)
    inv = lax.rsqrt(jnp.mean(center * center, -1, keepdims=True) + EPS)
    return center * inv, inv


def norm_back(grad, gain, hat, inv):
    tilted = grad * gain
    first = jnp.mean(tilted, -1, keepdims=True)
    cross = jnp.mean(tilted * hat, -1, keepdims=True)
    return inv * (tilted - first - hat * cross)


def where_am_i():
    f = lax.axis_index("fsdp")
    z = lax.axis_index("seq")
    return f, z, f // 2, f % 2


def meet(peers):
    barrier = pltpu.get_barrier_semaphore()
    for peer in peers:
        pl.semaphore_signal(barrier, inc=1, device_id=peer, device_id_type=MESH)
    pl.semaphore_wait(barrier, len(peers))


def column_peers(seq):
    f, z, m, c = where_am_i()
    peers = []
    for dc in range(2):
        for dz in range(seq):
            if dc or dz:
                peers.append((m * 2 + (c + dc) % 2, (z + dz) % seq))
    return peers


class Ship:
    def __init__(self, src, dst, send, recv, target):
        f, z, _, _ = where_am_i()
        self.here = jnp.logical_and(target[0] == f, target[1] == z)
        self.local = pltpu.make_async_copy(src, dst, recv)
        self.remote = pltpu.make_async_remote_copy(
            src, dst, send, recv, device_id=target, device_id_type=MESH
        )

    def start(self):
        pl.when(self.here)(self.local.start)
        pl.when(jnp.logical_not(self.here))(self.remote.start)

    def wait_send(self):
        pl.when(jnp.logical_not(self.here))(self.remote.wait_send)


def remote(src, dst, send, recv, target):
    return pltpu.make_async_remote_copy(
        src, dst, send, recv, device_id=target, device_id_type=MESH
    )


class Gather:
    def __init__(self, send_ref, full_ref, send_sem, recv_sem, pass_send, pass_recv, seq):
        f, z, m, c = where_am_i()
        self.ships = []
        for i in range(2):
            for h in range(2):
                slot = 2 * c + i
                self.ships.append(
                    Ship(
                        send_ref.at[i, h],
                        full_ref.at[z, h],
                        send_sem.at[i, h],
                        recv_sem.at[z],
                        (m * 2 + h, slot),
                    )
                )
        other = (m * 2 + 1 - c, z)
        chips = [(z + d) % seq for d in range(seq)]
        self.arrivals = [
            remote(send_ref.at[0, 0], full_ref.at[k, c], send_sem.at[0, 0], recv_sem.at[k], other)
            for k in chips
        ]
        self.passes = [
            remote(full_ref.at[k, c], full_ref.at[k, c], pass_send.at[d], pass_recv.at[d], other)
            for d, k in enumerate(chips)
        ]
        self.handed = [
            remote(
                full_ref.at[k, c], full_ref.at[k, 1 - c], pass_send.at[d], pass_recv.at[d], other
            )
            for d, k in enumerate(chips)
        ]

    def start(self):
        for ship in self.ships:
            ship.start()

    def hand_on(self, k):
        self.arrivals[k].wait_recv()
        self.passes[k].start()

    def ready(self, k):
        self.handed[k].wait_recv()

    def finish(self):
        for ship in self.ships:
            ship.wait_send()
        for item in self.passes:
            item.wait_send()


GATHER_SEMS = lambda seq: [
    pltpu.SemaphoreType.DMA((2, 2)),
    pltpu.SemaphoreType.DMA((seq,)),
    pltpu.SemaphoreType.DMA((seq,)),
    pltpu.SemaphoreType.DMA((seq,)),
]


class Return:
    def __init__(self, own_ref, back_ref, send_sem, recv_sem, seq):
        f, z, m, c = where_am_i()
        home = z // 2
        self.ships = [
            Ship(
                own_ref.at[k],
                back_ref.at[z % 2, c],
                send_sem.at[k],
                recv_sem.at[z % 2, c],
                (m * 2 + home, k),
            )
            for k in range(seq)
        ]
        self.arrivals = [
            remote(
                own_ref.at[0],
                back_ref.at[i, h],
                send_sem.at[0],
                recv_sem.at[i, h],
                (m * 2 + 1 - c, z),
            )
            for i in range(2)
            for h in range(2)
        ]

    def start(self):
        for ship in self.ships:
            ship.start()

    def finish(self):
        for ship in self.ships:
            ship.wait_send()
        for item in self.arrivals:
            item.wait_recv()


RETURN_SEMS = lambda seq: [pltpu.SemaphoreType.DMA((seq,)), pltpu.SemaphoreType.DMA((2, 2))]


class Spread:
    def __init__(self, source, full_ref, send_sem, recv_sem, local_sem, stride):
        f, z, m, c = where_am_i()
        n_f = lax.axis_size("fsdp")
        steps = n_f // stride
        slot = f if stride == 1 else m
        self.local = pltpu.make_async_copy(source(f), full_ref.at[slot], local_sem)
        self.sends = []
        self.arrivals = []
        for d in range(1, steps):
            to = (f + d * stride) % n_f
            back = (f + n_f - d * stride) % n_f
            self.sends.append(
                remote(source(to), full_ref.at[slot], send_sem.at[d], recv_sem.at[d], (to, z))
            )
            place = back if stride == 1 else back // 2
            self.arrivals.append(
                remote(source(f), full_ref.at[place], send_sem.at[d], recv_sem.at[d], (to, z))
            )

    def start(self):
        self.local.start()
        for item in self.sends:
            item.start()

    def relay(self):
        pass

    def ready(self):
        self.local.wait()
        for item in self.arrivals:
            item.wait_recv()

    def finish(self):
        for item in self.sends:
            item.wait_send()


class Relay:
    def __init__(self, source, full_ref, send_sem, recv_sem, local_sem, stride):
        f, z, m, c = where_am_i()
        x, y = m % 2, m // 2
        beside, above, far = y * 2 + 1 - x, (1 - y) * 2 + x, (1 - y) * 2 + 1 - x

        def slot(chip, core):
            return chip * 2 + core if stride == 1 else chip

        self.local = pltpu.make_async_copy(source(f), full_ref.at[slot(m, c)], local_sem)
        self.sends, self.inner, self.near, self.relays, self.rest = [], [], [], [], []
        rows = full_ref.shape[1] // 2
        parts = [pl.ds(0, rows), pl.ds(rows, rows)]
        k = 0
        for dc in range(2 // stride):
            core = (c + dc) % 2
            chips = [beside, above] + ([m] if dc else [])
            for chip in chips:
                to = (chip * 2 + core, z)
                mine = full_ref.at[slot(m, c)]
                theirs = full_ref.at[slot(chip, core)]
                src = source(chip * 2 + core)
                self.sends.append(remote(src, mine, send_sem.at[k], recv_sem.at[k], to))
                got = remote(src, theirs, send_sem.at[k], recv_sem.at[k], to)
                (self.inner if chip is m else self.near).append(got)
                k += 1
            for chip, onto, part in ((beside, above, parts[0]), (above, beside, parts[1])):
                to = (onto * 2 + c, z)
                piece = full_ref.at[slot(chip, core), part]
                self.relays.append(remote(piece, piece, send_sem.at[k], recv_sem.at[k], to))
                lands = full_ref.at[slot(far, core), part]
                self.rest.append(remote(lands, lands, send_sem.at[k], recv_sem.at[k], to))
                k += 1

    def start(self):
        self.local.start()
        for item in self.sends:
            item.start()

    def relay(self):
        for item in self.near:
            item.wait_recv()
        for item in self.relays:
            item.start()

    def ready(self):
        self.local.wait()
        for item in self.inner + self.rest:
            item.wait_recv()

    def finish(self):
        for item in self.sends + self.relays:
            item.wait_send()


def spreading(source, full_ref, sems, stride):
    kind = Relay if lax.axis_size("fsdp") == 8 else Spread
    return kind(source, full_ref, *sems, stride)


def spread_sems(steps):
    steps = max(steps, 9)
    return [
        pltpu.SemaphoreType.DMA((steps,)),
        pltpu.SemaphoreType.DMA((steps,)),
        pltpu.SemaphoreType.DMA,
    ]


def fsdp_peers():
    f, z, _, _ = where_am_i()
    n_f = lax.axis_size("fsdp")
    return [((f + d) % n_f, z) for d in range(1, n_f)]


def all_peers(seq):
    f, z, m, c = where_am_i()
    other = m * 2 + 1 - c
    peers = fsdp_peers()
    for d in range(1, seq):
        peers.append((f, (z + d) % seq))
        peers.append((other, (z + d) % seq))
    return peers


class Scatter:
    def __init__(self, part, got_ref, send_sem, recv_sem):
        f, z, m, c = where_am_i()
        n_m = lax.axis_size("fsdp") // 2
        self.part, self.got, self.chip = part, got_ref, m
        self.copies = []
        for d in range(1, n_m):
            to = (m + d) % n_m
            self.copies.append(
                remote(
                    part(to),
                    got_ref.at[d - 1],
                    send_sem.at[d],
                    recv_sem.at[d],
                    (to * 2 + c, z),
                )
            )

    def start(self):
        for item in self.copies:
            item.start()

    def total(self, own):
        for item in self.copies:
            item.wait_recv()
        result = own.astype(F32)
        for k in range(len(self.copies)):
            result = result + self.got[k].astype(F32)
        return result

    def finish(self):
        for item in self.copies:
            item.wait_send()


def scatter_sems():
    n_m = lax.axis_size("fsdp") // 2
    return [pltpu.SemaphoreType.DMA((n_m,)), pltpu.SemaphoreType.DMA((n_m,))]


class Across:
    def __init__(self, own_ref, spare_ref, sems):
        f, z, _, _ = where_am_i()
        self.own, self.spare = own_ref, spare_ref
        self.edge = jnp.logical_or(z == 0, z == 3)
        self.inner = jnp.logical_not(self.edge)
        beside = jnp.where(z < 2, 1 - z, 5 - z)
        self.up = remote(own_ref, spare_ref.at[0], sems.at[0], sems.at[1], (f, beside))
        self.swap = remote(own_ref, spare_ref.at[1], sems.at[2], sems.at[3], (f, 3 - z))
        self.down = remote(own_ref, spare_ref.at[1], sems.at[4], sems.at[5], (f, beside))

    def add(self, k):
        total = self.own[...].astype(F32) + self.spare[k].astype(F32)
        self.own[...] = total.astype(self.own.dtype)

    def rise(self):
        pl.when(self.edge)(self.up.start)

    def risen(self):
        @pl.when(self.inner)
        def _():
            self.up.wait_recv()
            self.add(0)

        pl.when(self.edge)(self.up.wait_send)

    def cross(self):
        pl.when(self.inner)(self.swap.start)

    def crossed(self):
        @pl.when(self.inner)
        def _():
            self.swap.wait()
            self.add(1)

    def fall(self):
        pl.when(self.inner)(self.down.start)

    def fallen(self):
        @pl.when(self.edge)
        def _():
            self.down.wait_recv()
            self.own[...] = self.spare[1]

        pl.when(self.inner)(self.down.wait_send)


ACROSS_SEMS = pltpu.SemaphoreType.DMA((6,))


def project_kernel(
    seq, x_send, wqkv_send, wo_send,
    first_gain, first_shift, query_bias, value_bias, output_bias, second_gain, second_shift,
    outer_bias, inner_bias,
    x_full, n1_out, q_out, k_out, v_out, wqkv_out, wo_out, vecs_out, ibias_out,
    ssem, rsem, psend, precv,
    qsend, qrecv, qlocal, osend, orecv, olocal, vsend, vrecv, vlocal,
    xv, wqkv, small, smalls, lsem, wsem,
):
    f, z, m, c = where_am_i()
    n_f = lax.axis_size("fsdp")
    share = first_gain.shape[1]
    piece = inner_bias.shape[1]
    small[...] = jnp.zeros_like(small)
    for r, ref in enumerate(
        (
            first_gain,
            first_shift,
            query_bias,
            value_bias,
            output_bias,
            second_gain,
            second_shift,
            outer_bias,
        )
    ):
        small[r : r + 1, :share] = ref[...].astype(F32)
    small[8:9, :piece] = inner_bias[...].astype(F32)
    meet(all_peers(seq))
    gather = Gather(x_send, xv, ssem, rsem, psend, precv, seq)
    vectors = Spread(lambda to: small, smalls, vsend, vrecv, vlocal, 1)
    weights = spreading(lambda to: wqkv_send.at[to % 2], wqkv, (qsend, qrecv, qlocal), 1)
    later = spreading(lambda to: wo_send, wo_out, (osend, orecv, olocal), 1)
    vectors.start()
    gather.start()
    weights.start()
    half = xv.shape[2]
    mine = q_out.shape[1]
    width = n1_out.shape[1]

    vectors.ready()
    row = lax.broadcasted_iota(jnp.int32, (128, width), 0)
    col = lax.broadcasted_iota(jnp.int32, (128, width), 1)
    vecs = jnp.zeros((16, width), F32)
    for k in range(n_f):
        spot = jnp.logical_and(col - k * share == row, row < share)
        vecs = vecs + nn(
            smalls[k, :, :128].astype(BF16), jnp.where(spot, 1.0, 0.0).astype(BF16)
        )
    vecs_out[...] = vecs[:8]
    for k in range(n_f // 2):
        ibias_out[0:1, k * piece : (k + 1) * piece] = smalls[2 * k + c, 8:9, :piece]
    weights.relay()
    later.start()
    weights.ready()
    keep_weights = pltpu.make_async_copy(wqkv, wqkv_out, wsem)
    keep_weights.start()
    gain = vecs_out[0:1, :]
    shift = vecs_out[1:2, :]
    cols = pl.ds(pl.multiple_of(c * mine, 128), mine)
    qb = vecs_out[2:3, cols]
    vb = vecs_out[3:4, cols]
    keeps = []
    for d in sorted(range(seq), key=lambda d: min(d, seq - d)):
        k = (z + d) % seq
        gather.hand_on(d)
        gather.ready(d)
        keeps.append(pltpu.make_async_copy(xv.at[k], x_full.at[k], lsem.at[d]))
        keeps[-1].start()
        rows = pl.ds(pl.multiple_of(k * 2 * half, 16), 2 * half)
        hat, _ = normalize(xv[k].reshape(2 * half, width).astype(F32))
        normed = (hat * gain + shift).astype(BF16)
        n1_out[rows, :] = normed
        qkv = nn(normed, wqkv[...].reshape(width, 3 * mine))
        q_out[rows, :] = (qkv[:, :mine] + qb).astype(BF16)
        k_out[rows, :] = qkv[:, mine : 2 * mine].astype(BF16)
        v_out[rows, :] = (qkv[:, 2 * mine :] + vb).astype(BF16)
        if d == 1:
            later.relay()
    gather.finish()
    for item in keeps:
        item.wait()
    later.ready()
    vectors.finish()
    weights.finish()
    later.finish()
    keep_weights.wait()


def project(x_send, wqkv_send, wo_send, vectors, seq):
    _, _, half, width = x_send.shape
    n_f = lax.axis_size("fsdp")
    rows = seq * 2 * half
    share = wo_send.shape[0]
    mine = wqkv_send.shape[2] // 3
    piece = vectors[-1].shape[1]
    lanes = max(128, piece)
    return pl.pallas_call(
        lambda *refs: project_kernel(seq, *refs),
        in_specs=[ANY] * 3 + [VMEM] * 9,
        out_specs=[ANY, VMEM, VMEM, VMEM, VMEM, ANY, ANY, VMEM, VMEM],
        out_shape=[
            jax.ShapeDtypeStruct((seq, 2, half, width), BF16),
            jax.ShapeDtypeStruct((rows, width), BF16),
        ]
        + [jax.ShapeDtypeStruct((rows, mine), BF16)] * 3
        + [
            jax.ShapeDtypeStruct((n_f, share, 3 * mine), BF16),
            jax.ShapeDtypeStruct((n_f, share, width), BF16),
            jax.ShapeDtypeStruct((8, width), F32),
            jax.ShapeDtypeStruct((1, piece * n_f // 2), F32),
        ],
        scratch_shapes=GATHER_SEMS(seq)
        + spread_sems(n_f)
        + spread_sems(n_f)
        + spread_sems(n_f)
        + [
            pltpu.VMEM((seq, 2, half, width), BF16),
            pltpu.VMEM((n_f, share, 3 * mine), BF16),
            pltpu.VMEM((16, lanes), F32),
            pltpu.VMEM((n_f, 16, lanes), F32),
            pltpu.SemaphoreType.DMA((seq,)),
            pltpu.SemaphoreType.DMA,
        ],
        compiler_params=pltpu.CompilerParams(
            collective_id=0, has_side_effects=True, vmem_limit_bytes=LIMIT
        ),
        name="project",
    )(x_send, wqkv_send, wo_send, *vectors)


def project_plain_kernel(seq, x_send, wqkv, vecs, x_full, n1_out, q_out, k_out, v_out,
                         ssem, rsem, psend, precv, xv, lsem):
    f, z, m, c = where_am_i()
    meet(column_peers(seq))
    gather = Gather(x_send, x_full, ssem, rsem, psend, precv, seq)
    gather.start()
    half = xv.shape[1]
    mine = q_out.shape[1]
    for d in range(seq):
        gather.hand_on(d)
    for d in range(seq):
        gather.ready(d)
    gain = vecs[0:1, :]
    shift = vecs[1:2, :]
    cols = pl.ds(pl.multiple_of(c * mine, 128), mine)
    qb = vecs[2:3, cols]
    vb = vecs[3:4, cols]
    for k in range(seq):
        copy = pltpu.make_async_copy(x_full.at[k], xv, lsem)
        copy.start()
        copy.wait()
        rows = pl.ds(k * 2 * half, 2 * half)
        hat, _ = normalize(xv[...].reshape(2 * half, -1).astype(F32))
        normed = (hat * gain + shift).astype(BF16)
        n1_out[rows, :] = normed
        qkv = nn(normed, wqkv[...])
        q_out[rows, :] = (qkv[:, :mine] + qb).astype(BF16)
        k_out[rows, :] = qkv[:, mine : 2 * mine].astype(BF16)
        v_out[rows, :] = (qkv[:, 2 * mine :] + vb).astype(BF16)
    gather.finish()


def project_plain(x_send, wqkv, vecs, seq):
    _, _, half, width = x_send.shape
    rows = seq * 2 * half
    mine = wqkv.shape[1] // 3
    return pl.pallas_call(
        lambda *refs: project_plain_kernel(seq, *refs),
        in_specs=[ANY, VMEM, VMEM],
        out_specs=[ANY, VMEM, VMEM, VMEM, VMEM],
        out_shape=[
            jax.ShapeDtypeStruct((seq, 2, half, width), BF16),
            jax.ShapeDtypeStruct((rows, width), BF16),
        ]
        + [jax.ShapeDtypeStruct((rows, mine), BF16)] * 3,
        scratch_shapes=GATHER_SEMS(seq)
        + [pltpu.VMEM((2, half, width), BF16), pltpu.SemaphoreType.DMA],
        compiler_params=pltpu.CompilerParams(
            collective_id=5, has_side_effects=True, vmem_limit_bytes=LIMIT
        ),
        name="project_plain",
    )(x_send, wqkv, vecs)


def attend_kernel(
    seq, local, pairs, cot_send, wi_send, q, k, v,
    e_out, o_out, linv_out, mixed_out, cot_full, wi_out,
    ssem, rsem, psend, precv, isend, irecv, ilocal,
    stage, qa, ka, va, msend, mrecv, mlocal,
):
    f, z, m, c = where_am_i()
    pair = pl.program_id(0)
    rows = q.shape[0]
    gather = Gather(cot_send, cot_full, ssem, rsem, psend, precv, seq)
    weights = spreading(lambda to: wi_send.at[to % 2], wi_out, (isend, irecv, ilocal), 1)
    other = (m * 2 + 1 - c, z)

    @pl.when(pair == 0)
    def _():
        meet(all_peers(seq))
        gather.start()
        weights.start()

    pl.when(pair == pairs - 1)(weights.relay)

    lane = lax.broadcasted_iota(jnp.int32, (1, 128), 1)
    low = lane < HD
    place = lax.broadcasted_iota(jnp.int32, (rows, 1), 0) % (rows // seq)
    bar = jnp.where(place < local, 0.0, -1e38).astype(F32)
    qf, kf, vf = q[...].astype(F32), k[...].astype(F32), v[...].astype(F32)
    for a in range(2):
        mine = low if a == 0 else jnp.logical_not(low)
        first = lane == HD * (1 - a)
        qa[a] = jnp.where(mine, qf, jnp.where(first, 1.0, 0.0)).astype(BF16)
        ka[a] = jnp.where(mine, kf, jnp.where(first, bar, 0.0)).astype(BF16)
        va[a] = jnp.where(mine, vf, 1.0).astype(BF16)
    factor = HD ** (-0.5) * math.log2(math.e)
    steps = [(i, a) for i in range(rows // QB) for a in range(2)]

    def block(i):
        return slice(i * QB, (i + 1) * QB)

    def scored(t):
        i, a = steps[t]
        return nt(qa[a, block(i), :], ka[a])

    raws = {}

    def finish(t, expo):
        i, a = steps[t]
        raws[a] = nn(expo, va[a])
        if a == 1:
            sl = block(i)
            total = pltpu.roll(jnp.where(low, raws[1], raws[0]), HD, 1)
            inv = 1.0 / total
            res = jnp.where(low, raws[0], raws[1]) * inv
            o_out[sl, :] = res
            linv_out[sl, :] = inv
            stage[pair, sl, :] = res.astype(BF16)

    scores, before = scored(0), None
    for t, (i, a) in enumerate(steps):
        peak = jnp.max(scores, -1, keepdims=True)
        upcoming = scored(t + 1) if t + 1 < len(steps) else None
        if before is not None:
            finish(t - 1, before)
        expo = jnp.exp2((scores - peak) * factor).astype(BF16)
        e_out[a, block(i), :] = expo
        scores, before = upcoming, expo
    finish(len(steps) - 1, before)

    def mixed_copies(p):
        return (
            pltpu.make_async_copy(stage.at[p], mixed_out.at[c, p], mlocal.at[p]),
            remote(stage.at[p], mixed_out.at[c, p], msend.at[p], mrecv.at[p], other),
            remote(stage.at[p], mixed_out.at[1 - c, p], msend.at[p], mrecv.at[p], other),
        )

    here, there, _ = mixed_copies(pair)
    here.start()
    there.start()

    @pl.when(pair == pairs - 1)
    def _():
        for item in range(seq):
            gather.hand_on(item)
        weights.ready()
        weights.finish()
        for item in range(seq):
            gather.ready(item)
        gather.finish()
        for p in range(pairs):
            here, there, back = mixed_copies(p)
            here.wait()
            there.wait_send()
            back.wait_recv()


def attend(cot_send, wi_send, q, k, v, local, seq):
    rows, mine = q.shape
    n_f = lax.axis_size("fsdp")
    _, _, half, width = cot_send.shape
    pairs = mine // 128
    by_pair = pl.BlockSpec((rows, 128), lambda p: (0, p))
    return pl.pallas_call(
        lambda *refs: attend_kernel(seq, local, pairs, *refs),
        grid=(pairs,),
        in_specs=[ANY, ANY, by_pair, by_pair, by_pair],
        out_specs=[
            pl.BlockSpec((2, rows, rows), lambda p: (p, 0, 0)),
            by_pair,
            by_pair,
            ANY,
            ANY,
            ANY,
        ],
        out_shape=[
            jax.ShapeDtypeStruct((2 * pairs, rows, rows), BF16),
            jax.ShapeDtypeStruct((rows, mine), F32),
            jax.ShapeDtypeStruct((rows, mine), F32),
            jax.ShapeDtypeStruct((2, pairs, rows, 128), BF16),
            jax.ShapeDtypeStruct((seq, 2, half, width), BF16),
            jax.ShapeDtypeStruct((n_f,) + wi_send.shape[1:], BF16),
        ],
        scratch_shapes=GATHER_SEMS(seq)
        + spread_sems(n_f)
        + [
            pltpu.VMEM((pairs, rows, 128), BF16),
            pltpu.VMEM((2, rows, 128), BF16),
            pltpu.VMEM((2, rows, 128), BF16),
            pltpu.VMEM((2, rows, 128), BF16),
            pltpu.SemaphoreType.DMA((pairs,)),
            pltpu.SemaphoreType.DMA((pairs,)),
            pltpu.SemaphoreType.DMA((pairs,)),
        ],
        compiler_params=pltpu.CompilerParams(
            collective_id=1, has_side_effects=True, vmem_limit_bytes=LIMIT
        ),
        name="attend",
    )(cot_send, wi_send, q, k, v)


def gelu_parts(u):
    x = jnp.abs(u) * (1.0 / math.sqrt(2.0))
    t = 1.0 / (1.0 + 0.3275911 * x)
    poly = t * (
        0.254829592
        + t * (-0.284496736 + t * (1.421413741 + t * (-1.453152027 + t * 1.061405429)))
    )
    expo = jnp.exp(-x * x)
    tail = 0.5 * poly * expo
    phi = jnp.where(u >= 0, 1.0 - tail, tail)
    return phi, u * expo * (1.0 / math.sqrt(2.0 * math.pi))


def dense_kernel(
    seq, x, mixed_in, cot_in, wo_in, wi_in, wu_send, vecs, ibias,
    out_back, gres_own, gm_out, gwo_out, gwi_out, ru_out, gvec_out, gib_out,
    xv, mixed, cot, wo, wi, wu, n2, hat2, inv2, resid, active, slope, out_own,
    pstage, precv, grecv, ugot, upart,
    psem, prsem, gsem, grsem, bsend, brecv, usend, urecv, wsend, wrecv, wlocal, lsem, xsem,
):
    f, z, m, c = where_am_i()
    other = (m * 2 + 1 - c, z)
    half = x.shape[2]
    chunk = 2 * half
    width = x.shape[3]
    mine = gm_out.shape[1]
    hidden = wi.shape[1]
    n_m = gwi_out.shape[0]
    share = gwi_out.shape[2]
    piece = upart.shape[1]
    rows = seq * chunk
    tile = 512

    def block(i):
        return pl.ds(i * chunk, chunk)

    def fetch_x(i):
        return pltpu.make_async_copy(x.at[i], xv.at[i % 2], xsem.at[i % 2])

    loads = [
        pltpu.make_async_copy(src, dst, lsem.at[k])
        for k, (src, dst) in enumerate(
            ((mixed_in, mixed), (wo_in, wo), (wi_in, wi), (cot_in, cot))
        )
    ]
    fetch_x(0).start()
    for item in loads:
        item.start()
    meet(all_peers(seq))
    weights = spreading(lambda to: wu_send, wu, (wsend, wrecv, wlocal), 2)
    weights.start()
    obias, gain, shift, ubias = vecs[4:5, :], vecs[5:6, :], vecs[6:7, :], vecs[7:8, :]
    back = Return(out_own, out_back, bsend, brecv, seq)
    gstage = active.at[:, :width]
    branch = active.at[:, width : 2 * width]
    gown = resid

    def p_copy(i):
        return remote(pstage.at[i, 1 - c], precv.at[i], psem.at[i], prsem.at[i], other)

    def g_copy(i):
        return remote(gstage.at[block(i)], grecv.at[block(i)], gsem.at[i], grsem.at[i], other)

    def mixed_rows(sl):
        return jnp.concatenate(
            [mixed[a, p, sl, :] for a in range(2) for p in range(mixed.shape[1])], axis=1
        )

    for item in loads[:3]:
        item.wait()
    for i in range(seq):
        sl = block(i)
        fetch_x(i).wait()
        if i + 1 < seq:
            fetch_x(i + 1).start()
        frames = xv[i % 2].reshape(chunk, width).astype(F32)
        res = frames + nn(mixed_rows(sl), wo[...]) + obias
        hat, inv = normalize(res)
        normed = (hat * gain + shift).astype(BF16)
        resid[sl, :] = res + ubias
        n2[sl, :] = normed
        hat2[sl, :] = hat
        inv2[sl, :] = jnp.broadcast_to(inv, (chunk, 128))
        for j in range(0, hidden, tile):
            cols = slice(j, j + tile)
            inner = nn(normed, wi[:, cols]) + ibias[:, cols]
            phi, bump = gelu_parts(inner)
            active[sl, cols] = (inner * phi).astype(BF16)
            slope[sl, cols] = (phi + bump).astype(BF16)
        if i == seq // 2:
            weights.relay()
    weights.ready()
    loads[3].wait()
    wuf = wu.at[...]

    def outer_weight():
        return wuf[...].reshape(hidden, width)

    for i in range(seq):
        sl = block(i)
        pout = nn(active[sl, :], outer_weight())
        resid[sl, :] += pout
        pstage[i] = pout.astype(BF16).reshape(2, half, width)
        p_copy(i).start()
    cots = cot[...].reshape(rows, width)
    outer = Scatter(lambda to: upart.at[to], ugot, usend, urecv)
    if piece % 128 == 0:
        for d in range(n_m):
            k = (m + 1 + d) % n_m
            at = pl.ds(pl.multiple_of(k * piece, 128), piece)
            upart[k] = tn(active[:, at], cots).astype(BF16)
            if d < n_m - 1:
                outer.copies[d].start()
    else:
        for k in range(n_m):
            upart[k] = tn(active[:, k * piece : (k + 1) * piece], cots).astype(BF16)
        outer.start()
    for i in range(seq):
        p_copy(i).wait_recv()
        out_own[i] = (
            resid[pl.ds(pl.multiple_of(i * chunk + c * half, 16), half), :]
            + precv[i].astype(F32)
        ).astype(BF16)
    back.start()
    gvec_out[0:1, :] = jnp.sum(cots.astype(F32), 0, keepdims=True)
    for i in range(seq):
        sl = block(i)
        g = cot[i].reshape(chunk, width)
        for j in range(0, hidden, piece):
            cols = slice(j, j + piece)
            gi = (nt(g, wu[j // piece]) * slope[sl, cols].astype(F32)).astype(BF16)
            slope[sl, cols] = gi
            line = jnp.sum(gi.astype(F32), 0, keepdims=True)
            if i == 0:
                gib_out[:, cols] = line
            else:
                gib_out[:, cols] += line
        gn2 = nt(slope[sl, :], wi[...])
        gown[sl, :] = gn2
        gstage[sl, :] = gn2.astype(BF16)
        g_copy(i).start()
    for j in range(0, hidden, tile):
        part = tn(n2[...], slope[:, j : j + tile])
        for k in range(n_m):
            for b in range(2):
                at = (2 * k + b) * share
                gwi_out[k, b, :, j : j + tile] = part[at : at + share, :].astype(BF16)
    wrows = pl.ds(pl.multiple_of(c * mine, 128), mine)
    for i in range(seq):
        sl = block(i)
        g_copy(i).wait_recv()
        gn2 = gown[sl, :] + grecv[sl, :].astype(F32)
        hat = hat2[sl, :]
        line = jnp.sum(gn2 * hat, 0, keepdims=True)
        flat = jnp.sum(gn2, 0, keepdims=True)
        g = cot[i].reshape(chunk, width).astype(F32)
        gres = g + norm_back(gn2, gain, hat, inv2[sl, 0:1])
        hat2[sl, :] = gres
        low = gres.astype(BF16)
        branch[sl, :] = low
        total = jnp.sum(low.astype(F32), 0, keepdims=True)
        if i == 0:
            lines, flats, totals = line, flat, total
        else:
            lines, flats, totals = lines + line, flats + flat, totals + total
        gm_out[sl, :] = nt(low, wo[wrows, :]).astype(BF16)
        gres_own[i] = hat2[pl.ds(pl.multiple_of(i * chunk + c * half, 16), half), :]
    gvec_out[1:2, :] = lines
    gvec_out[2:3, :] = flats
    gvec_out[3:4, :] = totals
    gvec_out[4:8, :] = jnp.zeros((4, width), F32)
    part = tn(
        mixed_rows(slice(None)),
        active[:, pl.ds(pl.multiple_of(width + c * mine, 128), mine)],
    )
    for k in range(n_m):
        for b in range(2):
            at = (2 * k + b) * share
            gwo_out[k, b] = part[at : at + share, :].astype(BF16)
    for i in range(seq):
        p_copy(i).wait_send()
        g_copy(i).wait_send()
    weights.finish()
    ru_out[...] = outer.total(upart[m]).astype(BF16)
    outer.finish()
    back.finish()


def dense(x, mixed, cot, wo, wi, wu_send, vecs, ibias):
    seq, _, half, width = x.shape
    rows = seq * 2 * half
    hidden = wi.shape[1]
    mine = width // 2
    n_f = lax.axis_size("fsdp")
    n_m = n_f // 2
    share = width // n_f
    piece = hidden // n_m
    return pl.pallas_call(
        lambda *refs: dense_kernel(seq, *refs),
        in_specs=[ANY] * 6 + [VMEM] * 2,
        out_specs=[ANY] + [VMEM] * 7,
        out_shape=[
            jax.ShapeDtypeStruct((2, 2, half, width), BF16),
            jax.ShapeDtypeStruct((seq, half, width), F32),
            jax.ShapeDtypeStruct((rows, mine), BF16),
            jax.ShapeDtypeStruct((n_m, 2, share, mine), BF16),
            jax.ShapeDtypeStruct((n_m, 2, share, hidden), BF16),
            jax.ShapeDtypeStruct((piece, width), BF16),
            jax.ShapeDtypeStruct((8, width), F32),
            jax.ShapeDtypeStruct((1, hidden), F32),
        ],
        scratch_shapes=[
            pltpu.VMEM((2, 2, half, width), BF16),
            pltpu.VMEM(mixed.shape, BF16),
            pltpu.VMEM(cot.shape, BF16),
            pltpu.VMEM(wo.shape, BF16),
            pltpu.VMEM(wi.shape, BF16),
            pltpu.VMEM((n_m, piece, width), BF16),
            pltpu.VMEM((rows, width), BF16),
            pltpu.VMEM((rows, width), F32),
            pltpu.VMEM((rows, 128), F32),
            pltpu.VMEM((rows, width), F32),
            pltpu.VMEM((rows, hidden), BF16),
            pltpu.VMEM((rows, hidden), BF16),
            pltpu.VMEM((seq, half, width), BF16),
            pltpu.VMEM((seq, 2, half, width), BF16),
            pltpu.VMEM((seq, half, width), BF16),
            pltpu.VMEM((rows, width), BF16),
            pltpu.VMEM((n_m - 1, piece, width), BF16),
            pltpu.VMEM((n_m, piece, width), BF16),
            pltpu.SemaphoreType.DMA((seq,)),
            pltpu.SemaphoreType.DMA((seq,)),
            pltpu.SemaphoreType.DMA((seq,)),
            pltpu.SemaphoreType.DMA((seq,)),
        ]
        + RETURN_SEMS(seq)
        + scatter_sems()
        + spread_sems(n_m)
        + [pltpu.SemaphoreType.DMA((4,)), pltpu.SemaphoreType.DMA((2,))],
        compiler_params=pltpu.CompilerParams(
            collective_id=2, has_side_effects=True, vmem_limit_bytes=LIMIT
        ),
        name="dense",
    )(x, mixed, cot, wo, wi, wu_send, vecs, ibias)


def attend_back_kernel(
    seq, pairs, gwi, gwo, ru, q, k, v, gm, o, linv, e,
    gq_out, gk_out, gv_out, ri_out, ro_out, gwu_out,
    asend, arecv, bsend, brecv, osend, orecv, zu, za, zb,
    uown, uspare, aown, aspare, bown, bspare, igot, ogot, oown, lsem,
    do, dot_, qt, va, km, dvt, dkt,
):
    pair = pl.program_id(0)
    rows = q.shape[0]
    m = lax.axis_index("fsdp") // 2
    inner = [
        Scatter(lambda to: gwi.at[to, 0], igot.at[0], asend, arecv),
        Scatter(lambda to: gwi.at[to, 1], igot.at[1], bsend, brecv),
    ]
    out = Scatter(lambda to: gwo.at[to], ogot, osend, orecv)
    outer = Across(uown, uspare, zu)
    halves = [Across(aown, aspare, za), Across(bown, bspare, zb)]
    loads = [
        pltpu.make_async_copy(src, dst, lsem.at[k])
        for k, (src, dst) in enumerate(
            ((ru, uown), (gwi.at[m, 0], aown), (gwi.at[m, 1], bown), (gwo.at[m], oown))
        )
    ]

    def sum_half(k):
        own = halves[k].own
        own[...] = inner[k].total(own[...]).astype(BF16)

    def at(step, place, action):
        def run():
            pl.when(pair == step)(action)

        events.setdefault(place, []).append(run)

    events = {}

    def begin():
        for item in loads:
            item.start()
        meet(all_peers(seq))
        inner[0].start()
        for item in loads:
            item.wait()
        outer.rise()

    def one():
        outer.risen()
        outer.cross()

    def two():
        inner[1].start()
        outer.crossed()
        outer.fall()

    def three():
        sum_half(0)
        halves[0].rise()

    def four():
        out.start()
        halves[0].risen()
        halves[0].cross()

    def five():
        sum_half(1)
        halves[1].rise()
        outer.fallen()
        gwu_out[...] = uown[...].astype(F32)

    at(0, 0, begin)
    at(0, 1, one)
    at(1, 0, two)
    at(1, 1, three)
    at(2, 0, four)
    at(2, 1, five)
    for run in events[0]:
        run()
    third = HD ** (-0.5)
    lane = lax.broadcasted_iota(jnp.int32, (1, 128), 1)
    low = lane < HD
    scaled = (gm[...].astype(F32) * linv[...]).astype(BF16).astype(F32)
    kf, vf = k[...].astype(F32), v[...].astype(F32)
    weighted = scaled * o[...]
    for a in range(2):
        mine = low if a == 0 else jnp.logical_not(low)
        delta = jnp.sum(jnp.where(mine, weighted, 0.0), -1, keepdims=True)
        high = delta.astype(BF16).astype(F32)
        middle = (delta - high).astype(BF16).astype(F32)
        last = delta - high - middle
        base = HD * (1 - a)
        extra = jnp.where(
            lane == base, high, jnp.where(lane == base + 1, middle, jnp.where(lane == base + 2, last, 0.0))
        )
        do[a] = jnp.where(mine, scaled, -extra).astype(BF16)
        va[a] = jnp.where(mine, vf, 1.0).astype(BF16)
        km[a] = jnp.where(mine, kf, 0.0).astype(BF16)
    dot_[...] = scaled.astype(BF16).T
    qt[...] = q[...].T
    steps = [(i, a) for i in range(rows // QB) for a in range(2)]

    def block(i):
        return slice(i * QB, (i + 1) * QB)

    def sub(a):
        return slice(a * HD, (a + 1) * HD)

    def pushed(t):
        i, a = steps[t]
        return nt(do[a, block(i), :], va[a])

    dqs = {}
    grads = pushed(0)
    for t, (i, a) in enumerate(steps):
        if t == len(steps) // 2:
            for run in events[1]:
                run()
        sl = block(i)
        p = e[a, sl, :]
        ds = (p.astype(F32) * grads).astype(BF16)
        grads = pushed(t + 1) if t + 1 < len(steps) else None
        dv = nn(dot_[sub(a), sl], p)
        dk = nn(qt[sub(a), sl], ds)
        dqs[a] = nn(ds, km[a])
        if i == 0:
            dvt[sub(a), :] = dv
            dkt[sub(a), :] = dk
        else:
            dvt[sub(a), :] += dv
            dkt[sub(a), :] += dk
        if a == 1:
            gq_out[sl, :] = ((dqs[0] + dqs[1]) * third).astype(BF16)
    gv_out[...] = dvt[...].astype(BF16).T
    gk_out[...] = (dkt[...] * third).astype(BF16).T

    @pl.when(pair == pairs - 1)
    def _():
        halves[0].crossed()
        ro_out[...] = out.total(oown[...]).astype(BF16)
        halves[1].risen()
        ri_out[0] = aown[...]
        ri_out[1] = bown[...]
        for item in inner + [out]:
            item.finish()


def attend_back(gwi, gwo, ru, q, k, v, gm, o, linv, e, seq):
    rows, mine = q.shape
    pairs = mine // 128
    n_m = gwi.shape[0]
    piece, width = ru.shape
    by_pair = pl.BlockSpec((rows, 128), lambda p: (0, p))
    return pl.pallas_call(
        lambda *refs: attend_back_kernel(seq, pairs, *refs),
        grid=(pairs,),
        in_specs=[ANY] * 3
        + [by_pair] * 6
        + [pl.BlockSpec((2, rows, rows), lambda p: (p, 0, 0))],
        out_specs=[by_pair] * 3
        + [
            pl.BlockSpec(gwi.shape[1:], lambda p: (0, 0, 0)),
            pl.BlockSpec(gwo.shape[1:], lambda p: (0, 0, 0)),
            pl.BlockSpec((piece, width), lambda p: (0, 0)),
        ],
        out_shape=[jax.ShapeDtypeStruct((rows, mine), BF16)] * 3
        + [
            jax.ShapeDtypeStruct(gwi.shape[1:], BF16),
            jax.ShapeDtypeStruct(gwo.shape[1:], BF16),
            jax.ShapeDtypeStruct((piece, width), F32),
        ],
        scratch_shapes=scatter_sems()
        + scatter_sems()
        + scatter_sems()
        + [ACROSS_SEMS] * 3
        + [
            pltpu.VMEM((piece, width), BF16),
            pltpu.VMEM((2, piece, width), BF16),
            pltpu.VMEM(gwi.shape[2:], BF16),
            pltpu.VMEM((2,) + gwi.shape[2:], BF16),
            pltpu.VMEM(gwi.shape[2:], BF16),
            pltpu.VMEM((2,) + gwi.shape[2:], BF16),
            pltpu.VMEM((2, n_m - 1) + gwi.shape[2:], BF16),
            pltpu.VMEM((n_m - 1,) + gwo.shape[1:], BF16),
            pltpu.VMEM(gwo.shape[1:], BF16),
            pltpu.SemaphoreType.DMA((4,)),
            pltpu.VMEM((2, rows, 128), BF16),
            pltpu.VMEM((128, rows), BF16),
            pltpu.VMEM((128, rows), BF16),
            pltpu.VMEM((2, rows, 128), BF16),
            pltpu.VMEM((2, rows, 128), BF16),
            pltpu.VMEM((128, rows), F32),
            pltpu.VMEM((128, rows), F32),
        ],
        compiler_params=pltpu.CompilerParams(
            collective_id=3, has_side_effects=True, vmem_limit_bytes=LIMIT
        ),
        name="attend_back",
    )(gwi, gwo, ru, q, k, v, gm, o, linv, e)


def project_back_kernel(
    seq, x_in, n1_in, gq_in, gk_in, gv_in, gres_in, wqkv_in, vecs, gvec, gib, ri_in, ro_in,
    gwq_out, gwk_out, gwv_out, gwo_out, gwi_out,
    fg_out, fs_out, qb_out, vb_out, ob_out, sg_out, ss_out, ub_out, ib_out, ig_back,
    x, n1, grads, gres, wqkv, gown, gstage, grecv, ig_own, qpart, qgot, vgot,
    ri, ispare, ito, ra, aspare, ato, vown, vspare, vto,
    gsem, grsem, bsend, brecv, qsend, qrecv, vsend, vrecv, zi, za, zv, pair_sems, lsem,
):
    f, z, m, c = where_am_i()
    other = (m * 2 + 1 - c, z)
    half = gres.shape[1]
    chunk = 2 * half
    width = gres.shape[2]
    rows = seq * chunk
    mine = width // 2
    n_m = qpart.shape[1]
    share = ri.shape[1]
    hidden = ri.shape[2]
    piece = hidden // n_m
    loads = [
        pltpu.make_async_copy(src, dst, lsem.at[k])
        for k, (src, dst) in enumerate(
            (
                (gq_in, grads.at[:, :mine]),
                (gk_in, grads.at[:, mine : 2 * mine]),
                (gv_in, grads.at[:, 2 * mine :]),
                (wqkv_in, wqkv),
                (ri_in, ri),
                (ro_in, ra.at[3]),
                (n1_in, n1),
                (gres_in, gres),
                (x_in.at[:, c], x),
            )
        )
    ]
    for item in loads:
        item.start()
    meet(all_peers(seq))
    gain = vecs[0:1, :]
    inner = [Across(ri.at[k], ispare.at[k], zi.at[k]) for k in range(2)]
    parts = [Across(ra.at[k], aspare.at[k], za.at[k]) for k in range(4)]
    vectors = Across(vown, vspare, zv)
    queries = [
        Scatter(lambda to, k=k: qpart.at[k, to], qgot.at[k], qsend.at[k], qrecv.at[k])
        for k in range(3)
    ]
    vspread = Scatter(lambda to: vown, vgot, vsend, vrecv)
    back = Return(ig_own, ig_back, bsend, brecv, seq)

    def g_copy(i):
        return remote(gstage.at[i, 1 - c], grecv.at[i], gsem.at[i], grsem.at[i], other)

    def pass_on(k, src, dst):
        return remote(src, dst, pair_sems.at[0, k], pair_sems.at[1, k], other)

    for item in loads[:6]:
        item.wait()
    inner[0].fall()
    inner[1].cross()
    parts[3].rise()
    for i in range(seq):
        gn1 = nt(grads[i * chunk : (i + 1) * chunk, :], wqkv[...])
        gown[i] = gn1.reshape(2, half, width)
        gstage[i] = gn1.astype(BF16).reshape(2, half, width)
        g_copy(i).start()
    for item in loads[6:]:
        item.wait()

    def weight(k):
        part = tn(n1[...], grads[:, k * mine : (k + 1) * mine])
        for j in range(n_m):
            for b in range(2):
                at = (2 * j + b) * share
                qpart[k, j, b] = part[at : at + share, :].astype(BF16)
        queries[k].start()

    weight(0)
    for k in range(seq):
        g_copy(k).wait_recv()
        gn1 = gown[k, c] + grecv[k].astype(F32)
        hat, inv = normalize(x[k].astype(F32))
        line = jnp.sum(gn1 * hat, 0, keepdims=True)
        flat = jnp.sum(gn1, 0, keepdims=True)
        if k == 0:
            gain_sum, shift_sum = line, flat
        else:
            gain_sum, shift_sum = gain_sum + line, shift_sum + flat
        ig_own[k] = (gres[k] + norm_back(gn1, gain, hat, inv)).astype(BF16)
        back.ships[k].start()
    vown[...] = jnp.zeros_like(vown)
    vown[0:1, :] = gain_sum
    vown[1:2, :] = shift_sum
    cols = pl.ds(pl.multiple_of(c * mine, 128), mine)
    vown[2:3, cols] = jnp.sum(grads[:, :mine].astype(F32), 0, keepdims=True)
    vown[3:4, cols] = jnp.sum(grads[:, 2 * mine :].astype(F32), 0, keepdims=True)
    for k, r in enumerate((3, 1, 2, 0)):
        vown[4 + k : 5 + k, :] = 0.5 * gvec[r : r + 1, :]
    lines = hidden // width
    for k in range(lines):
        vown[pl.ds(8 + lines * c + k, 1), :] = gib[:, k * width : (k + 1) * width]
    vspread.start()
    weight(1)
    parts[3].risen()
    parts[3].cross()
    weight(2)
    inner[1].crossed()
    inner[1].fall()
    total = vspread.total(vown[...])
    vspread.finish()
    vown[...] = total
    vectors.rise()
    parts[3].crossed()
    parts[3].fall()
    for k in range(3):
        ra[k] = queries[k].total(qpart[k, m]).astype(BF16)
        parts[k].rise()
    vectors.risen()
    vectors.cross()
    crosses = {}

    def hand_over(k, src, dst):
        crosses[k] = pass_on(k, src, dst)
        crosses[k].start()

    for k in range(2):
        inner[k].fallen()
        pl.when(c != k)(pass_on(k, ri.at[k], ito).start)
    for k in range(3):
        parts[k].risen()
        parts[k].cross()
    vectors.crossed()
    vectors.fall()
    parts[3].fallen()
    hand_over(5, ra.at[3, 1 - c], ato.at[3])
    for k in range(3):
        parts[k].crossed()
        parts[k].fall()
    vectors.fallen()
    hand_over(6, vown, vto)

    for k in range(2):
        pl.when(c == k)(pass_on(k, ri.at[1 - k], ito).wait_recv)
        pl.when(c != k)(pass_on(k, ri.at[k], ito).wait_send)
    if piece % 128:
        gwi_out[c] = ri[c].astype(F32)
        gwi_out[1 - c] = ito[...].astype(F32)
    else:
        for k in range(n_m):
            cols = slice(k * piece, (k + 1) * piece)
            here = pl.ds(pl.multiple_of((2 * k + c) * piece, 128), piece)
            there = pl.ds(pl.multiple_of((2 * k + 1 - c) * piece, 128), piece)
            gwi_out[:, here] = ri[c, :, cols].astype(F32)
            gwi_out[:, there] = ito[:, cols].astype(F32)
    for k in range(3):
        parts[k].fallen()
        hand_over(2 + k, ra.at[k, 1 - c], ato.at[k])
    here = pl.ds(pl.multiple_of(c * mine, 128), mine)
    there = pl.ds(pl.multiple_of((1 - c) * mine, 128), mine)
    for key, k, out in ((5, 3, gwo_out), (2, 0, gwq_out), (3, 1, gwk_out), (4, 2, gwv_out)):
        crosses[key].wait()
        out[:, here] = ra[k, c].astype(F32)
        out[:, there] = ato[k].astype(F32)
    crosses[6].wait()
    vto[...] = vown[...] + vto[...]
    turned = pltpu.roll(vto[0:8, :], (width - f * share) % width, 1)
    small = (fg_out, fs_out, qb_out, vb_out, ob_out, sg_out, ss_out, ub_out)
    for k, out in enumerate(small):
        out[...] = turned[k : k + 1, :share]
    per = width // piece
    line = jnp.broadcast_to(vto[pl.ds(8 + lines * c + m // per, 1), :], (8, width))
    ib_out[...] = pltpu.roll(line, (width - (m % per) * piece) % width, 1)[0:1, :piece]
    for k in range(seq):
        g_copy(k).wait_send()
    for k in range(3):
        queries[k].finish()
    back.finish()


def project_back(x, n1, gq, gk, gv, gres, wqkv, vecs, gvec, gib, ri, ro):
    seq, _, half, width = x.shape
    _, share, hidden = ri.shape
    rows, mine = gq.shape
    n_m = lax.axis_size("fsdp") // 2
    piece = hidden // n_m
    square = jax.ShapeDtypeStruct((share, width), F32)
    block = (2, share, mine)
    return pl.pallas_call(
        lambda *refs: project_back_kernel(seq, *refs),
        in_specs=[ANY] * 7 + [VMEM] * 3 + [ANY] * 2,
        out_specs=[VMEM] * 14 + [ANY],
        out_shape=[square] * 4
        + [
            jax.ShapeDtypeStruct(
                (2, share, hidden) if piece % 128 else (share, 2 * hidden), F32
            )
        ]
        + [jax.ShapeDtypeStruct((1, share), F32)] * 8
        + [
            jax.ShapeDtypeStruct((1, piece), F32),
            jax.ShapeDtypeStruct((2, 2, half, width), BF16),
        ],
        scratch_shapes=[
            pltpu.VMEM((seq, half, width), BF16),
            pltpu.VMEM((rows, width), BF16),
            pltpu.VMEM((rows, 3 * mine), BF16),
            pltpu.VMEM((seq, half, width), F32),
            pltpu.VMEM(wqkv.shape, BF16),
            pltpu.VMEM((seq, 2, half, width), F32),
            pltpu.VMEM((seq, 2, half, width), BF16),
            pltpu.VMEM((seq, half, width), BF16),
            pltpu.VMEM((seq, half, width), BF16),
            pltpu.VMEM((3, n_m) + block, BF16),
            pltpu.VMEM((3, n_m - 1) + block, BF16),
            pltpu.VMEM((n_m - 1, 16, width), F32),
            pltpu.VMEM((2, share, hidden), BF16),
            pltpu.VMEM((2, 2, share, hidden), BF16),
            pltpu.VMEM((share, hidden), BF16),
            pltpu.VMEM((4,) + block, BF16),
            pltpu.VMEM((4, 2) + block, BF16),
            pltpu.VMEM((4, share, mine), BF16),
            pltpu.VMEM((16, width), F32),
            pltpu.VMEM((2, 16, width), F32),
            pltpu.VMEM((16, width), F32),
            pltpu.SemaphoreType.DMA((seq,)),
            pltpu.SemaphoreType.DMA((seq,)),
        ]
        + RETURN_SEMS(seq)
        + [
            pltpu.SemaphoreType.DMA((3, n_m)),
            pltpu.SemaphoreType.DMA((3, n_m)),
            pltpu.SemaphoreType.DMA((n_m,)),
            pltpu.SemaphoreType.DMA((n_m,)),
            pltpu.SemaphoreType.DMA((2, 6)),
            pltpu.SemaphoreType.DMA((4, 6)),
            ACROSS_SEMS,
            pltpu.SemaphoreType.DMA((2, 7)),
            pltpu.SemaphoreType.DMA((9,)),
        ],
        compiler_params=pltpu.CompilerParams(
            collective_id=4, has_side_effects=True, vmem_limit_bytes=LIMIT
        ),
        name="project_back",
    )(x, n1, gq, gk, gv, gres, wqkv, vecs, gvec, gib, ri, ro)


def per_device(
    frames,
    cotangent,
    valid_slots,
    first_gain,
    first_shift,
    query_weight,
    query_bias,
    key_weight,
    value_weight,
    value_bias,
    output_weight,
    output_bias,
    second_gain,
    second_shift,
    inner_weight,
    inner_bias,
    outer_weight,
    outer_bias,
):
    seq = lax.axis_size("seq")
    n_f = lax.axis_size("fsdp")
    f = lax.axis_index("fsdp")
    m, c = f // 2, f % 2
    slots, local, width = frames.shape
    chunk = -(-local // 128) * 128
    half = chunk // 2
    mine = width // 2
    share = width // n_f
    piece = inner_bias.shape[0]
    hidden = piece * n_f // 2

    keep = valid_slots.astype(BF16)[:, None, None]
    pad = ((0, 0), (0, chunk - local), (0, 0))
    x_send = jnp.pad(frames, pad).reshape(slots, 2, half, width)
    cot_send = jnp.pad(cotangent * keep, pad).reshape(slots, 2, half, width)
    wi_send = inner_weight.reshape(share, n_f // 2, 2, piece).transpose(2, 0, 1, 3)
    wi_send = wi_send.reshape(2, share, hidden)
    vectors = (
        first_gain,
        first_shift,
        query_bias,
        value_bias,
        output_bias,
        second_gain,
        second_shift,
        outer_bias,
    )
    if share % 16 == 0 and piece % 128 == 0:
        wqkv_send = jnp.concatenate(
            [
                w.reshape(share, 2, mine).transpose(1, 0, 2)
                for w in (query_weight, key_weight, value_weight)
            ],
            axis=-1,
        )
        x, n1, q, k, v, wqkv, wo, vecs, ibias = project(
            x_send,
            wqkv_send,
            output_weight,
            [value[None] for value in vectors] + [inner_bias[None]],
            seq,
        )
        wqkv = wqkv.reshape(width, 3 * mine)
        wo = wo.reshape(width, width)
    else:

        def gathered(value, axis=0):
            return lax.all_gather(value, "fsdp", axis=axis, tiled=True)

        def my_columns(value):
            return lax.dynamic_slice_in_dim(value, c * mine, mine, axis=1)

        wqkv = jnp.concatenate(
            [my_columns(gathered(w)) for w in (query_weight, key_weight, value_weight)], axis=1
        )
        wo = gathered(output_weight)
        vecs = gathered(jnp.stack(vectors), 1).astype(F32)
        ibias = gathered(inner_bias).astype(F32).reshape(n_f // 2, 2, piece)
        ibias = lax.dynamic_index_in_dim(ibias, c, 1, keepdims=False).reshape(1, hidden)
        x, n1, q, k, v = project_plain(x_send, wqkv, vecs, seq)

    e, o, linv, mixed, cot, wi = attend(cot_send, wi_send, q, k, v, local, seq)
    wi = wi.reshape(width, hidden)
    out_back, gres, gm, gwo, gwi, ru, gvec, gib = dense(
        x, mixed, cot, wo, wi, outer_weight, vecs, ibias
    )
    gq, gk, gv, ri, ro, gwu = attend_back(gwi, gwo, ru, q, k, v, gm, o, linv, e, seq)
    gwq, gwk, gwv, gwo, gwi, fg, fs, qb, vb, ob, sg, ss, ub, ib, ig_back = project_back(
        x, n1, gq, gk, gv, gres, wqkv, vecs, gvec, gib, ri, ro
    )
    if gwi.ndim == 3:
        gwi = gwi.reshape(2, share, n_f // 2, piece).transpose(1, 2, 0, 3)
        gwi = gwi.reshape(share, 2 * hidden)
    keep32 = valid_slots.astype(F32)[:, None, None]
    outputs = (out_back.reshape(slots, chunk, width)[:, :local].astype(F32) * keep32).astype(BF16)
    input_grad = ig_back.reshape(slots, chunk, width)[:, :local]
    return (
        outputs,
        input_grad,
        fg[0],
        fs[0],
        gwq,
        qb[0],
        gwk,
        gwv,
        vb[0],
        gwo,
        ob[0],
        sg[0],
        ss[0],
        gwi,
        ib[0],
        gwu,
        ub[0],
    )


def solution(mesh):
    rows = P("fsdp", "seq", None)
    vector, matrix = P("fsdp"), P("fsdp", None)
    weights = (
        vector,
        vector,
        matrix,
        vector,
        matrix,
        matrix,
        vector,
        matrix,
        vector,
        vector,
        vector,
        matrix,
        vector,
        matrix,
        vector,
    )
    return jax.shard_map(
        per_device,
        mesh=mesh,
        in_specs=(rows, rows, vector) + weights,
        out_specs=(rows, rows) + weights,
        check_vma=False,
    )
```

```python
import math

import jax
import jax.numpy as jnp
from jax import lax
from jax.experimental import pallas as pl
from jax.experimental.pallas import tpu as pltpu
from jax.sharding import PartitionSpec as P

H = 12
HD = 64
EPS = 1e-05
MESH = pl.DeviceIdType.MESH
F32 = jnp.float32
BF16 = jnp.bfloat16
ANY = pl.BlockSpec(memory_space=pl.ANY)
VMEM = pl.BlockSpec(memory_space=pltpu.VMEM)
LIMIT = 62 << 20
QB = 256


def nn(a, b):
    return lax.dot_general(a, b, (((1,), (0,)), ((), ())), preferred_element_type=F32)


def nt(a, b):
    return lax.dot_general(a, b, (((1,), (1,)), ((), ())), preferred_element_type=F32)


def tn(a, b):
    return lax.dot_general(a, b, (((0,), (0,)), ((), ())), preferred_element_type=F32)


def normalize(rows):
    center = rows - jnp.mean(rows, -1, keepdims=True)
    inv = lax.rsqrt(jnp.mean(center * center, -1, keepdims=True) + EPS)
    return center * inv, inv


def norm_back(grad, gain, hat, inv):
    tilted = grad * gain
    first = jnp.mean(tilted, -1, keepdims=True)
    cross = jnp.mean(tilted * hat, -1, keepdims=True)
    return inv * (tilted - first - hat * cross)


def where_am_i():
    f = lax.axis_index("fsdp")
    z = lax.axis_index("seq")
    return f, z, f // 2, f % 2


def meet(peers):
    barrier = pltpu.get_barrier_semaphore()
    for peer in peers:
        pl.semaphore_signal(barrier, inc=1, device_id=peer, device_id_type=MESH)
    pl.semaphore_wait(barrier, len(peers))


def column_peers(seq):
    f, z, m, c = where_am_i()
    peers = []
    for dc in range(2):
        for dz in range(seq):
            if dc or dz:
                peers.append((m * 2 + (c + dc) % 2, (z + dz) % seq))
    return peers


class Ship:
    def __init__(self, src, dst, send, recv, target):
        f, z, _, _ = where_am_i()
        self.here = jnp.logical_and(target[0] == f, target[1] == z)
        self.local = pltpu.make_async_copy(src, dst, recv)
        self.remote = pltpu.make_async_remote_copy(
            src, dst, send, recv, device_id=target, device_id_type=MESH
        )

    def start(self):
        pl.when(self.here)(self.local.start)
        pl.when(jnp.logical_not(self.here))(self.remote.start)

    def wait_send(self):
        pl.when(jnp.logical_not(self.here))(self.remote.wait_send)


def remote(src, dst, send, recv, target):
    return pltpu.make_async_remote_copy(
        src, dst, send, recv, device_id=target, device_id_type=MESH
    )


class Gather:
    def __init__(self, send_ref, full_ref, send_sem, recv_sem, pass_send, pass_recv, seq):
        f, z, m, c = where_am_i()
        self.ships = []
        for i in range(2):
            for h in range(2):
                slot = 2 * c + i
                self.ships.append(
                    Ship(
                        send_ref.at[i, h],
                        full_ref.at[z, h],
                        send_sem.at[i, h],
                        recv_sem.at[z],
                        (m * 2 + h, slot),
                    )
                )
        other = (m * 2 + 1 - c, z)
        chips = [(z + d) % seq for d in range(seq)]
        self.arrivals = [
            remote(send_ref.at[0, 0], full_ref.at[k, c], send_sem.at[0, 0], recv_sem.at[k], other)
            for k in chips
        ]
        self.passes = [
            remote(full_ref.at[k, c], full_ref.at[k, c], pass_send.at[d], pass_recv.at[d], other)
            for d, k in enumerate(chips)
        ]
        self.handed = [
            remote(
                full_ref.at[k, c], full_ref.at[k, 1 - c], pass_send.at[d], pass_recv.at[d], other
            )
            for d, k in enumerate(chips)
        ]

    def start(self):
        for ship in self.ships:
            ship.start()

    def arrived(self):
        for item in self.arrivals:
            item.wait_recv()
        for ship in self.ships:
            ship.wait_send()

    def hand_on(self, k):
        self.arrivals[k].wait_recv()
        self.passes[k].start()

    def ready(self, k):
        self.handed[k].wait_recv()

    def finish(self):
        for ship in self.ships:
            ship.wait_send()
        for item in self.passes:
            item.wait_send()


GATHER_SEMS = lambda seq: [
    pltpu.SemaphoreType.DMA((2, 2)),
    pltpu.SemaphoreType.DMA((seq,)),
    pltpu.SemaphoreType.DMA((seq,)),
    pltpu.SemaphoreType.DMA((seq,)),
]


class Return:
    def __init__(self, own_ref, back_ref, send_sem, recv_sem, seq):
        f, z, m, c = where_am_i()
        home = z // 2
        self.ships = [
            Ship(
                own_ref.at[k],
                back_ref.at[z % 2, c],
                send_sem.at[k],
                recv_sem.at[z % 2, c],
                (m * 2 + home, k),
            )
            for k in range(seq)
        ]
        self.arrivals = [
            remote(
                own_ref.at[0],
                back_ref.at[i, h],
                send_sem.at[0],
                recv_sem.at[i, h],
                (m * 2 + 1 - c, z),
            )
            for i in range(2)
            for h in range(2)
        ]

    def start(self):
        for ship in self.ships:
            ship.start()

    def finish(self):
        for ship in self.ships:
            ship.wait_send()
        for item in self.arrivals:
            item.wait_recv()


RETURN_SEMS = lambda seq: [pltpu.SemaphoreType.DMA((seq,)), pltpu.SemaphoreType.DMA((2, 2))]


class Spread:
    def __init__(self, source, full_ref, send_sem, recv_sem, local_sem, stride):
        f, z, m, c = where_am_i()
        n_f = lax.axis_size("fsdp")
        steps = n_f // stride
        slot = f if stride == 1 else m
        self.local = pltpu.make_async_copy(source(f), full_ref.at[slot], local_sem)
        self.sends = []
        self.arrivals = []
        for d in range(1, steps):
            to = (f + d * stride) % n_f
            back = (f + n_f - d * stride) % n_f
            self.sends.append(
                remote(source(to), full_ref.at[slot], send_sem.at[d], recv_sem.at[d], (to, z))
            )
            place = back if stride == 1 else back // 2
            self.arrivals.append(
                remote(source(f), full_ref.at[place], send_sem.at[d], recv_sem.at[d], (to, z))
            )

    def start(self):
        self.local.start()
        for item in self.sends:
            item.start()

    def relay(self):
        pass

    def ready(self):
        self.local.wait()
        for item in self.arrivals:
            item.wait_recv()

    def finish(self):
        for item in self.sends:
            item.wait_send()


def square_chips():
    _, _, m, _ = where_am_i()
    x, y = m % 2, m // 2
    return y * 2 + 1 - x, (1 - y) * 2 + x, (1 - y) * 2 + 1 - x


class Near:
    def __init__(self, source, full_ref, send_sem, recv_sem, local_sem, stride):
        f, z, m, c = where_am_i()
        beside, above, _ = square_chips()

        def slot(chip, core):
            return chip * 2 + core if stride == 1 else chip

        mine = full_ref.at[slot(m, c)]
        self.local = pltpu.make_async_copy(source(f), mine, local_sem)
        self.sends, self.arrivals = [], []
        k = 0
        for dc in range(2 // stride):
            core = (c + dc) % 2
            for chip in [beside, above] + ([m] if dc else []):
                to = (chip * 2 + core, z)
                src = source(chip * 2 + core)
                theirs = full_ref.at[slot(chip, core)]
                self.sends.append(remote(src, mine, send_sem.at[k], recv_sem.at[k], to))
                self.arrivals.append(remote(src, theirs, send_sem.at[k], recv_sem.at[k], to))
                k += 1

    def start(self):
        self.local.start()
        for item in self.sends:
            item.start()

    def ready(self):
        self.local.wait()
        for item in self.arrivals:
            item.wait_recv()

    def finish(self):
        for item in self.sends:
            item.wait_send()


class Far:
    def __init__(self, have_ref, full_ref, send_sem, recv_sem, stride):
        f, z, m, c = where_am_i()
        beside, above, far = square_chips()

        def slot(chip, core):
            return chip * 2 + core if stride == 1 else chip

        rows = full_ref.shape[1] // 2
        halves = [pl.ds(0, rows), pl.ds(rows, rows)]
        self.sends, self.arrivals = [], []
        k = 5
        for dc in range(2 // stride):
            core = (c + dc) % 2
            for chip, onto, part in ((beside, above, halves[0]), (above, beside, halves[1])):
                to = (onto * 2 + c, z)
                src = have_ref.at[slot(chip, core), part]
                dst = full_ref.at[slot(chip, core), part]
                lands = full_ref.at[slot(far, core), part]
                self.sends.append(remote(src, dst, send_sem.at[k], recv_sem.at[k], to))
                self.arrivals.append(remote(src, lands, send_sem.at[k], recv_sem.at[k], to))
                k += 1

    def start(self):
        for item in self.sends:
            item.start()

    def ready(self):
        for item in self.arrivals:
            item.wait_recv()

    def finish(self):
        for item in self.sends:
            item.wait_send()


class Relay:
    def __init__(self, source, full_ref, send_sem, recv_sem, local_sem, stride):
        self.near = Near(source, full_ref, send_sem, recv_sem, local_sem, stride)
        self.far = Far(full_ref, full_ref, send_sem, recv_sem, stride)

    def start(self):
        self.near.start()

    def relay(self):
        self.near.ready()
        self.far.start()

    def ready(self):
        self.far.ready()

    def finish(self):
        self.near.finish()
        self.far.finish()


def squared():
    return lax.axis_size("fsdp") == 8


def spreading(source, full_ref, sems, stride):
    kind = Relay if squared() else Spread
    return kind(source, full_ref, *sems, stride)


def spread_sems(steps):
    steps = max(steps, 9)
    return [
        pltpu.SemaphoreType.DMA((steps,)),
        pltpu.SemaphoreType.DMA((steps,)),
        pltpu.SemaphoreType.DMA,
    ]


def fsdp_peers():
    f, z, _, _ = where_am_i()
    n_f = lax.axis_size("fsdp")
    return [((f + d) % n_f, z) for d in range(1, n_f)]


def all_peers(seq):
    f, z, m, c = where_am_i()
    other = m * 2 + 1 - c
    peers = fsdp_peers()
    for d in range(1, seq):
        peers.append((f, (z + d) % seq))
        peers.append((other, (z + d) % seq))
    return peers


class Scatter:
    def __init__(self, part, got_ref, send_sem, recv_sem):
        f, z, m, c = where_am_i()
        n_m = lax.axis_size("fsdp") // 2
        self.part, self.got, self.chip = part, got_ref, m
        self.copies = []
        for d in range(1, n_m):
            to = (m + d) % n_m
            self.copies.append(
                remote(
                    part(to),
                    got_ref.at[d - 1],
                    send_sem.at[d],
                    recv_sem.at[d],
                    (to * 2 + c, z),
                )
            )

    def start(self):
        for item in self.copies:
            item.start()

    def total(self, own):
        for item in self.copies:
            item.wait_recv()
        result = own.astype(F32)
        for k in range(len(self.copies)):
            result = result + self.got[k].astype(F32)
        return result

    def finish(self):
        for item in self.copies:
            item.wait_send()


def scatter_sems():
    n_m = lax.axis_size("fsdp") // 2
    return [pltpu.SemaphoreType.DMA((n_m,)), pltpu.SemaphoreType.DMA((n_m,))]


class Across:
    def __init__(self, own_ref, spare_ref, sems):
        f, z, _, _ = where_am_i()
        self.own, self.spare = own_ref, spare_ref
        self.edge = jnp.logical_or(z == 0, z == 3)
        self.inner = jnp.logical_not(self.edge)
        beside = jnp.where(z < 2, 1 - z, 5 - z)
        self.up = remote(own_ref, spare_ref.at[0], sems.at[0], sems.at[1], (f, beside))
        self.swap = remote(own_ref, spare_ref.at[1], sems.at[2], sems.at[3], (f, 3 - z))
        self.down = remote(own_ref, spare_ref.at[1], sems.at[4], sems.at[5], (f, beside))

    def add(self, k):
        total = self.own[...].astype(F32) + self.spare[k].astype(F32)
        self.own[...] = total.astype(self.own.dtype)

    def rise(self):
        pl.when(self.edge)(self.up.start)

    def risen(self):
        @pl.when(self.inner)
        def _():
            self.up.wait_recv()
            self.add(0)

        pl.when(self.edge)(self.up.wait_send)

    def cross(self):
        pl.when(self.inner)(self.swap.start)

    def crossed(self):
        @pl.when(self.inner)
        def _():
            self.swap.wait()
            self.add(1)

    def fall(self):
        pl.when(self.inner)(self.down.start)

    def fallen(self):
        @pl.when(self.edge)
        def _():
            self.down.wait_recv()
            self.own[...] = self.spare[1]

        pl.when(self.inner)(self.down.wait_send)


ACROSS_SEMS = pltpu.SemaphoreType.DMA((6,))


def front_kernel(seq, local, gathers, *refs):
    refs = list(refs)

    def take(n):
        got = refs[:n]
        del refs[:n]
        return got

    x_send, cot_send, wo_send, wu_send = take(4)
    if gathers:
        squares, wi = take(3), take(1)[0]
        given = take(9)
    else:
        wqkv, vecs_out = take(2)
    x_full, n1_out, q, k, v, e_out, o_out, linv_out, mixed_out, cot_full, wo_out, wu_out = take(12)
    if gathers:
        wqkv_out, wi_out, vecs_out, ibias_out = take(4)
    xsems, csems, osems, usems = take(4), take(4), take(3), take(3)
    xv, stage, qa, ka, va, ebuf, lsem, esem, nsem, msend, mrecv, mlocal, nbuf = take(13)
    if gathers:
        wqkv, wqkv_send, wi_send, small, smalls, wsem, tsem = take(7)
        qsems, isems, vsems = take(3), take(3), take(3)
    f, z, m, c = where_am_i()
    n_f = lax.axis_size("fsdp")
    half = xv.shape[2]
    chunk = 2 * half
    rows, mine = q.shape
    width = xv.shape[3]
    pairs = mine // 128
    other = (m * 2 + 1 - c, z)
    if gathers:
        share = given[0].shape[1]
        piece = given[8].shape[1]
        sorts = []
        for b in range(2):
            for t, ref in enumerate(squares):
                sorts.append(
                    (ref.at[:, pl.ds(b * mine, mine)], wqkv_send.at[b, :, pl.ds(t * mine, mine)])
                )
        for b in range(2):
            for t in range(n_f // 2):
                cols = pl.ds((2 * t + b) * piece, piece)
                sorts.append((wi.at[:, cols], wi_send.at[b, :, pl.ds(t * piece, piece)]))
        sorts = [
            pltpu.make_async_copy(src, dst, tsem.at[n]) for n, (src, dst) in enumerate(sorts)
        ]
        for item in sorts:
            item.start()
        small[...] = jnp.zeros_like(small)
        for r in range(8):
            small[r : r + 1, :share] = given[r][...].astype(F32)
        small[8:9, :piece] = given[8][...].astype(F32)
        for item in sorts:
            item.wait()
        vectors = Spread(lambda to: small, smalls, *vsems, 1)
        attn = spreading(lambda to: wqkv_send.at[to % 2], wqkv, qsems, 1)
        feed = spreading(lambda to: wi_send.at[to % 2], wi_out, isems, 1)
    meet(all_peers(seq))
    gather = Gather(x_send, xv, *xsems, seq)
    gather_cot = Gather(cot_send, cot_full, *csems, seq)
    out = spreading(lambda to: wo_send, wo_out, osems, 1)
    outer = (Near if squared() else Spread)(lambda to: wu_send, wu_out, *usems, 2)
    if gathers:
        vectors.start()
        gather.start()
        attn.start()
        vectors.ready()
        row = lax.broadcasted_iota(jnp.int32, (128, width), 0)
        col = lax.broadcasted_iota(jnp.int32, (128, width), 1)
        vecs = jnp.zeros((16, width), F32)
        for n in range(n_f):
            spot = jnp.logical_and(col - n * share == row, row < share)
            vecs = vecs + nn(
                smalls[n, :, :128].astype(BF16), jnp.where(spot, 1.0, 0.0).astype(BF16)
            )
        vecs_out[...] = vecs[:8]
        for n in range(n_f // 2):
            ibias_out[0:1, n * piece : (n + 1) * piece] = smalls[2 * n + c, 8:9, :piece]
        attn.relay()
        feed.start()
        attn.ready()
        keep_weights = pltpu.make_async_copy(wqkv, wqkv_out, wsem)
        keep_weights.start()
    else:
        gather.start()
    gain = vecs_out[0:1, :]
    shift = vecs_out[1:2, :]
    cols = pl.ds(pl.multiple_of(c * mine, 128), mine)
    qb = vecs_out[2:3, cols]
    vb = vecs_out[3:4, cols]
    keeps = []
    for n, d in enumerate(sorted(range(seq), key=lambda d: min(d, seq - d))):
        at = (z + d) % seq
        gather.hand_on(d)
        if n == seq - 1:
            gather_cot.start()
        gather.ready(d)
        sl = pl.ds(pl.multiple_of(at * chunk, 16), chunk)
        hat, _ = normalize(xv[at].reshape(chunk, width).astype(F32))
        normed = (hat * gain + shift).astype(BF16)
        nbuf[sl, :] = normed
        keeps.append(pltpu.make_async_copy(xv.at[at], x_full.at[at], lsem.at[d]))
        keeps.append(pltpu.make_async_copy(nbuf.at[sl], n1_out.at[sl], nsem.at[d]))
        for item in keeps[-2:]:
            item.start()
        qkv = nn(normed, wqkv[...].reshape(width, 3 * mine))
        q[sl, :] = (qkv[:, :mine] + qb).astype(BF16)
        k[sl, :] = qkv[:, mine : 2 * mine].astype(BF16)
        v[sl, :] = (qkv[:, 2 * mine :] + vb).astype(BF16)
    lane = lax.broadcasted_iota(jnp.int32, (1, 128), 1)
    low = lane < HD
    factor = HD ** (-0.5) * math.log2(math.e)
    steps = [(i, a) for i in range(rows // QB) for a in range(2)]

    def block(i):
        return slice(i * QB, (i + 1) * QB)

    def e_copy(p):
        return pltpu.make_async_copy(ebuf.at[p % 2], e_out.at[pl.ds(2 * p, 2)], esem.at[p % 2])

    def mixed_copies(p):
        return (
            pltpu.make_async_copy(stage.at[p], mixed_out.at[c, p], mlocal.at[p]),
            remote(stage.at[p], mixed_out.at[c, p], msend.at[p], mrecv.at[p], other),
            remote(stage.at[p], mixed_out.at[1 - c, p], msend.at[p], mrecv.at[p], other),
        )

    def heads(pair, _):
        @pl.when(pair == 0)
        def _():
            if gathers:
                feed.relay()
            out.start()

        pl.when(pair == 1)(outer.start)
        pl.when(pair == pairs - 1)(out.relay)
        pl.when(pair >= 2)(lambda: e_copy(pair - 2).wait())
        here = pl.ds(pl.multiple_of(pair * 128, 128), 128)
        place = lax.broadcasted_iota(jnp.int32, (rows, 1), 0) % (rows // seq)
        bar = jnp.where(place < local, 0.0, -1e38).astype(F32)
        qf, kf, vf = q[:, here].astype(F32), k[:, here].astype(F32), v[:, here].astype(F32)
        for a in range(2):
            own = low if a == 0 else jnp.logical_not(low)
            first = lane == HD * (1 - a)
            qa[a] = jnp.where(own, qf, jnp.where(first, 1.0, 0.0)).astype(BF16)
            ka[a] = jnp.where(own, kf, jnp.where(first, bar, 0.0)).astype(BF16)
            va[a] = jnp.where(own, vf, 1.0).astype(BF16)

        def scored(t):
            i, a = steps[t]
            return nt(qa[a, block(i), :], ka[a])

        raws = {}

        def finish(t, expo):
            i, a = steps[t]
            raws[a] = nn(expo, va[a])
            if a == 1:
                sl = block(i)
                total = pltpu.roll(jnp.where(low, raws[1], raws[0]), HD, 1)
                inv = 1.0 / total
                res = jnp.where(low, raws[0], raws[1]) * inv
                o_out[sl, here] = res
                linv_out[sl, here] = inv
                stage[pair, sl, :] = res.astype(BF16)

        scores, before = scored(0), None
        for t, (i, a) in enumerate(steps):
            peak = jnp.max(scores, -1, keepdims=True)
            upcoming = scored(t + 1) if t + 1 < len(steps) else None
            if before is not None:
                finish(t - 1, before)
            expo = jnp.exp2((scores - peak) * factor).astype(BF16)
            ebuf[pair % 2, a, block(i), :] = expo
            scores, before = upcoming, expo
        finish(len(steps) - 1, before)
        e_copy(pair).start()
        to_self, to_other, _ = mixed_copies(pair)
        to_self.start()
        to_other.start()
        return 0

    lax.fori_loop(0, pairs, heads, 0)
    for item in keeps:
        item.wait()
    gather.finish()
    if gathers:
        keep_weights.wait()
        vectors.finish()
        attn.finish()
        feed.ready()
        feed.finish()
    out.ready()
    out.finish()
    outer.ready()
    outer.finish()
    for p in range(pairs):
        to_self, to_other, back = mixed_copies(p)
        to_self.wait()
        to_other.wait_send()
        back.wait_recv()
    for p in range(max(0, pairs - 2), pairs):
        e_copy(p).wait()
    gather_cot.arrived()


def front(x_send, cot_send, wo_send, wu_send, rest, local, seq, gathers):
    _, _, half, width = x_send.shape
    n_f = lax.axis_size("fsdp")
    rows = seq * 2 * half
    share = wo_send.shape[0]
    mine = width // 2
    pairs = mine // 128
    frames = jax.ShapeDtypeStruct((seq, 2, half, width), BF16)
    heads = jax.ShapeDtypeStruct((rows, mine), BF16)
    wide = jax.ShapeDtypeStruct((rows, mine), F32)
    out_specs = [ANY, ANY, VMEM, VMEM, VMEM, ANY, VMEM, VMEM, ANY, ANY, ANY, ANY]
    out_shape = [
        frames,
        jax.ShapeDtypeStruct((rows, width), BF16),
        heads,
        heads,
        heads,
        jax.ShapeDtypeStruct((2 * pairs, rows, rows), BF16),
        wide,
        wide,
        jax.ShapeDtypeStruct((2, pairs, rows, 128), BF16),
        frames,
        jax.ShapeDtypeStruct((n_f,) + wo_send.shape, BF16),
        jax.ShapeDtypeStruct((n_f // 2,) + wu_send.shape, BF16),
    ]
    scratch = (
        GATHER_SEMS(seq)
        + GATHER_SEMS(seq)
        + spread_sems(n_f)
        + spread_sems(n_f // 2)
        + [
            pltpu.VMEM((seq, 2, half, width), BF16),
            pltpu.VMEM((pairs, rows, 128), BF16),
            pltpu.VMEM((2, rows, 128), BF16),
            pltpu.VMEM((2, rows, 128), BF16),
            pltpu.VMEM((2, rows, 128), BF16),
            pltpu.VMEM((2, 2, rows, rows), BF16),
            pltpu.SemaphoreType.DMA((seq,)),
            pltpu.SemaphoreType.DMA((2,)),
            pltpu.SemaphoreType.DMA((seq,)),
            pltpu.SemaphoreType.DMA((pairs,)),
            pltpu.SemaphoreType.DMA((pairs,)),
            pltpu.SemaphoreType.DMA((pairs,)),
            pltpu.VMEM((rows, width), BF16),
        ]
    )
    in_specs = [ANY] * 4 + [VMEM] * 2
    if gathers:
        piece = rest[-1].shape[1]
        hidden = rest[3].shape[1] // 2
        lanes = max(128, piece)
        in_specs = [ANY] * 8 + [VMEM] * 9
        out_specs += [ANY, ANY, VMEM, VMEM]
        out_shape += [
            jax.ShapeDtypeStruct((n_f, share, 3 * mine), BF16),
            jax.ShapeDtypeStruct((n_f, share, hidden), BF16),
            jax.ShapeDtypeStruct((8, width), F32),
            jax.ShapeDtypeStruct((1, hidden), F32),
        ]
        scratch += [
            pltpu.VMEM((n_f, share, 3 * mine), BF16),
            pltpu.VMEM((2, share, 3 * mine), BF16),
            pltpu.VMEM((2, share, hidden), BF16),
            pltpu.VMEM((16, lanes), F32),
            pltpu.VMEM((n_f, 16, lanes), F32),
            pltpu.SemaphoreType.DMA,
            pltpu.SemaphoreType.DMA((6 + n_f,)),
        ]
        scratch += spread_sems(n_f) + spread_sems(n_f) + spread_sems(n_f)
    return pl.pallas_call(
        lambda *refs: front_kernel(seq, local, gathers, *refs),
        in_specs=in_specs,
        out_specs=out_specs,
        out_shape=out_shape,
        scratch_shapes=scratch,
        compiler_params=pltpu.CompilerParams(
            collective_id=0, has_side_effects=True, vmem_limit_bytes=LIMIT
        ),
        name="front",
    )(x_send, cot_send, wo_send, wu_send, *rest)


def gelu_parts(u):
    x = jnp.abs(u) * (1.0 / math.sqrt(2.0))
    t = 1.0 / (1.0 + 0.3275911 * x)
    poly = t * (
        0.254829592
        + t * (-0.284496736 + t * (1.421413741 + t * (-1.453152027 + t * 1.061405429)))
    )
    expo = jnp.exp(-x * x)
    tail = 0.5 * poly * expo
    phi = jnp.where(u >= 0, 1.0 - tail, tail)
    return phi, u * expo * (1.0 / math.sqrt(2.0 * math.pi))


def dense_kernel(
    seq, x, mixed_in, cot_in, wo_in, wi_in, wu_in, vecs, ibias,
    out_back, gres_own, gm_out, gwo_out, gwi_out, ru_out, gvec_out, gib_out,
    xv, mixed, cot, wo, wi, wu, n2, hat2, inv2, resid, active, slope, out_own,
    pstage, precv, grecv, ugot, upart,
    psem, prsem, gsem, grsem, bsend, brecv, usend, urecv, lsem, xsem, csend, crecv, fsend, frecv,
):
    f, z, m, c = where_am_i()
    other = (m * 2 + 1 - c, z)
    half = x.shape[2]
    chunk = 2 * half
    width = x.shape[3]
    mine = gm_out.shape[1]
    hidden = wi.shape[1]
    n_m = gwi_out.shape[0]
    share = gwi_out.shape[2]
    piece = upart.shape[1]
    rows = seq * chunk
    tile = 512

    def block(i):
        return pl.ds(i * chunk, chunk)

    def fetch_x(i):
        return pltpu.make_async_copy(x.at[i], xv.at[i % 2], xsem.at[i % 2])

    def load(k, src, dst):
        return pltpu.make_async_copy(src, dst, lsem.at[k])

    loads = [load(0, mixed_in, mixed), load(1, wo_in, wo), load(2, wi_in, wi)]
    late = [load(3 + k, cot_in.at[k, c], cot.at[k, c]) for k in range(seq)]
    if squared():
        beside, above, _ = square_chips()
        late += [
            load(3 + seq + k, wu_in.at[chip], wu.at[chip])
            for k, chip in enumerate((m, beside, above))
        ]
    else:
        late.append(load(3 + seq, wu_in, wu))
    fetch_x(0).start()
    for item in loads + late:
        item.start()
    meet(all_peers(seq))
    if squared():
        tail = Far(wu_in, wu, fsend, frecv, 2)
        tail.start()
    passes = [
        remote(cot_in.at[k, c], cot.at[k, c], csend.at[k], crecv.at[k], other) for k in range(seq)
    ]
    handed = [
        remote(cot_in.at[k, c], cot.at[k, 1 - c], csend.at[k], crecv.at[k], other)
        for k in range(seq)
    ]
    for item in passes:
        item.start()
    obias, gain, shift, ubias = vecs[4:5, :], vecs[5:6, :], vecs[6:7, :], vecs[7:8, :]
    back = Return(out_own, out_back, bsend, brecv, seq)
    gstage = active.at[:, :width]
    branch = active.at[:, width : 2 * width]
    gown = resid

    def p_copy(i):
        return remote(pstage.at[i, 1 - c], precv.at[i], psem.at[i], prsem.at[i], other)

    def g_copy(i):
        return remote(gstage.at[block(i)], grecv.at[block(i)], gsem.at[i], grsem.at[i], other)

    def mixed_rows(sl):
        return jnp.concatenate(
            [mixed[a, p, sl, :] for a in range(2) for p in range(mixed.shape[1])], axis=1
        )

    def push(i):
        sl = block(i)
        pout = nn(active[sl, :], wu[...].reshape(hidden, width))
        resid[sl, :] += pout
        pstage[i] = pout.astype(BF16).reshape(2, half, width)
        p_copy(i).start()

    for item in loads:
        item.wait()
    for i in range(seq):
        sl = block(i)
        fetch_x(i).wait()
        if i + 1 < seq:
            fetch_x(i + 1).start()
        frames = xv[i % 2].reshape(chunk, width).astype(F32)
        res = frames + nn(mixed_rows(sl), wo[...]) + obias
        hat, inv = normalize(res)
        normed = (hat * gain + shift).astype(BF16)
        resid[sl, :] = res + ubias
        n2[sl, :] = normed
        hat2[sl, :] = hat
        inv2[sl, :] = jnp.broadcast_to(inv, (chunk, 128))
        for j in range(0, hidden, tile):
            cols = slice(j, j + tile)
            inner = nn(normed, wi[:, cols]) + ibias[:, cols]
            phi, bump = gelu_parts(inner)
            active[sl, cols] = (inner * phi).astype(BF16)
            slope[sl, cols] = (phi + bump).astype(BF16)
        if i == 1:
            for item in late:
                item.wait()
            if squared():
                tail.ready()
        if i:
            push(i - 1)
    push(seq - 1)
    for item in handed:
        item.wait_recv()
    cots = cot[...].reshape(rows, width)
    outer = Scatter(lambda to: upart.at[to], ugot, usend, urecv)
    if piece % 128 == 0:
        for d in range(n_m):
            k = (m + 1 + d) % n_m
            at = pl.ds(pl.multiple_of(k * piece, 128), piece)
            upart[k] = tn(active[:, at], cots).astype(BF16)
            if d < n_m - 1:
                outer.copies[d].start()
    else:
        for k in range(n_m):
            upart[k] = tn(active[:, k * piece : (k + 1) * piece], cots).astype(BF16)
        outer.start()
    for i in range(seq):
        p_copy(i).wait_recv()
        out_own[i] = (
            resid[pl.ds(pl.multiple_of(i * chunk + c * half, 16), half), :]
            + precv[i].astype(F32)
        ).astype(BF16)
    back.start()
    gvec_out[0:1, :] = jnp.sum(cots.astype(F32), 0, keepdims=True)
    for i in range(seq):
        sl = block(i)
        g = cot[i].reshape(chunk, width)
        for j in range(0, hidden, piece):
            cols = slice(j, j + piece)
            gi = (nt(g, wu[j // piece]) * slope[sl, cols].astype(F32)).astype(BF16)
            slope[sl, cols] = gi
            line = jnp.sum(gi.astype(F32), 0, keepdims=True)
            if i == 0:
                gib_out[:, cols] = line
            else:
                gib_out[:, cols] += line
        gn2 = nt(slope[sl, :], wi[...])
        gown[sl, :] = gn2
        gstage[sl, :] = gn2.astype(BF16)
        g_copy(i).start()
    for j in range(0, hidden, tile):
        part = tn(n2[...], slope[:, j : j + tile])
        for k in range(n_m):
            for b in range(2):
                at = (2 * k + b) * share
                gwi_out[k, b, :, j : j + tile] = part[at : at + share, :].astype(BF16)
    wrows = pl.ds(pl.multiple_of(c * mine, 128), mine)
    for i in range(seq):
        sl = block(i)
        g_copy(i).wait_recv()
        gn2 = gown[sl, :] + grecv[sl, :].astype(F32)
        hat = hat2[sl, :]
        line = jnp.sum(gn2 * hat, 0, keepdims=True)
        flat = jnp.sum(gn2, 0, keepdims=True)
        g = cot[i].reshape(chunk, width).astype(F32)
        gres = g + norm_back(gn2, gain, hat, inv2[sl, 0:1])
        hat2[sl, :] = gres
        low = gres.astype(BF16)
        branch[sl, :] = low
        total = jnp.sum(low.astype(F32), 0, keepdims=True)
        if i == 0:
            lines, flats, totals = line, flat, total
        else:
            lines, flats, totals = lines + line, flats + flat, totals + total
        gm_out[sl, :] = nt(low, wo[wrows, :]).astype(BF16)
        gres_own[i] = hat2[pl.ds(pl.multiple_of(i * chunk + c * half, 16), half), :]
    gvec_out[1:2, :] = lines
    gvec_out[2:3, :] = flats
    gvec_out[3:4, :] = totals
    gvec_out[4:8, :] = jnp.zeros((4, width), F32)
    part = tn(
        mixed_rows(slice(None)),
        active[:, pl.ds(pl.multiple_of(width + c * mine, 128), mine)],
    )
    for k in range(n_m):
        for b in range(2):
            at = (2 * k + b) * share
            gwo_out[k, b] = part[at : at + share, :].astype(BF16)
    for i in range(seq):
        p_copy(i).wait_send()
        g_copy(i).wait_send()
        passes[i].wait_send()
    if squared():
        tail.finish()
    ru_out[...] = outer.total(upart[m]).astype(BF16).reshape(ru_out.shape)
    outer.finish()
    back.finish()


def dense(x, mixed, cot, wo, wi, wu, vecs, ibias):
    seq, _, half, width = x.shape
    rows = seq * 2 * half
    hidden = wi.shape[1]
    mine = width // 2
    n_f = lax.axis_size("fsdp")
    n_m = n_f // 2
    share = width // n_f
    piece = hidden // n_m
    return pl.pallas_call(
        lambda *refs: dense_kernel(seq, *refs),
        in_specs=[ANY] * 6 + [VMEM] * 2,
        out_specs=[ANY] + [VMEM] * 7,
        out_shape=[
            jax.ShapeDtypeStruct((2, 2, half, width), BF16),
            jax.ShapeDtypeStruct((seq, half, width), F32),
            jax.ShapeDtypeStruct((rows, mine), BF16),
            jax.ShapeDtypeStruct((n_m, 2, share, mine), BF16),
            jax.ShapeDtypeStruct((n_m, 2, share, hidden), BF16),
            jax.ShapeDtypeStruct((2, piece // 2, width), BF16),
            jax.ShapeDtypeStruct((8, width), F32),
            jax.ShapeDtypeStruct((1, hidden), F32),
        ],
        scratch_shapes=[
            pltpu.VMEM((2, 2, half, width), BF16),
            pltpu.VMEM(mixed.shape, BF16),
            pltpu.VMEM(cot.shape, BF16),
            pltpu.VMEM(wo.shape, BF16),
            pltpu.VMEM(wi.shape, BF16),
            pltpu.VMEM((n_m, piece, width), BF16),
            pltpu.VMEM((rows, width), BF16),
            pltpu.VMEM((rows, width), F32),
            pltpu.VMEM((rows, 128), F32),
            pltpu.VMEM((rows, width), F32),
            pltpu.VMEM((rows, hidden), BF16),
            pltpu.VMEM((rows, hidden), BF16),
            pltpu.VMEM((seq, half, width), BF16),
            pltpu.VMEM((seq, 2, half, width), BF16),
            pltpu.VMEM((seq, half, width), BF16),
            pltpu.VMEM((rows, width), BF16),
            pltpu.VMEM((n_m - 1, piece, width), BF16),
            pltpu.VMEM((n_m, piece, width), BF16),
            pltpu.SemaphoreType.DMA((seq,)),
            pltpu.SemaphoreType.DMA((seq,)),
            pltpu.SemaphoreType.DMA((seq,)),
            pltpu.SemaphoreType.DMA((seq,)),
        ]
        + RETURN_SEMS(seq)
        + scatter_sems()
        + [
            pltpu.SemaphoreType.DMA((6 + seq,)),
            pltpu.SemaphoreType.DMA((2,)),
            pltpu.SemaphoreType.DMA((seq,)),
            pltpu.SemaphoreType.DMA((seq,)),
            pltpu.SemaphoreType.DMA((7,)),
            pltpu.SemaphoreType.DMA((7,)),
        ],
        compiler_params=pltpu.CompilerParams(
            collective_id=2, has_side_effects=True, vmem_limit_bytes=LIMIT
        ),
        name="dense",
    )(x, mixed, cot, wo, wi, wu, vecs, ibias)


def attend_back_kernel(
    seq, pairs, gwi, gwo, ru, q, k, v, gm, o, linv, e,
    gq_out, gk_out, gv_out, ri_out, ro_out, gwu_out,
    asend, arecv, bsend, brecv, osend, orecv, zu, za, zb,
    uown, uspare, aown, aspare, bown, bspare, igot, ogot, oown, lsem,
    do, dot_, qt, va, km, dvt, dkt,
):
    pair = pl.program_id(0)
    rows = q.shape[0]
    m = lax.axis_index("fsdp") // 2
    inner = [
        Scatter(lambda to: gwi.at[to, 0], igot.at[0], asend, arecv),
        Scatter(lambda to: gwi.at[to, 1], igot.at[1], bsend, brecv),
    ]
    out = Scatter(lambda to: gwo.at[to], ogot, osend, orecv)
    outer = [Across(uown.at[k], uspare.at[k], zu.at[k]) for k in range(2)]
    halves = [Across(aown, aspare, za), Across(bown, bspare, zb)]
    loads = [
        pltpu.make_async_copy(src, dst, lsem.at[k])
        for k, (src, dst) in enumerate(
            ((ru, uown), (gwi.at[m, 0], aown), (gwi.at[m, 1], bown), (gwo.at[m], oown))
        )
    ]

    def sum_half(k):
        own = halves[k].own
        own[...] = inner[k].total(own[...]).astype(BF16)

    def at(step, place, action):
        def run():
            pl.when(pair == step)(action)

        events.setdefault(place, []).append(run)

    events = {}

    def begin():
        for item in loads:
            item.start()
        meet(all_peers(seq))
        inner[0].start()
        for item in loads:
            item.wait()
        outer[0].rise()

    def event_1():
        outer[0].risen()
        outer[0].cross()
        outer[1].rise()

    def event_2():
        sum_half(0)
        halves[0].rise()
        outer[1].risen()
        outer[1].cross()
        outer[0].crossed()
        outer[0].fall()

    def event_3():
        halves[0].risen()
        halves[0].cross()
        outer[1].crossed()
        outer[1].fall()

    def event_4():
        sum_half(1)
        halves[1].rise()
        out.start()
        outer[0].fallen()

    at(0, 0, begin)
    at(0, 8, event_1)
    at(1, 0, inner[1].start)
    at(1, 4, event_2)
    at(2, 0, event_3)
    at(2, 4, event_4)
    for run in events[0]:
        run()
    third = HD ** (-0.5)
    lane = lax.broadcasted_iota(jnp.int32, (1, 128), 1)
    low = lane < HD
    scaled = (gm[...].astype(F32) * linv[...]).astype(BF16).astype(F32)
    kf, vf = k[...].astype(F32), v[...].astype(F32)
    weighted = scaled * o[...]
    for a in range(2):
        mine = low if a == 0 else jnp.logical_not(low)
        delta = jnp.sum(jnp.where(mine, weighted, 0.0), -1, keepdims=True)
        high = delta.astype(BF16).astype(F32)
        middle = (delta - high).astype(BF16).astype(F32)
        last = delta - high - middle
        base = HD * (1 - a)
        extra = jnp.where(
            lane == base, high, jnp.where(lane == base + 1, middle, jnp.where(lane == base + 2, last, 0.0))
        )
        do[a] = jnp.where(mine, scaled, -extra).astype(BF16)
        va[a] = jnp.where(mine, vf, 1.0).astype(BF16)
        km[a] = jnp.where(mine, kf, 0.0).astype(BF16)
    dot_[...] = scaled.astype(BF16).T
    qt[...] = q[...].T
    steps = [(i, a) for i in range(rows // QB) for a in range(2)]

    def block(i):
        return slice(i * QB, (i + 1) * QB)

    def sub(a):
        return slice(a * HD, (a + 1) * HD)

    def pushed(t):
        i, a = steps[t]
        return nt(do[a, block(i), :], va[a])

    dqs = {}
    grads = pushed(0)
    for t, (i, a) in enumerate(steps):
        for run in events.get(t, []) if t else []:
            run()
        sl = block(i)
        p = e[a, sl, :]
        ds = (p.astype(F32) * grads).astype(BF16)
        grads = pushed(t + 1) if t + 1 < len(steps) else None
        dv = nn(dot_[sub(a), sl], p)
        dk = nn(qt[sub(a), sl], ds)
        dqs[a] = nn(ds, km[a])
        if i == 0:
            dvt[sub(a), :] = dv
            dkt[sub(a), :] = dk
        else:
            dvt[sub(a), :] += dv
            dkt[sub(a), :] += dk
        if a == 1:
            gq_out[sl, :] = ((dqs[0] + dqs[1]) * third).astype(BF16)
    gv_out[...] = dvt[...].astype(BF16).T
    gk_out[...] = (dkt[...] * third).astype(BF16).T

    @pl.when(pair == pairs - 1)
    def _():
        ro_out[...] = out.total(oown[...]).astype(BF16)
        halves[1].risen()
        halves[0].crossed()
        outer[1].fallen()
        gwu_out[...] = uown[...]
        ri_out[0] = aown[...]
        ri_out[1] = bown[...]
        for item in inner + [out]:
            item.finish()


def attend_back(gwi, gwo, ru, q, k, v, gm, o, linv, e, seq):
    rows, mine = q.shape
    pairs = mine // 128
    n_m = gwi.shape[0]
    by_pair = pl.BlockSpec((rows, 128), lambda p: (0, p))
    return pl.pallas_call(
        lambda *refs: attend_back_kernel(seq, pairs, *refs),
        grid=(pairs,),
        in_specs=[ANY] * 3
        + [by_pair] * 6
        + [pl.BlockSpec((2, rows, rows), lambda p: (p, 0, 0))],
        out_specs=[by_pair] * 3
        + [
            pl.BlockSpec(gwi.shape[1:], lambda p: (0, 0, 0)),
            pl.BlockSpec(gwo.shape[1:], lambda p: (0, 0, 0)),
            pl.BlockSpec(ru.shape, lambda p: (0, 0, 0)),
        ],
        out_shape=[jax.ShapeDtypeStruct((rows, mine), BF16)] * 3
        + [
            jax.ShapeDtypeStruct(gwi.shape[1:], BF16),
            jax.ShapeDtypeStruct(gwo.shape[1:], BF16),
            jax.ShapeDtypeStruct(ru.shape, BF16),
        ],
        scratch_shapes=scatter_sems()
        + scatter_sems()
        + scatter_sems()
        + [pltpu.SemaphoreType.DMA((2, 6)), ACROSS_SEMS, ACROSS_SEMS]
        + [
            pltpu.VMEM(ru.shape, BF16),
            pltpu.VMEM((2,) + ru.shape, BF16),
            pltpu.VMEM(gwi.shape[2:], BF16),
            pltpu.VMEM((2,) + gwi.shape[2:], BF16),
            pltpu.VMEM(gwi.shape[2:], BF16),
            pltpu.VMEM((2,) + gwi.shape[2:], BF16),
            pltpu.VMEM((2, n_m - 1) + gwi.shape[2:], BF16),
            pltpu.VMEM((n_m - 1,) + gwo.shape[1:], BF16),
            pltpu.VMEM(gwo.shape[1:], BF16),
            pltpu.SemaphoreType.DMA((4,)),
            pltpu.VMEM((2, rows, 128), BF16),
            pltpu.VMEM((128, rows), BF16),
            pltpu.VMEM((128, rows), BF16),
            pltpu.VMEM((2, rows, 128), BF16),
            pltpu.VMEM((2, rows, 128), BF16),
            pltpu.VMEM((128, rows), F32),
            pltpu.VMEM((128, rows), F32),
        ],
        compiler_params=pltpu.CompilerParams(
            collective_id=3, has_side_effects=True, vmem_limit_bytes=LIMIT
        ),
        name="attend_back",
    )(gwi, gwo, ru, q, k, v, gm, o, linv, e)


def project_back_kernel(
    seq, x_in, n1_in, gq_in, gk_in, gv_in, gres_in, wqkv_in, vecs, gvec, gib, ri_in, ro_in,
    w_out, gwi_out, vec_out, ib_out, ig_back,
    x, n1, grads, gres, wqkv, gown, gstage, grecv, ig_own, qpart, qgot, vgot,
    ri, ispare, ito, ra, aspare, ato, vown, vspare, vto,
    gsem, grsem, bsend, brecv, qsend, qrecv, vsend, vrecv, zi, za, zv, pair_sems, lsem,
):
    f, z, m, c = where_am_i()
    other = (m * 2 + 1 - c, z)
    half = gres.shape[1]
    chunk = 2 * half
    width = gres.shape[2]
    rows = seq * chunk
    mine = width // 2
    n_m = qpart.shape[1]
    share = ri.shape[1]
    hidden = ri.shape[2]
    piece = hidden // n_m
    loads = [
        pltpu.make_async_copy(src, dst, lsem.at[k])
        for k, (src, dst) in enumerate(
            (
                (gq_in, grads.at[:, :mine]),
                (gk_in, grads.at[:, mine : 2 * mine]),
                (gv_in, grads.at[:, 2 * mine :]),
                (wqkv_in, wqkv),
                (ri_in, ri),
                (ro_in, ra.at[3]),
                (n1_in, n1),
                (gres_in, gres),
                (x_in.at[:, c], x),
            )
        )
    ]
    for item in loads:
        item.start()
    meet(all_peers(seq))
    gain = vecs[0:1, :]
    inner = [Across(ri.at[k], ispare.at[k], zi.at[k]) for k in range(2)]
    parts = [Across(ra.at[k], aspare.at[k], za.at[k]) for k in range(4)]
    vectors = Across(vown, vspare, zv)
    queries = [
        Scatter(lambda to, k=k: qpart.at[k, to], qgot.at[k], qsend.at[k], qrecv.at[k])
        for k in range(3)
    ]
    vspread = Scatter(lambda to: vown, vgot, vsend, vrecv)
    back = Return(ig_own, ig_back, bsend, brecv, seq)

    def g_copy(i):
        return remote(gstage.at[i, 1 - c], grecv.at[i], gsem.at[i], grsem.at[i], other)

    def pass_on(k, src, dst):
        return remote(src, dst, pair_sems.at[0, k], pair_sems.at[1, k], other)

    for item in loads[:6]:
        item.wait()
    inner[0].fall()
    inner[1].cross()
    parts[3].rise()
    for i in range(seq):
        gn1 = nt(grads[i * chunk : (i + 1) * chunk, :], wqkv[...])
        gown[i] = gn1.reshape(2, half, width)
        gstage[i] = gn1.astype(BF16).reshape(2, half, width)
        g_copy(i).start()
    for item in loads[6:]:
        item.wait()

    def weight(k):
        part = tn(n1[...], grads[:, k * mine : (k + 1) * mine])
        for j in range(n_m):
            for b in range(2):
                at = (2 * j + b) * share
                qpart[k, j, b] = part[at : at + share, :].astype(BF16)
        queries[k].start()

    for k in range(3):
        weight(k)
    for k in range(seq):
        g_copy(k).wait_recv()
        gn1 = gown[k, c] + grecv[k].astype(F32)
        hat, inv = normalize(x[k].astype(F32))
        line = jnp.sum(gn1 * hat, 0, keepdims=True)
        flat = jnp.sum(gn1, 0, keepdims=True)
        if k == 0:
            gain_sum, shift_sum = line, flat
        else:
            gain_sum, shift_sum = gain_sum + line, shift_sum + flat
        ig_own[k] = (gres[k] + norm_back(gn1, gain, hat, inv)).astype(BF16)
        back.ships[k].start()
    vown[...] = jnp.zeros_like(vown)
    vown[0:1, :] = gain_sum
    vown[1:2, :] = shift_sum
    cols = pl.ds(pl.multiple_of(c * mine, 128), mine)
    vown[2:3, cols] = jnp.sum(grads[:, :mine].astype(F32), 0, keepdims=True)
    vown[3:4, cols] = jnp.sum(grads[:, 2 * mine :].astype(F32), 0, keepdims=True)
    for k, r in enumerate((3, 1, 2, 0)):
        vown[4 + k : 5 + k, :] = 0.5 * gvec[r : r + 1, :]
    lines = hidden // width
    for k in range(lines):
        vown[pl.ds(8 + lines * c + k, 1), :] = gib[:, k * width : (k + 1) * width]
    vspread.start()
    parts[3].risen()
    parts[3].cross()
    inner[1].crossed()
    inner[1].fall()
    total = vspread.total(vown[...])
    vspread.finish()
    vown[...] = total
    vectors.rise()
    parts[3].crossed()
    parts[3].fall()
    for k in range(3):
        ra[k] = queries[k].total(qpart[k, m]).astype(BF16)
        parts[k].rise()
    vectors.risen()
    vectors.cross()
    crosses = {}

    def hand_over(k, src, dst):
        crosses[k] = pass_on(k, src, dst)
        crosses[k].start()

    for k in range(2):
        inner[k].fallen()
        pl.when(c != k)(pass_on(k, ri.at[k], ito).start)
    for k in range(3):
        parts[k].risen()
        parts[k].cross()
    vectors.crossed()
    vectors.fall()
    parts[3].fallen()
    hand_over(5, ra.at[3, 1 - c], ato.at[3])
    for k in range(3):
        parts[k].crossed()
        parts[k].fall()
    vectors.fallen()
    hand_over(6, vown, vto)

    for k in range(2):
        pl.when(c == k)(pass_on(k, ri.at[1 - k], ito).wait_recv)
        pl.when(c != k)(pass_on(k, ri.at[k], ito).wait_send)
    if piece % 128:
        gwi_out[c] = ri[c]
        gwi_out[1 - c] = ito[...]
    else:
        for k in range(n_m):
            cols = slice(k * piece, (k + 1) * piece)
            here = pl.ds(pl.multiple_of((2 * k + c) * piece, 128), piece)
            there = pl.ds(pl.multiple_of((2 * k + 1 - c) * piece, 128), piece)
            gwi_out[:, here] = ri[c, :, cols]
            gwi_out[:, there] = ito[:, cols]
    for k in range(3):
        parts[k].fallen()
        hand_over(2 + k, ra.at[k, 1 - c], ato.at[k])
    here = pl.ds(pl.multiple_of(c * mine, 128), mine)
    there = pl.ds(pl.multiple_of((1 - c) * mine, 128), mine)
    for key, k in ((5, 3), (2, 0), (3, 1), (4, 2)):
        crosses[key].wait()
        w_out[k, :, here] = ra[k, c]
        w_out[k, :, there] = ato[k]
    crosses[6].wait()
    vto[...] = vown[...] + vto[...]
    turned = pltpu.roll(vto[0:8, :], (width - f * share) % width, 1)
    vec_out[...] = turned[:, :share]
    per = width // piece
    line = jnp.broadcast_to(vto[pl.ds(8 + lines * c + m // per, 1), :], (8, width))
    ib_out[...] = pltpu.roll(line, (width - (m % per) * piece) % width, 1)[0:1, :piece]
    for k in range(seq):
        g_copy(k).wait_send()
    for k in range(3):
        queries[k].finish()
    back.finish()


def project_back(x, n1, gq, gk, gv, gres, wqkv, vecs, gvec, gib, ri, ro):
    seq, _, half, width = x.shape
    _, share, hidden = ri.shape
    rows, mine = gq.shape
    n_m = lax.axis_size("fsdp") // 2
    piece = hidden // n_m
    block = (2, share, mine)
    return pl.pallas_call(
        lambda *refs: project_back_kernel(seq, *refs),
        in_specs=[ANY] * 7 + [VMEM] * 3 + [ANY] * 2,
        out_specs=[VMEM] * 4 + [ANY],
        out_shape=[
            jax.ShapeDtypeStruct((4, share, width), BF16),
            jax.ShapeDtypeStruct(
                (2, share, hidden) if piece % 128 else (share, 2 * hidden), BF16
            ),
            jax.ShapeDtypeStruct((8, share), F32),
            jax.ShapeDtypeStruct((1, piece), F32),
            jax.ShapeDtypeStruct((2, 2, half, width), BF16),
        ],
        scratch_shapes=[
            pltpu.VMEM((seq, half, width), BF16),
            pltpu.VMEM((rows, width), BF16),
            pltpu.VMEM((rows, 3 * mine), BF16),
            pltpu.VMEM((seq, half, width), F32),
            pltpu.VMEM(wqkv.shape, BF16),
            pltpu.VMEM((seq, 2, half, width), F32),
            pltpu.VMEM((seq, 2, half, width), BF16),
            pltpu.VMEM((seq, half, width), BF16),
            pltpu.VMEM((seq, half, width), BF16),
            pltpu.VMEM((3, n_m) + block, BF16),
            pltpu.VMEM((3, n_m - 1) + block, BF16),
            pltpu.VMEM((n_m - 1, 16, width), F32),
            pltpu.VMEM((2, share, hidden), BF16),
            pltpu.VMEM((2, 2, share, hidden), BF16),
            pltpu.VMEM((share, hidden), BF16),
            pltpu.VMEM((4,) + block, BF16),
            pltpu.VMEM((4, 2) + block, BF16),
            pltpu.VMEM((4, share, mine), BF16),
            pltpu.VMEM((16, width), F32),
            pltpu.VMEM((2, 16, width), F32),
            pltpu.VMEM((16, width), F32),
            pltpu.SemaphoreType.DMA((seq,)),
            pltpu.SemaphoreType.DMA((seq,)),
        ]
        + RETURN_SEMS(seq)
        + [
            pltpu.SemaphoreType.DMA((3, n_m)),
            pltpu.SemaphoreType.DMA((3, n_m)),
            pltpu.SemaphoreType.DMA((n_m,)),
            pltpu.SemaphoreType.DMA((n_m,)),
            pltpu.SemaphoreType.DMA((2, 6)),
            pltpu.SemaphoreType.DMA((4, 6)),
            ACROSS_SEMS,
            pltpu.SemaphoreType.DMA((2, 7)),
            pltpu.SemaphoreType.DMA((9,)),
        ],
        compiler_params=pltpu.CompilerParams(
            collective_id=4, has_side_effects=True, vmem_limit_bytes=LIMIT
        ),
        name="project_back",
    )(x, n1, gq, gk, gv, gres, wqkv, vecs, gvec, gib, ri, ro)


def widen_kernel(w, gwi, gwu, vec, ib, *outs):
    for k in range(4):
        outs[k][...] = w[k].astype(F32)
    outs[4][...] = gwi[...].astype(F32)
    outs[5][...] = gwu[...].astype(F32)
    outs[6][...] = ib[...]
    for k in range(8):
        outs[7 + k][...] = vec[k : k + 1, :]


def widen(w, gwi, gwu, vec, ib):
    square = jax.ShapeDtypeStruct(w.shape[1:], F32)
    return pl.pallas_call(
        widen_kernel,
        in_specs=[VMEM] * 5,
        out_specs=[VMEM] * 15,
        out_shape=[square] * 4
        + [jax.ShapeDtypeStruct(value.shape, F32) for value in (gwi, gwu, ib)]
        + [jax.ShapeDtypeStruct((1, vec.shape[1]), F32)] * 8,
        compiler_params=pltpu.CompilerParams(vmem_limit_bytes=LIMIT),
        name="widen",
    )(w, gwi, gwu, vec, ib)


def per_device(
    frames,
    cotangent,
    valid_slots,
    first_gain,
    first_shift,
    query_weight,
    query_bias,
    key_weight,
    value_weight,
    value_bias,
    output_weight,
    output_bias,
    second_gain,
    second_shift,
    inner_weight,
    inner_bias,
    outer_weight,
    outer_bias,
):
    seq = lax.axis_size("seq")
    n_f = lax.axis_size("fsdp")
    f = lax.axis_index("fsdp")
    m, c = f // 2, f % 2
    slots, local, width = frames.shape
    chunk = -(-local // 128) * 128
    half = chunk // 2
    mine = width // 2
    share = width // n_f
    piece = inner_bias.shape[0]
    hidden = piece * n_f // 2

    keep = valid_slots.astype(BF16)[:, None, None]
    pad = ((0, 0), (0, chunk - local), (0, 0))
    x_send = jnp.pad(frames, pad).reshape(slots, 2, half, width)
    cot_send = jnp.pad(cotangent * keep, pad).reshape(slots, 2, half, width)
    vectors = (
        first_gain,
        first_shift,
        query_bias,
        value_bias,
        output_bias,
        second_gain,
        second_shift,
        outer_bias,
    )
    if share % 16 == 0 and piece % 128 == 0:
        rest = [query_weight, key_weight, value_weight, inner_weight]
        rest += [value[None] for value in vectors] + [inner_bias.astype(F32)[None]]
        *kept, wqkv, wi, vecs, ibias = front(
            x_send, cot_send, output_weight, outer_weight, rest, local, seq, True
        )
        wqkv = wqkv.reshape(width, 3 * mine)
        wi = wi.reshape(width, hidden)
    else:

        def gathered(value, axis=0):
            return lax.all_gather(value, "fsdp", axis=axis, tiled=True)

        def my_columns(value):
            return lax.dynamic_slice_in_dim(value, c * mine, mine, axis=1)

        wqkv = jnp.concatenate(
            [my_columns(gathered(w)) for w in (query_weight, key_weight, value_weight)], axis=1
        )
        wi = gathered(inner_weight).reshape(width, n_f // 2, 2, piece)
        wi = lax.dynamic_index_in_dim(wi, c, 2, keepdims=False).reshape(width, hidden)
        vecs = gathered(jnp.stack(vectors), 1).astype(F32)
        ibias = gathered(inner_bias).astype(F32).reshape(n_f // 2, 2, piece)
        ibias = lax.dynamic_index_in_dim(ibias, c, 1, keepdims=False).reshape(1, hidden)
        kept = front(
            x_send, cot_send, output_weight, outer_weight, [wqkv, vecs], local, seq, False
        )

    x, n1, q, k, v, e, o, linv, mixed, cot, wo, wu = kept
    wo = wo.reshape(width, width)
    out_back, gres, gm, gwo, gwi, ru, gvec, gib = dense(x, mixed, cot, wo, wi, wu, vecs, ibias)
    gq, gk, gv, ri, ro, gwu = attend_back(gwi, gwo, ru, q, k, v, gm, o, linv, e, seq)
    w, gwi, vec, ib, ig_back = project_back(
        x, n1, gq, gk, gv, gres, wqkv, vecs, gvec, gib, ri, ro
    )
    if gwi.ndim == 3:
        gwi = gwi.reshape(2, share, n_f // 2, piece).transpose(1, 2, 0, 3)
        gwi = gwi.reshape(share, 2 * hidden)
    gwq, gwk, gwv, gwo, gwi, gwu, ib, fg, fs, qb, vb, ob, sg, ss, ub = widen(
        w, gwi, gwu.reshape(piece, width), vec, ib
    )
    keep32 = valid_slots.astype(F32)[:, None, None]
    outputs = (out_back.reshape(slots, chunk, width)[:, :local].astype(F32) * keep32).astype(BF16)
    input_grad = ig_back.reshape(slots, chunk, width)[:, :local]
    return (
        outputs,
        input_grad,
        fg[0],
        fs[0],
        gwq,
        qb[0],
        gwk,
        gwv,
        vb[0],
        gwo,
        ob[0],
        sg[0],
        ss[0],
        gwi,
        ib[0],
        gwu,
        ub[0],
    )


def solution(mesh):
    rows = P("fsdp", "seq", None)
    vector, matrix = P("fsdp"), P("fsdp", None)
    weights = (
        vector,
        vector,
        matrix,
        vector,
        matrix,
        matrix,
        vector,
        matrix,
        vector,
        vector,
        vector,
        matrix,
        vector,
        matrix,
        vector,
    )
    return jax.shard_map(
        per_device,
        mesh=mesh,
        in_specs=(rows, rows, vector) + weights,
        out_specs=(rows, rows) + weights,
        check_vma=False,
    )
```

```python
import math

import jax
import jax.numpy as jnp
from jax import lax
from jax.experimental import pallas as pl
from jax.experimental.pallas import tpu as pltpu
from jax.sharding import PartitionSpec as P

H = 12
HD = 64
EPS = 1e-05
MESH = pl.DeviceIdType.MESH
F32 = jnp.float32
BF16 = jnp.bfloat16
ANY = pl.BlockSpec(memory_space=pl.ANY)
VMEM = pl.BlockSpec(memory_space=pltpu.VMEM)
LIMIT = 62 << 20
QB = 256


def nn(a, b):
    return lax.dot_general(a, b, (((1,), (0,)), ((), ())), preferred_element_type=F32)


def nt(a, b):
    return lax.dot_general(a, b, (((1,), (1,)), ((), ())), preferred_element_type=F32)


def tn(a, b):
    return lax.dot_general(a, b, (((0,), (0,)), ((), ())), preferred_element_type=F32)


def normalize(rows):
    center = rows - jnp.mean(rows, -1, keepdims=True)
    inv = lax.rsqrt(jnp.mean(center * center, -1, keepdims=True) + EPS)
    return center * inv, inv


def norm_back(grad, gain, hat, inv):
    tilted = grad * gain
    first = jnp.mean(tilted, -1, keepdims=True)
    cross = jnp.mean(tilted * hat, -1, keepdims=True)
    return inv * (tilted - first - hat * cross)


def where_am_i():
    f = lax.axis_index("fsdp")
    z = lax.axis_index("seq")
    return f, z, f // 2, f % 2


def meet(peers):
    barrier = pltpu.get_barrier_semaphore()
    for peer in peers:
        pl.semaphore_signal(barrier, inc=1, device_id=peer, device_id_type=MESH)
    pl.semaphore_wait(barrier, len(peers))


def column_peers(seq):
    f, z, m, c = where_am_i()
    peers = []
    for dc in range(2):
        for dz in range(seq):
            if dc or dz:
                peers.append((m * 2 + (c + dc) % 2, (z + dz) % seq))
    return peers


class Ship:
    def __init__(self, src, dst, send, recv, target):
        f, z, _, _ = where_am_i()
        self.here = jnp.logical_and(target[0] == f, target[1] == z)
        self.local = pltpu.make_async_copy(src, dst, recv)
        self.remote = pltpu.make_async_remote_copy(
            src, dst, send, recv, device_id=target, device_id_type=MESH
        )

    def start(self):
        pl.when(self.here)(self.local.start)
        pl.when(jnp.logical_not(self.here))(self.remote.start)

    def wait_send(self):
        pl.when(jnp.logical_not(self.here))(self.remote.wait_send)


def remote(src, dst, send, recv, target):
    return pltpu.make_async_remote_copy(
        src, dst, send, recv, device_id=target, device_id_type=MESH
    )


class Gather:
    def __init__(self, send_ref, full_ref, send_sem, recv_sem, pass_send, pass_recv, seq):
        f, z, m, c = where_am_i()
        self.ships = []
        for i in range(2):
            for h in range(2):
                slot = 2 * c + i
                self.ships.append(
                    Ship(
                        send_ref.at[i, h],
                        full_ref.at[z, h],
                        send_sem.at[i, h],
                        recv_sem.at[z],
                        (m * 2 + h, slot),
                    )
                )
        other = (m * 2 + 1 - c, z)
        chips = [(z + d) % seq for d in range(seq)]
        self.arrivals = [
            remote(send_ref.at[0, 0], full_ref.at[k, c], send_sem.at[0, 0], recv_sem.at[k], other)
            for k in chips
        ]
        self.passes = [
            remote(full_ref.at[k, c], full_ref.at[k, c], pass_send.at[d], pass_recv.at[d], other)
            for d, k in enumerate(chips)
        ]
        self.handed = [
            remote(
                full_ref.at[k, c], full_ref.at[k, 1 - c], pass_send.at[d], pass_recv.at[d], other
            )
            for d, k in enumerate(chips)
        ]

    def start(self):
        for ship in self.ships:
            ship.start()

    def arrived(self):
        for item in self.arrivals:
            item.wait_recv()
        for ship in self.ships:
            ship.wait_send()

    def hand_on(self, k):
        self.arrivals[k].wait_recv()
        self.passes[k].start()

    def ready(self, k):
        self.handed[k].wait_recv()

    def finish(self):
        for ship in self.ships:
            ship.wait_send()
        for item in self.passes:
            item.wait_send()


GATHER_SEMS = lambda seq: [
    pltpu.SemaphoreType.DMA((2, 2)),
    pltpu.SemaphoreType.DMA((seq,)),
    pltpu.SemaphoreType.DMA((seq,)),
    pltpu.SemaphoreType.DMA((seq,)),
]


class Return:
    def __init__(self, own_ref, back_ref, send_sem, recv_sem, seq):
        f, z, m, c = where_am_i()
        home = z // 2
        self.ships = [
            Ship(
                own_ref.at[k],
                back_ref.at[z % 2, c],
                send_sem.at[k],
                recv_sem.at[z % 2, c],
                (m * 2 + home, k),
            )
            for k in range(seq)
        ]
        self.arrivals = [
            remote(
                own_ref.at[0],
                back_ref.at[i, h],
                send_sem.at[0],
                recv_sem.at[i, h],
                (m * 2 + 1 - c, z),
            )
            for i in range(2)
            for h in range(2)
        ]

    def start(self):
        for ship in self.ships:
            ship.start()

    def finish(self):
        for ship in self.ships:
            ship.wait_send()
        for item in self.arrivals:
            item.wait_recv()


RETURN_SEMS = lambda seq: [pltpu.SemaphoreType.DMA((seq,)), pltpu.SemaphoreType.DMA((2, 2))]


class Spread:
    def __init__(self, source, full_ref, send_sem, recv_sem, local_sem, stride):
        f, z, m, c = where_am_i()
        n_f = lax.axis_size("fsdp")
        steps = n_f // stride
        slot = f if stride == 1 else m
        self.local = pltpu.make_async_copy(source(f), full_ref.at[slot], local_sem)
        self.sends = []
        self.arrivals = []
        for d in range(1, steps):
            to = (f + d * stride) % n_f
            back = (f + n_f - d * stride) % n_f
            self.sends.append(
                remote(source(to), full_ref.at[slot], send_sem.at[d], recv_sem.at[d], (to, z))
            )
            place = back if stride == 1 else back // 2
            self.arrivals.append(
                remote(source(f), full_ref.at[place], send_sem.at[d], recv_sem.at[d], (to, z))
            )

    def start(self):
        self.local.start()
        for item in self.sends:
            item.start()

    def relay(self):
        pass

    def ready(self):
        self.local.wait()
        for item in self.arrivals:
            item.wait_recv()

    def finish(self):
        for item in self.sends:
            item.wait_send()


def square_chips():
    _, _, m, _ = where_am_i()
    x, y = m % 2, m // 2
    return y * 2 + 1 - x, (1 - y) * 2 + x, (1 - y) * 2 + 1 - x


class Near:
    def __init__(self, source, full_ref, send_sem, recv_sem, local_sem, stride):
        f, z, m, c = where_am_i()
        beside, above, _ = square_chips()

        def slot(chip, core):
            return chip * 2 + core if stride == 1 else chip

        mine = full_ref.at[slot(m, c)]
        self.local = pltpu.make_async_copy(source(f), mine, local_sem)
        self.sends, self.arrivals = [], []
        k = 0
        for dc in range(2 // stride):
            core = (c + dc) % 2
            for chip in [beside, above] + ([m] if dc else []):
                to = (chip * 2 + core, z)
                src = source(chip * 2 + core)
                theirs = full_ref.at[slot(chip, core)]
                self.sends.append(remote(src, mine, send_sem.at[k], recv_sem.at[k], to))
                self.arrivals.append(remote(src, theirs, send_sem.at[k], recv_sem.at[k], to))
                k += 1

    def start(self):
        self.local.start()
        for item in self.sends:
            item.start()

    def ready(self):
        self.local.wait()
        for item in self.arrivals:
            item.wait_recv()

    def finish(self):
        for item in self.sends:
            item.wait_send()


class Far:
    def __init__(self, have_ref, full_ref, send_sem, recv_sem, stride):
        f, z, m, c = where_am_i()
        beside, above, far = square_chips()

        def slot(chip, core):
            return chip * 2 + core if stride == 1 else chip

        rows = full_ref.shape[1] // 2
        halves = [pl.ds(0, rows), pl.ds(rows, rows)]
        self.sends, self.arrivals = [], []
        k = 5
        for dc in range(2 // stride):
            core = (c + dc) % 2
            for chip, onto, part in ((beside, above, halves[0]), (above, beside, halves[1])):
                to = (onto * 2 + c, z)
                src = have_ref.at[slot(chip, core), part]
                dst = full_ref.at[slot(chip, core), part]
                lands = full_ref.at[slot(far, core), part]
                self.sends.append(remote(src, dst, send_sem.at[k], recv_sem.at[k], to))
                self.arrivals.append(remote(src, lands, send_sem.at[k], recv_sem.at[k], to))
                k += 1

    def start(self):
        for item in self.sends:
            item.start()

    def ready(self):
        for item in self.arrivals:
            item.wait_recv()

    def finish(self):
        for item in self.sends:
            item.wait_send()


class Relay:
    def __init__(self, source, full_ref, send_sem, recv_sem, local_sem, stride):
        self.near = Near(source, full_ref, send_sem, recv_sem, local_sem, stride)
        self.far = Far(full_ref, full_ref, send_sem, recv_sem, stride)

    def start(self):
        self.near.start()

    def relay(self):
        self.near.ready()
        self.far.start()

    def ready(self):
        self.far.ready()

    def finish(self):
        self.near.finish()
        self.far.finish()


def squared():
    return lax.axis_size("fsdp") == 8


def spreading(source, full_ref, sems, stride):
    kind = Relay if squared() else Spread
    return kind(source, full_ref, *sems, stride)


def spread_sems(steps):
    steps = max(steps, 9)
    return [
        pltpu.SemaphoreType.DMA((steps,)),
        pltpu.SemaphoreType.DMA((steps,)),
        pltpu.SemaphoreType.DMA,
    ]


def fsdp_peers():
    f, z, _, _ = where_am_i()
    n_f = lax.axis_size("fsdp")
    return [((f + d) % n_f, z) for d in range(1, n_f)]


def all_peers(seq):
    f, z, m, c = where_am_i()
    other = m * 2 + 1 - c
    peers = fsdp_peers()
    for d in range(1, seq):
        peers.append((f, (z + d) % seq))
        peers.append((other, (z + d) % seq))
    return peers


class Scatter:
    def __init__(self, part, got_ref, send_sem, recv_sem):
        f, z, m, c = where_am_i()
        n_m = lax.axis_size("fsdp") // 2
        self.part, self.got, self.chip = part, got_ref, m
        self.copies = []
        for d in range(1, n_m):
            to = (m + d) % n_m
            self.copies.append(
                remote(
                    part(to),
                    got_ref.at[d - 1],
                    send_sem.at[d],
                    recv_sem.at[d],
                    (to * 2 + c, z),
                )
            )

    def start(self):
        for item in self.copies:
            item.start()

    def turn(self):
        pass

    def total(self, own):
        for item in self.copies:
            item.wait_recv()
        result = own.astype(F32)
        for k in range(len(self.copies)):
            result = result + self.got[k].astype(F32)
        return result

    def finish(self):
        for item in self.copies:
            item.wait_send()


class Fold:
    def __init__(self, part, got_ref, send_sem, recv_sem):
        f, z, m, c = where_am_i()
        beside, above, far = square_chips()
        self.chips = (beside, above, far)
        count = got_ref.shape[1] // 2

        def half(ref, n):
            return ref.at[pl.ds(n * count, count)]

        def sent(n, src, dst, chip):
            return remote(src, dst, send_sem.at[n], recv_sem.at[n], (chip * 2 + c, z))

        self.got = got_ref
        passing = [half(got_ref.at[2], 0), half(got_ref.at[2], 1)]
        adding = [half(part(beside), 0), half(part(above), 1)]
        self.joins = list(zip(passing, adding))
        self.copies = [
            sent(0, half(part(far), 0), passing[0], above),
            sent(1, half(part(far), 1), passing[1], beside),
            sent(2, half(part(beside), 1), half(got_ref.at[0], 1), beside),
            sent(3, half(part(above), 0), half(got_ref.at[1], 0), above),
            sent(4, passing[0], half(got_ref.at[0], 0), beside),
            sent(5, passing[1], half(got_ref.at[1], 1), above),
        ]

    def start(self):
        for item in self.copies[:4]:
            item.start()

    def turn(self):
        for n in range(2):
            passing, adding = self.joins[n]
            self.copies[n].wait_recv()
            joined = passing[...].astype(F32) + adding[...].astype(F32)
            passing[...] = joined.astype(passing.dtype)
            self.copies[4 + n].start()

    def total(self, own):
        for item in self.copies[2:]:
            item.wait_recv()
        return own.astype(F32) + self.got[0].astype(F32) + self.got[1].astype(F32)

    def finish(self):
        for item in self.copies:
            item.wait_send()


def folding(*args):
    return (Fold if squared() else Scatter)(*args)


def scatter_sems():
    n_m = lax.axis_size("fsdp") // 2
    return [pltpu.SemaphoreType.DMA((max(n_m, 6),)), pltpu.SemaphoreType.DMA((max(n_m, 6),))]


class Across:
    def __init__(self, own_ref, spare_ref, sems):
        f, z, _, _ = where_am_i()
        self.own, self.spare = own_ref, spare_ref
        self.edge = jnp.logical_or(z == 0, z == 3)
        self.inner = jnp.logical_not(self.edge)
        beside = jnp.where(z < 2, 1 - z, 5 - z)
        self.up = remote(own_ref, spare_ref.at[0], sems.at[0], sems.at[1], (f, beside))
        self.swap = remote(own_ref, spare_ref.at[1], sems.at[2], sems.at[3], (f, 3 - z))
        self.down = remote(own_ref, spare_ref.at[1], sems.at[4], sems.at[5], (f, beside))

    def add(self, k):
        total = self.own[...].astype(F32) + self.spare[k].astype(F32)
        self.own[...] = total.astype(self.own.dtype)

    def rise(self):
        pl.when(self.edge)(self.up.start)

    def risen(self):
        @pl.when(self.inner)
        def _():
            self.up.wait_recv()
            self.add(0)

        pl.when(self.edge)(self.up.wait_send)

    def cross(self):
        pl.when(self.inner)(self.swap.start)

    def crossed(self):
        @pl.when(self.inner)
        def _():
            self.swap.wait()
            self.add(1)

    def fall(self):
        pl.when(self.inner)(self.down.start)

    def fallen(self):
        @pl.when(self.edge)
        def _():
            self.down.wait_recv()
            self.own[...] = self.spare[1]

        pl.when(self.inner)(self.down.wait_send)


ACROSS_SEMS = pltpu.SemaphoreType.DMA((6,))


def front_kernel(seq, local, gathers, *refs):
    refs = list(refs)

    def take(n):
        got = refs[:n]
        del refs[:n]
        return got

    x_send, cot_send, wo_send, wu_send = take(4)
    if gathers:
        squares, wi = take(3), take(1)[0]
        given = take(9)
    else:
        wqkv, vecs_out = take(2)
    x_full, n1_out, q_out, k_out, v_out, e_out, o_out, linv_out = take(8)
    mixed_out, cot_full, wo_out, wu_out = take(4)
    if gathers:
        wqkv_out, wi_out, vecs_out, ibias_out = take(4)
    xsems, csems, osems, usems = take(4), take(4), take(3), take(3)
    xv, stage, qa, ka, va, ebuf, lsem, esem, nsem, msend, mrecv, mlocal, nbuf = take(13)
    q, k, v, obuf, lbuf, qkv_sem, osem = take(7)
    if gathers:
        wqkv, wqkv_send, wi_send, small, smalls, wsem, tsem = take(7)
        qsems, isems, vsems = take(3), take(3), take(3)
    f, z, m, c = where_am_i()
    n_f = lax.axis_size("fsdp")
    half = xv.shape[2]
    chunk = 2 * half
    rows, mine = q.shape
    width = xv.shape[3]
    pairs = mine // 128
    other = (m * 2 + 1 - c, z)
    if gathers:
        share = given[0].shape[1]
        piece = given[8].shape[1]
        sorts = []
        for b in range(2):
            for t, ref in enumerate(squares):
                sorts.append(
                    (ref.at[:, pl.ds(b * mine, mine)], wqkv_send.at[b, :, pl.ds(t * mine, mine)])
                )
        for b in range(2):
            for t in range(n_f // 2):
                cols = pl.ds((2 * t + b) * piece, piece)
                sorts.append((wi.at[:, cols], wi_send.at[b, :, pl.ds(t * piece, piece)]))
        sorts = [
            pltpu.make_async_copy(src, dst, tsem.at[n]) for n, (src, dst) in enumerate(sorts)
        ]
        for item in sorts:
            item.start()
        small[...] = jnp.zeros_like(small)
        for r in range(8):
            small[r : r + 1, :share] = given[r][...].astype(F32)
        small[8:9, :piece] = given[8][...].astype(F32)
        vectors = Spread(lambda to: small, smalls, *vsems, 1)
        attn = spreading(lambda to: wqkv_send.at[to % 2], wqkv, qsems, 1)
        feed = spreading(lambda to: wi_send.at[to % 2], wi_out, isems, 1)
    meet(all_peers(seq))
    gather = Gather(x_send, xv, *xsems, seq)
    gather_cot = Gather(cot_send, cot_full, *csems, seq)
    out = spreading(lambda to: wo_send, wo_out, osems, 1)
    outer = (Near if squared() else Spread)(lambda to: wu_send, wu_out, *usems, 2)
    if gathers:
        gather.start()
        vectors.start()
        for item in sorts:
            item.wait()
        attn.start()
        vectors.ready()
        row = lax.broadcasted_iota(jnp.int32, (128, width), 0)
        col = lax.broadcasted_iota(jnp.int32, (128, width), 1)
        vecs = jnp.zeros((16, width), F32)
        for n in range(n_f):
            spot = jnp.logical_and(col - n * share == row, row < share)
            vecs = vecs + nn(
                smalls[n, :, :128].astype(BF16), jnp.where(spot, 1.0, 0.0).astype(BF16)
            )
        vecs_out[...] = vecs[:8]
        for n in range(n_f // 2):
            ibias_out[0:1, n * piece : (n + 1) * piece] = smalls[2 * n + c, 8:9, :piece]
        attn.relay()
        feed.start()
        attn.ready()
        keep_weights = pltpu.make_async_copy(wqkv, wqkv_out, wsem)
        keep_weights.start()
    else:
        gather.start()
    gain = vecs_out[0:1, :]
    shift = vecs_out[1:2, :]
    cols = pl.ds(pl.multiple_of(c * mine, 128), mine)
    qb = vecs_out[2:3, cols]
    vb = vecs_out[3:4, cols]
    keeps = []
    for n, d in enumerate(sorted(range(seq), key=lambda d: min(d, seq - d))):
        at = (z + d) % seq
        gather.hand_on(d)
        if n == seq - 1:
            gather_cot.start()
        gather.ready(d)
        sl = pl.ds(pl.multiple_of(at * chunk, 16), chunk)
        hat, _ = normalize(xv[at].reshape(chunk, width).astype(F32))
        normed = (hat * gain + shift).astype(BF16)
        nbuf[sl, :] = normed
        keeps.append(pltpu.make_async_copy(xv.at[at], x_full.at[at], lsem.at[d]))
        keeps.append(pltpu.make_async_copy(nbuf.at[sl], n1_out.at[sl], nsem.at[d]))
        for item in keeps[-2:]:
            item.start()
        qkv = nn(normed, wqkv[...].reshape(width, 3 * mine))
        q[sl, :] = (qkv[:, :mine] + qb).astype(BF16)
        k[sl, :] = qkv[:, mine : 2 * mine].astype(BF16)
        v[sl, :] = (qkv[:, 2 * mine :] + vb).astype(BF16)
    for n, (src, dst) in enumerate(((q, q_out), (k, k_out), (v, v_out))):
        keeps.append(pltpu.make_async_copy(src, dst, qkv_sem.at[n]))
        keeps[-1].start()
    lane = lax.broadcasted_iota(jnp.int32, (1, 128), 1)
    low = lane < HD
    factor = HD ** (-0.5) * math.log2(math.e)
    steps = [(i, a) for i in range(rows // QB) for a in range(2)]

    def block(i):
        return slice(i * QB, (i + 1) * QB)

    def e_copy(p, i):
        return pltpu.make_async_copy(
            ebuf.at[p % 2, i], e_out.at[p, i], esem.at[p % 2, i]
        )

    def o_copies(p):
        cols = pl.ds(pl.multiple_of(p * 128, 128), 128)
        return (
            pltpu.make_async_copy(obuf.at[p], o_out.at[:, cols], osem.at[0, p]),
            pltpu.make_async_copy(lbuf.at[p], linv_out.at[:, cols], osem.at[1, p]),
        )

    def mixed_copies(p):
        return (
            pltpu.make_async_copy(stage.at[p], mixed_out.at[c, p], mlocal.at[p]),
            remote(stage.at[p], mixed_out.at[c, p], msend.at[p], mrecv.at[p], other),
            remote(stage.at[p], mixed_out.at[1 - c, p], msend.at[p], mrecv.at[p], other),
        )

    def heads(pair, _):
        @pl.when(pair == 0)
        def _():
            if gathers:
                feed.relay()
            out.start()

        pl.when(pair == 1)(outer.start)
        pl.when(pair == pairs - 1)(out.relay)

        @pl.when(pair >= 2)
        def _():
            for i in range(rows // QB):
                e_copy(pair - 2, i).wait()

        here = pl.ds(pl.multiple_of(pair * 128, 128), 128)
        place = lax.broadcasted_iota(jnp.int32, (rows, 1), 0) % (rows // seq)
        bar = jnp.where(place < local, 0.0, -1e38).astype(F32)
        qf, kf, vf = q[:, here].astype(F32), k[:, here].astype(F32), v[:, here].astype(F32)
        for a in range(2):
            own = low if a == 0 else jnp.logical_not(low)
            first = lane == HD * (1 - a)
            qa[a] = jnp.where(own, qf, jnp.where(first, 1.0, 0.0)).astype(BF16)
            ka[a] = jnp.where(own, kf, jnp.where(first, bar, 0.0)).astype(BF16)
            va[a] = jnp.where(own, vf, 1.0).astype(BF16)

        def scored(t):
            i, a = steps[t]
            return nt(qa[a, block(i), :], ka[a])

        raws = {}

        def finish(t, expo):
            i, a = steps[t]
            raws[a] = nn(expo, va[a])
            if a == 1:
                sl = block(i)
                total = pltpu.roll(jnp.where(low, raws[1], raws[0]), HD, 1)
                inv = 1.0 / total
                res = jnp.where(low, raws[0], raws[1]) * inv
                obuf[pair, sl, :] = res
                lbuf[pair, sl, :] = inv
                stage[pair, sl, :] = res.astype(BF16)

        scores, before = scored(0), None
        for t, (i, a) in enumerate(steps):
            peak = jnp.max(scores, -1, keepdims=True)
            upcoming = scored(t + 1) if t + 1 < len(steps) else None
            if before is not None:
                finish(t - 1, before)
            expo = jnp.exp2((scores - peak) * factor).astype(BF16)
            ebuf[pair % 2, i, a] = expo
            if a == 1:
                e_copy(pair, i).start()
            scores, before = upcoming, expo
        finish(len(steps) - 1, before)
        for item in o_copies(pair):
            item.start()
        to_self, to_other, _ = mixed_copies(pair)
        to_self.start()
        to_other.start()
        return 0

    lax.fori_loop(0, pairs, heads, 0)
    for item in keeps:
        item.wait()
    gather.finish()
    if gathers:
        keep_weights.wait()
        vectors.finish()
        attn.finish()
        feed.ready()
        feed.finish()
    out.ready()
    out.finish()
    outer.ready()
    outer.finish()
    for p in range(pairs):
        to_self, to_other, back = mixed_copies(p)
        to_self.wait()
        to_other.wait_send()
        back.wait_recv()
        for item in o_copies(p):
            item.wait()
    for p in range(max(0, pairs - 2), pairs):
        for i in range(rows // QB):
            e_copy(p, i).wait()
    gather_cot.arrived()


def front(x_send, cot_send, wo_send, wu_send, rest, local, seq, gathers):
    _, _, half, width = x_send.shape
    n_f = lax.axis_size("fsdp")
    rows = seq * 2 * half
    share = wo_send.shape[0]
    mine = width // 2
    pairs = mine // 128
    frames = jax.ShapeDtypeStruct((seq, 2, half, width), BF16)
    heads = jax.ShapeDtypeStruct((rows, mine), BF16)
    wide = jax.ShapeDtypeStruct((rows, mine), F32)
    out_specs = [ANY] * 12
    out_shape = [
        frames,
        jax.ShapeDtypeStruct((rows, width), BF16),
        heads,
        heads,
        heads,
        jax.ShapeDtypeStruct((pairs, rows // QB, 2, QB, rows), BF16),
        wide,
        wide,
        jax.ShapeDtypeStruct((2, pairs, rows, 128), BF16),
        frames,
        jax.ShapeDtypeStruct((n_f,) + wo_send.shape, BF16),
        jax.ShapeDtypeStruct((n_f // 2,) + wu_send.shape, BF16),
    ]
    scratch = (
        GATHER_SEMS(seq)
        + GATHER_SEMS(seq)
        + spread_sems(n_f)
        + spread_sems(n_f // 2)
        + [
            pltpu.VMEM((seq, 2, half, width), BF16),
            pltpu.VMEM((pairs, rows, 128), BF16),
            pltpu.VMEM((2, rows, 128), BF16),
            pltpu.VMEM((2, rows, 128), BF16),
            pltpu.VMEM((2, rows, 128), BF16),
            pltpu.VMEM((2, rows // QB, 2, QB, rows), BF16),
            pltpu.SemaphoreType.DMA((seq,)),
            pltpu.SemaphoreType.DMA((2, rows // QB)),
            pltpu.SemaphoreType.DMA((seq,)),
            pltpu.SemaphoreType.DMA((pairs,)),
            pltpu.SemaphoreType.DMA((pairs,)),
            pltpu.SemaphoreType.DMA((pairs,)),
            pltpu.VMEM((rows, width), BF16),
            pltpu.VMEM((rows, mine), BF16),
            pltpu.VMEM((rows, mine), BF16),
            pltpu.VMEM((rows, mine), BF16),
            pltpu.VMEM((pairs, rows, 128), F32),
            pltpu.VMEM((pairs, rows, 128), F32),
            pltpu.SemaphoreType.DMA((3,)),
            pltpu.SemaphoreType.DMA((2, pairs)),
        ]
    )
    in_specs = [ANY] * 4 + [VMEM] * 2
    if gathers:
        piece = rest[-1].shape[1]
        hidden = rest[3].shape[1] // 2
        lanes = max(128, piece)
        in_specs = [ANY] * 8 + [VMEM] * 9
        out_specs += [ANY, ANY, VMEM, VMEM]
        out_shape += [
            jax.ShapeDtypeStruct((n_f, share, 3 * mine), BF16),
            jax.ShapeDtypeStruct((n_f, share, hidden), BF16),
            jax.ShapeDtypeStruct((8, width), F32),
            jax.ShapeDtypeStruct((1, hidden), F32),
        ]
        scratch += [
            pltpu.VMEM((n_f, share, 3 * mine), BF16),
            pltpu.VMEM((2, share, 3 * mine), BF16),
            pltpu.VMEM((2, share, hidden), BF16),
            pltpu.VMEM((16, lanes), F32),
            pltpu.VMEM((n_f, 16, lanes), F32),
            pltpu.SemaphoreType.DMA,
            pltpu.SemaphoreType.DMA((6 + n_f,)),
        ]
        scratch += spread_sems(n_f) + spread_sems(n_f) + spread_sems(n_f)
    return pl.pallas_call(
        lambda *refs: front_kernel(seq, local, gathers, *refs),
        in_specs=in_specs,
        out_specs=out_specs,
        out_shape=out_shape,
        scratch_shapes=scratch,
        compiler_params=pltpu.CompilerParams(
            collective_id=0, has_side_effects=True, vmem_limit_bytes=LIMIT
        ),
        name="front",
    )(x_send, cot_send, wo_send, wu_send, *rest)


def inverse(y):
    guess = pl.reciprocal(y, approx=True)
    return guess * (2.0 - y * guess)


def gelu_parts(u):
    t = inverse(1.0 + (0.3275911 / math.sqrt(2.0)) * jnp.abs(u))
    poly = t * (
        0.127414796
        + t * (-0.142248368 + t * (0.7107068705 + t * (-0.7265760135 + t * 0.5307027145)))
    )
    expo = jnp.exp2((u * u) * (-0.5 * math.log2(math.e)))
    tail = poly * expo
    phi = jnp.where(u >= 0, 1.0 - tail, tail)
    return phi, u * expo * (1.0 / math.sqrt(2.0 * math.pi))


def dense_kernel(
    seq, x, mixed_in, cot_in, wo_in, wi_in, wu_in, vecs, ibias,
    out_back, gres_own, gm_out, gwo_out, gwi_out, ru_out, gvec_out, gib_out,
    xv, mixed, cot, wo, wi, wu, n2, hat2, inv2, resid, active, slope, out_own,
    pstage, precv, grecv, ugot, upart,
    psem, prsem, gsem, grsem, bsend, brecv, usend, urecv, lsem, xsem, csend, crecv, fsend, frecv,
):
    f, z, m, c = where_am_i()
    other = (m * 2 + 1 - c, z)
    half = x.shape[2]
    chunk = 2 * half
    width = x.shape[3]
    mine = gm_out.shape[1]
    hidden = wi.shape[1]
    n_m = gwi_out.shape[0]
    share = gwi_out.shape[2]
    piece = upart.shape[1]
    rows = seq * chunk
    tile = 512

    def block(i):
        return pl.ds(i * chunk, chunk)

    def fetch_x(i):
        return pltpu.make_async_copy(x.at[i], xv.at[i % 2], xsem.at[i % 2])

    def load(k, src, dst):
        return pltpu.make_async_copy(src, dst, lsem.at[k])

    loads = [load(0, mixed_in, mixed), load(1, wo_in, wo), load(2, wi_in, wi)]
    late = [load(3 + k, cot_in.at[k, c], cot.at[k, c]) for k in range(seq)]
    if squared():
        beside, above, _ = square_chips()
        late += [
            load(3 + seq + k, wu_in.at[chip], wu.at[chip])
            for k, chip in enumerate((m, beside, above))
        ]
    else:
        late.append(load(3 + seq, wu_in, wu))
    fetch_x(0).start()
    for item in loads + late:
        item.start()
    meet(all_peers(seq))
    if squared():
        tail = Far(wu_in, wu, fsend, frecv, 2)
        tail.start()
    passes = [
        remote(cot_in.at[k, c], cot.at[k, c], csend.at[k], crecv.at[k], other) for k in range(seq)
    ]
    handed = [
        remote(cot_in.at[k, c], cot.at[k, 1 - c], csend.at[k], crecv.at[k], other)
        for k in range(seq)
    ]
    for item in passes:
        item.start()
    obias, gain, shift, ubias = vecs[4:5, :], vecs[5:6, :], vecs[6:7, :], vecs[7:8, :]
    back = Return(out_own, out_back, bsend, brecv, seq)
    gstage = active.at[:, :width]
    branch = active.at[:, width : 2 * width]
    gown = resid

    def p_copy(i):
        return remote(pstage.at[i, 1 - c], precv.at[i], psem.at[i], prsem.at[i], other)

    def g_copy(i):
        return remote(gstage.at[block(i)], grecv.at[block(i)], gsem.at[i], grsem.at[i], other)

    def mixed_rows(sl):
        return jnp.concatenate(
            [mixed[a, p, sl, :] for a in range(2) for p in range(mixed.shape[1])], axis=1
        )

    def push(i):
        sl = block(i)
        pout = nn(active[sl, :], wu[...].reshape(hidden, width))
        resid[sl, :] += pout
        pstage[i] = pout.astype(BF16).reshape(2, half, width)
        p_copy(i).start()

    for item in loads:
        item.wait()
    for i in range(seq):
        sl = block(i)
        fetch_x(i).wait()
        if i + 1 < seq:
            fetch_x(i + 1).start()
        frames = xv[i % 2].reshape(chunk, width).astype(F32)
        res = frames + nn(mixed_rows(sl), wo[...]) + obias
        hat, inv = normalize(res)
        normed = (hat * gain + shift).astype(BF16)
        resid[sl, :] = res + ubias
        n2[sl, :] = normed
        hat2[sl, :] = hat
        inv2[sl, :] = jnp.broadcast_to(inv, (chunk, 128))
        for j in range(0, hidden, tile):
            cols = slice(j, j + tile)
            inner = nn(normed, wi[:, cols]) + ibias[:, cols]
            phi, bump = gelu_parts(inner)
            active[sl, cols] = (inner * phi).astype(BF16)
            slope[sl, cols] = (phi + bump).astype(BF16)
        if i == 1:
            for item in late:
                item.wait()
            if squared():
                tail.ready()
        if i:
            push(i - 1)
    push(seq - 1)
    for item in handed:
        item.wait_recv()
    cots = cot[...].reshape(rows, width)
    outer = folding(lambda to: upart.at[to], ugot, usend, urecv)

    def give_back():
        for i in range(seq):
            p_copy(i).wait_recv()
            out_own[i] = (
                resid[pl.ds(pl.multiple_of(i * chunk + c * half, 16), half), :]
                + precv[i].astype(F32)
            ).astype(BF16)
        back.start()

    if squared() and piece % 128 == 0:
        for n, chip in enumerate((outer.chips[2], outer.chips[0], outer.chips[1], m)):
            at = pl.ds(pl.multiple_of(chip * piece, 128), piece)
            upart[chip] = tn(active[:, at], cots).astype(BF16)
            for item in (outer.copies[0:2], outer.copies[2:3], outer.copies[3:4], [])[n]:
                item.start()
            if n == 0:
                give_back()
    else:
        for k in range(n_m):
            upart[k] = tn(active[:, k * piece : (k + 1) * piece], cots).astype(BF16)
        outer.start()
        give_back()
    gvec_out[0:1, :] = jnp.sum(cots.astype(F32), 0, keepdims=True)
    for i in range(seq):
        sl = block(i)
        g = cot[i].reshape(chunk, width)
        for j in range(0, hidden, piece):
            cols = slice(j, j + piece)
            gi = (nt(g, wu[j // piece]) * slope[sl, cols].astype(F32)).astype(BF16)
            slope[sl, cols] = gi
            line = jnp.sum(gi.astype(F32), 0, keepdims=True)
            if i == 0:
                gib_out[:, cols] = line
            else:
                gib_out[:, cols] += line
        gn2 = nt(slope[sl, :], wi[...])
        gown[sl, :] = gn2
        gstage[sl, :] = gn2.astype(BF16)
        g_copy(i).start()
        if i == 1:
            outer.turn()
    for j in range(0, hidden, tile):
        part = tn(n2[...], slope[:, j : j + tile])
        for k in range(n_m):
            for b in range(2):
                at = (2 * k + b) * share
                gwi_out[k, b, :, j : j + tile] = part[at : at + share, :].astype(BF16)
    wrows = pl.ds(pl.multiple_of(c * mine, 128), mine)
    for i in range(seq):
        sl = block(i)
        g_copy(i).wait_recv()
        gn2 = gown[sl, :] + grecv[sl, :].astype(F32)
        hat = hat2[sl, :]
        line = jnp.sum(gn2 * hat, 0, keepdims=True)
        flat = jnp.sum(gn2, 0, keepdims=True)
        g = cot[i].reshape(chunk, width).astype(F32)
        gres = g + norm_back(gn2, gain, hat, inv2[sl, 0:1])
        hat2[sl, :] = gres
        low = gres.astype(BF16)
        branch[sl, :] = low
        total = jnp.sum(low.astype(F32), 0, keepdims=True)
        if i == 0:
            lines, flats, totals = line, flat, total
        else:
            lines, flats, totals = lines + line, flats + flat, totals + total
        gm_out[sl, :] = nt(low, wo[wrows, :]).astype(BF16)
        gres_own[i] = hat2[pl.ds(pl.multiple_of(i * chunk + c * half, 16), half), :]
    gvec_out[1:2, :] = lines
    gvec_out[2:3, :] = flats
    gvec_out[3:4, :] = totals
    gvec_out[4:8, :] = jnp.zeros((4, width), F32)
    part = tn(
        mixed_rows(slice(None)),
        active[:, pl.ds(pl.multiple_of(width + c * mine, 128), mine)],
    )
    for k in range(n_m):
        for b in range(2):
            at = (2 * k + b) * share
            gwo_out[k, b] = part[at : at + share, :].astype(BF16)
    for i in range(seq):
        p_copy(i).wait_send()
        g_copy(i).wait_send()
        passes[i].wait_send()
    if squared():
        tail.finish()
    ru_out[...] = outer.total(upart[m]).astype(BF16).reshape(ru_out.shape)
    outer.finish()
    back.finish()


def dense(x, mixed, cot, wo, wi, wu, vecs, ibias):
    seq, _, half, width = x.shape
    rows = seq * 2 * half
    hidden = wi.shape[1]
    mine = width // 2
    n_f = lax.axis_size("fsdp")
    n_m = n_f // 2
    share = width // n_f
    piece = hidden // n_m
    return pl.pallas_call(
        lambda *refs: dense_kernel(seq, *refs),
        in_specs=[ANY] * 6 + [VMEM] * 2,
        out_specs=[ANY] + [VMEM] * 7,
        out_shape=[
            jax.ShapeDtypeStruct((2, 2, half, width), BF16),
            jax.ShapeDtypeStruct((seq, half, width), F32),
            jax.ShapeDtypeStruct((rows, mine), BF16),
            jax.ShapeDtypeStruct((n_m, 2, share, mine), BF16),
            jax.ShapeDtypeStruct((n_m, 2, share, hidden), BF16),
            jax.ShapeDtypeStruct((2, piece // 2, width), BF16),
            jax.ShapeDtypeStruct((8, width), F32),
            jax.ShapeDtypeStruct((1, hidden), F32),
        ],
        scratch_shapes=[
            pltpu.VMEM((2, 2, half, width), BF16),
            pltpu.VMEM(mixed.shape, BF16),
            pltpu.VMEM(cot.shape, BF16),
            pltpu.VMEM(wo.shape, BF16),
            pltpu.VMEM(wi.shape, BF16),
            pltpu.VMEM((n_m, piece, width), BF16),
            pltpu.VMEM((rows, width), BF16),
            pltpu.VMEM((rows, width), F32),
            pltpu.VMEM((rows, 128), F32),
            pltpu.VMEM((rows, width), F32),
            pltpu.VMEM((rows, hidden), BF16),
            pltpu.VMEM((rows, hidden), BF16),
            pltpu.VMEM((seq, half, width), BF16),
            pltpu.VMEM((seq, 2, half, width), BF16),
            pltpu.VMEM((seq, half, width), BF16),
            pltpu.VMEM((rows, width), BF16),
            pltpu.VMEM((n_m - 1, piece, width), BF16),
            pltpu.VMEM((n_m, piece, width), BF16),
            pltpu.SemaphoreType.DMA((seq,)),
            pltpu.SemaphoreType.DMA((seq,)),
            pltpu.SemaphoreType.DMA((seq,)),
            pltpu.SemaphoreType.DMA((seq,)),
        ]
        + RETURN_SEMS(seq)
        + scatter_sems()
        + [
            pltpu.SemaphoreType.DMA((6 + seq,)),
            pltpu.SemaphoreType.DMA((2,)),
            pltpu.SemaphoreType.DMA((seq,)),
            pltpu.SemaphoreType.DMA((seq,)),
            pltpu.SemaphoreType.DMA((7,)),
            pltpu.SemaphoreType.DMA((7,)),
        ],
        compiler_params=pltpu.CompilerParams(
            collective_id=2, has_side_effects=True, vmem_limit_bytes=LIMIT
        ),
        name="dense",
    )(x, mixed, cot, wo, wi, wu, vecs, ibias)


def back_kernel(seq, *refs):
    refs = list(refs)

    def take(n):
        got = refs[:n]
        del refs[:n]
        return got

    gwi, gwo, ru, q_in, k_in, v_in, gm_in, o_in, linv_in, e_in = take(10)
    n1_in, x_in, gres_in, wqkv_in, vecs, gvec, gib = take(7)
    gwu_out, w_out, gwi_out, vec_out, ib_out, ig_back = take(6)
    q, k, v, gm, o, linv, ebuf, n1, x, gres, wqkv, grads = take(12)
    do, dot_, qt, va, km, dvt, dkt = take(7)
    uown, uspare, ri, ispare, igot, ogot, ra, aspare, ito, ato = take(10)
    qpart, qgot, gstage, grecv, ig_own, vown, vspare, vgot, vto = take(9)
    isems, osems, qsems, vsems, gsems, bsems, pair_sems = [take(2) for _ in range(7)]
    zu, zi, za, zv, lsem, esem, wsem = take(7)
    gwiv, gwov = take(2)
    f, z, m, c = where_am_i()
    other = (m * 2 + 1 - c, z)
    rows, mine = q.shape
    half, width = gres.shape[1], gres.shape[2]
    chunk = 2 * half
    pairs = mine // 128
    n_m = gwi.shape[0]
    share, hidden = ri.shape[1], ri.shape[2]
    piece = hidden // n_m
    blocks = rows // QB

    def e_load(p, i):
        return pltpu.make_async_copy(e_in.at[p, i], ebuf.at[i], esem.at[i])

    first = [
        pltpu.make_async_copy(src, dst, lsem.at[n])
        for n, (src, dst) in enumerate(
            (
                (gwi, gwiv),
                (ru, uown),
                (gm_in, gm),
                (linv_in, linv),
                (o_in, o),
                (q_in, q),
                (k_in, k),
                (v_in, v),
                (gwo, gwov),
            )
        )
    ]
    later = [
        pltpu.make_async_copy(src, dst, lsem.at[len(first) + n])
        for n, (src, dst) in enumerate(((n1_in, n1), (gres_in, gres), (x_in.at[:, c], x)))
    ]
    for p in range(pairs):
        for t in range(3):
            later.append(
                pltpu.make_async_copy(
                    wqkv_in.at[:, pl.ds(t * mine + p * 128, 128)],
                    wqkv.at[:, pl.ds((3 * p + t) * 128, 128)],
                    wsem.at[p, t],
                )
            )
    for item in first:
        item.start()
    for i in range(blocks):
        e_load(0, i).start()
    for item in later:
        item.start()
    meet(all_peers(seq))

    outer = [Across(uown.at[n], uspare.at[n], zu.at[n]) for n in range(2)]
    inner = [Across(ri.at[n], ispare.at[n], zi.at[n]) for n in range(2)]
    parts = [Across(ra.at[n], aspare.at[n], za.at[n]) for n in range(4)]
    vectors = Across(vown, vspare, zv)
    inner_sums = [
        folding(lambda to, n=n: gwiv.at[to, n], igot.at[n], isems[0].at[n], isems[1].at[n])
        for n in range(2)
    ]
    out_sum = folding(lambda to: gwov.at[to], ogot, *osems)
    pair_sums = [
        folding(lambda to, n=n: qpart.at[n, to], qgot.at[n], qsems[0].at[n], qsems[1].at[n])
        for n in range(pairs)
    ]
    vector_sum = Scatter(lambda to: vown, vgot, *vsems)
    back = Return(ig_own, ig_back, *bsems, seq)

    def g_copy(i):
        return remote(
            gstage.at[i, 1 - c], grecv.at[i], gsems[0].at[i], gsems[1].at[i], other
        )

    def pass_on(n, src, dst):
        return remote(src, dst, pair_sems[0].at[n], pair_sems[1].at[n], other)

    def summed(n):
        ri[n] = inner_sums[n].total(gwiv[m, n]).astype(BF16)
        inner[n].rise()

    for item in first[:2]:
        item.wait()
    inner_sums[0].start()
    outer[0].rise()
    for item in first[2:]:
        item.wait()

    def part_sum(n):
        if n == 3:
            ra[3] = out_sum.total(gwov[m]).astype(BF16)
        else:
            ra[n] = pair_sums[n].total(qpart[n, m]).astype(BF16)
        parts[n].rise()

    def event_1():
        outer[0].risen()
        outer[0].cross()
        outer[1].rise()
        inner_sums[0].turn()
        inner_sums[1].start()

    def event_2():
        outer[0].crossed()
        outer[0].fall()
        outer[1].risen()
        outer[1].cross()
        summed(0)

    def event_3():
        inner[0].risen()
        inner[0].cross()
        outer[1].crossed()
        outer[1].fall()
        out_sum.start()

    def event_4():
        summed(1)
        out_sum.turn()
        pair_sums[0].start()

    def event_5():
        inner[0].crossed()
        inner[0].fall()
        part_sum(3)
        pair_sums[0].turn()
        pair_sums[1].start()

    def event_6():
        inner[1].risen()
        inner[1].cross()
        part_sum(0)
        pair_sums[1].turn()
        parts[3].risen()
        parts[3].cross()

    events = {
        0: [(2, event_4)],
        2: [(1, event_2)],
        4: [(1, inner_sums[1].turn), (2, event_5)],
        8: [(0, event_1), (1, event_3), (2, event_6)],
    }
    third = HD ** (-0.5)
    lane = lax.broadcasted_iota(jnp.int32, (1, 128), 1)
    low = lane < HD
    steps = [(i, a) for i in range(blocks) for a in range(2)]

    def block(i):
        return slice(i * QB, (i + 1) * QB)

    def sub(a):
        return slice(a * HD, (a + 1) * HD)

    for item in later:
        item.wait()

    def heads(pair, _):
        for when, action in events[0]:
            pl.when(pair == when)(action)
        here = pl.ds(pl.multiple_of(pair * 128, 128), 128)

        def spot(t):
            return pl.ds(pl.multiple_of((3 * pair + t) * 128, 128), 128)

        scaled = (gm[:, here].astype(F32) * linv[:, here]).astype(BF16).astype(F32)
        kf, vf = k[:, here].astype(F32), v[:, here].astype(F32)
        weighted = scaled * o[:, here]
        for a in range(2):
            own = low if a == 0 else jnp.logical_not(low)
            delta = jnp.sum(jnp.where(own, weighted, 0.0), -1, keepdims=True)
            high = delta.astype(BF16).astype(F32)
            middle = (delta - high).astype(BF16).astype(F32)
            last = delta - high - middle
            base = HD * (1 - a)
            extra = jnp.where(
                lane == base,
                high,
                jnp.where(lane == base + 1, middle, jnp.where(lane == base + 2, last, 0.0)),
            )
            do[a] = jnp.where(own, scaled, -extra).astype(BF16)
            va[a] = jnp.where(own, vf, 1.0).astype(BF16)
            km[a] = jnp.where(own, kf, 0.0).astype(BF16)
        dot_[...] = scaled.astype(BF16).T
        qt[...] = q[:, here].T

        def pushed(t):
            i, a = steps[t]
            return nt(do[a, block(i), :], va[a])

        dqs = {}
        upcoming = jnp.minimum(pair + 1, pairs - 1)
        push = pushed(0)
        for t, (i, a) in enumerate(steps):
            for when, action in events.get(t, []) if t else []:
                pl.when(pair == when)(action)
            if a == 0:
                e_load(pair, i).wait()
            sl = block(i)
            p = ebuf[i, a]
            ds = (p.astype(F32) * push).astype(BF16)
            push = pushed(t + 1) if t + 1 < len(steps) else None
            dv = nn(dot_[sub(a), sl], p)
            dk = nn(qt[sub(a), sl], ds)
            dqs[a] = nn(ds, km[a])
            if i == 0:
                dvt[sub(a), :] = dv
                dkt[sub(a), :] = dk
            else:
                dvt[sub(a), :] += dv
                dkt[sub(a), :] += dk
            if a == 1:
                e_load(upcoming, i).start()
                grads[sl, spot(0)] = ((dqs[0] + dqs[1]) * third).astype(BF16)
        grads[:, spot(1)] = (dkt[...] * third).astype(BF16).T
        grads[:, spot(2)] = dvt[...].astype(BF16).T
        cols = pl.ds(pl.multiple_of(3 * pair * 128, 128), 3 * 128)
        part = tn(n1[...], grads[:, cols])
        for j in range(n_m):
            for b in range(2):
                at = (2 * j + b) * share
                qpart[pair, j, b] = part[at : at + share, :].astype(BF16)
        return 0

    lax.fori_loop(0, pairs, heads, 0)
    pair_sums[2].start()
    part_sum(1)
    parts[0].risen()
    parts[0].cross()
    for i in range(blocks):
        e_load(pairs - 1, i).wait()
    for i in range(seq):
        sl = slice(i * chunk, (i + 1) * chunk)
        gn1 = nt(grads[sl, :], wqkv[...])
        o[sl, :] = gn1[:, :mine]
        linv[sl, :] = gn1[:, mine:]
        gstage[i] = gn1.astype(BF16).reshape(2, half, width)
        g_copy(i).start()
    pair_sums[2].turn()
    inner[1].crossed()
    inner[1].fall()
    parts[1].risen()
    parts[1].cross()
    parts[3].crossed()
    parts[3].fall()
    vown[...] = jnp.zeros_like(vown)
    for p in range(pairs):
        cols = pl.ds(pl.multiple_of(c * mine + p * 128, 128), 128)
        for r, t in ((2, 0), (3, 2)):
            at = (3 * p + t) * 128
            vown[r : r + 1, cols] = jnp.sum(
                grads[:, at : at + 128].astype(F32), 0, keepdims=True
            )
    for n, r in enumerate((3, 1, 2, 0)):
        vown[4 + n : 5 + n, :] = 0.5 * gvec[r : r + 1, :]
    lines = hidden // width
    for n in range(lines):
        vown[pl.ds(8 + lines * c + n, 1), :] = gib[:, n * width : (n + 1) * width]
    gain = vecs[0:1, :]
    for i in range(seq):
        g_copy(i).wait_recv()
        sl = pl.ds(pl.multiple_of(i * chunk + c * half, 16), half)
        gn1 = jnp.concatenate([o[sl, :], linv[sl, :]], axis=1) + grecv[i].astype(F32)
        hat, inv = normalize(x[i].astype(F32))
        line = jnp.sum(gn1 * hat, 0, keepdims=True)
        flat = jnp.sum(gn1, 0, keepdims=True)
        if i == 0:
            gain_sum, shift_sum = line, flat
        else:
            gain_sum, shift_sum = gain_sum + line, shift_sum + flat
        ig_own[i] = (gres[i] + norm_back(gn1, gain, hat, inv)).astype(BF16)
        pl.when((z < 2) == (i < 2))(back.ships[i].start)
        if i == seq // 2:
            part_sum(2)
            parts[0].crossed()
            parts[0].fall()
    parts[2].risen()
    parts[2].cross()
    for i in range(seq):
        pl.when((z < 2) != (i < 2))(back.ships[i].start)
    parts[1].crossed()
    parts[1].fall()
    vown[0:1, :] = gain_sum
    vown[1:2, :] = shift_sum
    vector_sum.start()
    total = vector_sum.total(vown[...])
    vector_sum.finish()
    vown[...] = total
    vectors.rise()
    parts[2].crossed()
    parts[2].fall()
    vectors.risen()
    vectors.cross()
    outer[0].fallen()
    outer[1].fallen()
    gwu_out[...] = uown[...]
    inner[0].fallen()
    crosses = {}

    def hand_over(n, src, dst):
        crosses[n] = pass_on(n, src, dst)
        crosses[n].start()

    for n in range(2):
        if n:
            inner[n].fallen()
        pl.when(c != n)(pass_on(n, ri.at[n], ito).start)
    parts[3].fallen()
    hand_over(5, ra.at[3, 1 - c], ato.at[3])
    parts[0].fallen()
    hand_over(2, ra.at[0, 1 - c], ato.at[0])
    vectors.crossed()
    vectors.fall()
    for n in range(2):
        pl.when(c == n)(pass_on(n, ri.at[1 - n], ito).wait_recv)
        pl.when(c != n)(pass_on(n, ri.at[n], ito).wait_send)
    if piece % 128:
        gwi_out[c] = ri[c]
        gwi_out[1 - c] = ito[...]
    else:
        for n in range(n_m):
            cols = slice(n * piece, (n + 1) * piece)
            here = pl.ds(pl.multiple_of((2 * n + c) * piece, 128), piece)
            there = pl.ds(pl.multiple_of((2 * n + 1 - c) * piece, 128), piece)
            gwi_out[:, here] = ri[c, :, cols]
            gwi_out[:, there] = ito[:, cols]
    for p in (1, 2):
        parts[p].fallen()
        hand_over(2 + p, ra.at[p, 1 - c], ato.at[p])
    here = pl.ds(pl.multiple_of(c * mine, 128), mine)
    there = pl.ds(pl.multiple_of((1 - c) * mine, 128), mine)
    crosses[5].wait()
    w_out[3, :, here] = ra[3, c]
    w_out[3, :, there] = ato[3]
    for p in range(pairs):
        crosses[2 + p].wait()
        here = pl.ds(pl.multiple_of(c * mine + p * 128, 128), 128)
        there = pl.ds(pl.multiple_of((1 - c) * mine + p * 128, 128), 128)
        for t in range(3):
            w_out[t, :, here] = ra[p, c, :, t * 128 : (t + 1) * 128]
            w_out[t, :, there] = ato[p, :, t * 128 : (t + 1) * 128]
    vectors.fallen()
    hand_over(6, vown, vto)
    crosses[6].wait()
    vto[...] = vown[...] + vto[...]
    turned = pltpu.roll(vto[0:8, :], (width - f * share) % width, 1)
    vec_out[...] = turned[:, :share]
    per = width // piece
    line = jnp.broadcast_to(vto[pl.ds(8 + lines * c + m // per, 1), :], (8, width))
    ib_out[...] = pltpu.roll(line, (width - (m % per) * piece) % width, 1)[0:1, :piece]
    for i in range(seq):
        g_copy(i).wait_send()
    for item in inner_sums + [out_sum] + pair_sums:
        item.finish()
    back.finish()


def back(gwi, gwo, ru, q, k, v, gm, o, linv, e, n1, x, gres, wqkv, vecs, gvec, gib):
    seq, _, half, width = x.shape
    n_m, _, share, hidden = gwi.shape
    rows, mine = q.shape
    pairs = mine // 128
    piece = hidden // n_m
    block = (2, share, mine)
    assert pairs == 3 and seq == 4

    def sems(*shape):
        return pltpu.SemaphoreType.DMA(shape)

    def two(*shape):
        return [sems(*shape), sems(*shape)]

    return pl.pallas_call(
        lambda *refs: back_kernel(seq, *refs),
        in_specs=[ANY] * 14 + [VMEM] * 3,
        out_specs=[VMEM] * 5 + [ANY],
        out_shape=[
            jax.ShapeDtypeStruct(ru.shape, BF16),
            jax.ShapeDtypeStruct((4, share, width), BF16),
            jax.ShapeDtypeStruct(
                (2, share, hidden) if piece % 128 else (share, 2 * hidden), BF16
            ),
            jax.ShapeDtypeStruct((8, share), F32),
            jax.ShapeDtypeStruct((1, piece), F32),
            jax.ShapeDtypeStruct((2, 2, half, width), BF16),
        ],
        scratch_shapes=[
            pltpu.VMEM((rows, mine), BF16),
            pltpu.VMEM((rows, mine), BF16),
            pltpu.VMEM((rows, mine), BF16),
            pltpu.VMEM((rows, mine), BF16),
            pltpu.VMEM((rows, mine), F32),
            pltpu.VMEM((rows, mine), F32),
            pltpu.VMEM(e.shape[1:], BF16),
            pltpu.VMEM((rows, width), BF16),
            pltpu.VMEM((seq, half, width), BF16),
            pltpu.VMEM((seq, half, width), F32),
            pltpu.VMEM(wqkv.shape, BF16),
            pltpu.VMEM((rows, 3 * mine), BF16),
            pltpu.VMEM((2, rows, 128), BF16),
            pltpu.VMEM((128, rows), BF16),
            pltpu.VMEM((128, rows), BF16),
            pltpu.VMEM((2, rows, 128), BF16),
            pltpu.VMEM((2, rows, 128), BF16),
            pltpu.VMEM((128, rows), F32),
            pltpu.VMEM((128, rows), F32),
            pltpu.VMEM(ru.shape, BF16),
            pltpu.VMEM((2,) + ru.shape, BF16),
            pltpu.VMEM((2, share, hidden), BF16),
            pltpu.VMEM((2, 2, share, hidden), BF16),
            pltpu.VMEM((2, n_m - 1, share, hidden), BF16),
            pltpu.VMEM((n_m - 1,) + block, BF16),
            pltpu.VMEM((4,) + block, BF16),
            pltpu.VMEM((4, 2) + block, BF16),
            pltpu.VMEM((share, hidden), BF16),
            pltpu.VMEM((4, share, mine), BF16),
            pltpu.VMEM((pairs, n_m) + block, BF16),
            pltpu.VMEM((pairs, n_m - 1) + block, BF16),
            pltpu.VMEM((seq, 2, half, width), BF16),
            pltpu.VMEM((seq, half, width), BF16),
            pltpu.VMEM((seq, half, width), BF16),
            pltpu.VMEM((16, width), F32),
            pltpu.VMEM((2, 16, width), F32),
            pltpu.VMEM((n_m - 1, 16, width), F32),
            pltpu.VMEM((16, width), F32),
        ]
        + two(2, max(n_m, 6))
        + two(max(n_m, 6))
        + two(pairs, max(n_m, 6))
        + two(n_m)
        + two(seq)
        + RETURN_SEMS(seq)
        + two(7)
        + [sems(2, 6), sems(2, 6), sems(4, 6), sems(6), sems(12), sems(rows // QB)]
        + [sems(pairs, 3), pltpu.VMEM(gwi.shape, BF16), pltpu.VMEM(gwo.shape, BF16)],
        compiler_params=pltpu.CompilerParams(
            collective_id=3, has_side_effects=True, vmem_limit_bytes=LIMIT
        ),
        name="back",
    )(gwi, gwo, ru, q, k, v, gm, o, linv, e, n1, x, gres, wqkv, vecs, gvec, gib)


def widen_kernel(w, gwi, gwu, vec, ib, *outs):
    for k in range(4):
        outs[k][...] = w[k].astype(F32)
    outs[4][...] = gwi[...].astype(F32)
    outs[5][...] = gwu[...].astype(F32)
    outs[6][...] = ib[...]
    for k in range(8):
        outs[7 + k][...] = vec[k : k + 1, :]


def widen(w, gwi, gwu, vec, ib):
    square = jax.ShapeDtypeStruct(w.shape[1:], F32)
    return pl.pallas_call(
        widen_kernel,
        in_specs=[VMEM] * 5,
        out_specs=[VMEM] * 15,
        out_shape=[square] * 4
        + [jax.ShapeDtypeStruct(value.shape, F32) for value in (gwi, gwu, ib)]
        + [jax.ShapeDtypeStruct((1, vec.shape[1]), F32)] * 8,
        compiler_params=pltpu.CompilerParams(vmem_limit_bytes=LIMIT),
        name="widen",
    )(w, gwi, gwu, vec, ib)


def per_device(
    frames,
    cotangent,
    valid_slots,
    first_gain,
    first_shift,
    query_weight,
    query_bias,
    key_weight,
    value_weight,
    value_bias,
    output_weight,
    output_bias,
    second_gain,
    second_shift,
    inner_weight,
    inner_bias,
    outer_weight,
    outer_bias,
):
    seq = lax.axis_size("seq")
    n_f = lax.axis_size("fsdp")
    f = lax.axis_index("fsdp")
    m, c = f // 2, f % 2
    slots, local, width = frames.shape
    chunk = -(-local // 128) * 128
    half = chunk // 2
    mine = width // 2
    share = width // n_f
    piece = inner_bias.shape[0]
    hidden = piece * n_f // 2

    keep = valid_slots.astype(BF16)[:, None, None]
    pad = ((0, 0), (0, chunk - local), (0, 0))
    x_send = jnp.pad(frames, pad).reshape(slots, 2, half, width)
    cot_send = jnp.pad(cotangent * keep, pad).reshape(slots, 2, half, width)
    vectors = (
        first_gain,
        first_shift,
        query_bias,
        value_bias,
        output_bias,
        second_gain,
        second_shift,
        outer_bias,
    )
    if share % 16 == 0 and piece % 128 == 0:
        rest = [query_weight, key_weight, value_weight, inner_weight]
        rest += [value[None] for value in vectors] + [inner_bias.astype(F32)[None]]
        *kept, wqkv, wi, vecs, ibias = front(
            x_send, cot_send, output_weight, outer_weight, rest, local, seq, True
        )
        wqkv = wqkv.reshape(width, 3 * mine)
        wi = wi.reshape(width, hidden)
    else:

        def gathered(value, axis=0):
            return lax.all_gather(value, "fsdp", axis=axis, tiled=True)

        def my_columns(value):
            return lax.dynamic_slice_in_dim(value, c * mine, mine, axis=1)

        wqkv = jnp.concatenate(
            [my_columns(gathered(w)) for w in (query_weight, key_weight, value_weight)], axis=1
        )
        wi = gathered(inner_weight).reshape(width, n_f // 2, 2, piece)
        wi = lax.dynamic_index_in_dim(wi, c, 2, keepdims=False).reshape(width, hidden)
        vecs = gathered(jnp.stack(vectors), 1).astype(F32)
        ibias = gathered(inner_bias).astype(F32).reshape(n_f // 2, 2, piece)
        ibias = lax.dynamic_index_in_dim(ibias, c, 1, keepdims=False).reshape(1, hidden)
        kept = front(
            x_send, cot_send, output_weight, outer_weight, [wqkv, vecs], local, seq, False
        )

    x, n1, q, k, v, e, o, linv, mixed, cot, wo, wu = kept
    wo = wo.reshape(width, width)
    out_back, gres, gm, gwo, gwi, ru, gvec, gib = dense(x, mixed, cot, wo, wi, wu, vecs, ibias)
    gwu, w, gwi, vec, ib, ig_back = back(
        gwi, gwo, ru, q, k, v, gm, o, linv, e, n1, x, gres, wqkv, vecs, gvec, gib
    )
    if gwi.ndim == 3:
        gwi = gwi.reshape(2, share, n_f // 2, piece).transpose(1, 2, 0, 3)
        gwi = gwi.reshape(share, 2 * hidden)
    gwq, gwk, gwv, gwo, gwi, gwu, ib, fg, fs, qb, vb, ob, sg, ss, ub = widen(
        w, gwi, gwu.reshape(piece, width), vec, ib
    )
    keep32 = valid_slots.astype(F32)[:, None, None]
    outputs = (out_back.reshape(slots, chunk, width)[:, :local].astype(F32) * keep32).astype(BF16)
    input_grad = ig_back.reshape(slots, chunk, width)[:, :local]
    return (
        outputs,
        input_grad,
        fg[0],
        fs[0],
        gwq,
        qb[0],
        gwk,
        gwv,
        vb[0],
        gwo,
        ob[0],
        sg[0],
        ss[0],
        gwi,
        ib.reshape(piece),
        gwu,
        ub[0],
    )


def solution(mesh):
    rows = P("fsdp", "seq", None)
    vector, matrix = P("fsdp"), P("fsdp", None)
    weights = (
        vector,
        vector,
        matrix,
        vector,
        matrix,
        matrix,
        vector,
        matrix,
        vector,
        vector,
        vector,
        matrix,
        vector,
        matrix,
        vector,
    )
    return jax.shard_map(
        per_device,
        mesh=mesh,
        in_specs=(rows, rows, vector) + weights,
        out_specs=(rows, rows) + weights,
        check_vma=False,
    )
```

```python
import math

import jax
import jax.numpy as jnp
from jax import lax
from jax.experimental import pallas as pl
from jax.experimental.pallas import tpu as pltpu
from jax.sharding import PartitionSpec as P

H = 12
HD = 64
EPS = 1e-05
MESH = pl.DeviceIdType.MESH
F32 = jnp.float32
BF16 = jnp.bfloat16
ANY = pl.BlockSpec(memory_space=pl.ANY)
VMEM = pl.BlockSpec(memory_space=pltpu.VMEM)
LIMIT = 62 << 20
QB = 256


def nn(a, b):
    return lax.dot_general(a, b, (((1,), (0,)), ((), ())), preferred_element_type=F32)


def nt(a, b):
    return lax.dot_general(a, b, (((1,), (1,)), ((), ())), preferred_element_type=F32)


def tn(a, b):
    return lax.dot_general(a, b, (((0,), (0,)), ((), ())), preferred_element_type=F32)


def normalize(rows):
    center = rows - jnp.mean(rows, -1, keepdims=True)
    inv = lax.rsqrt(jnp.mean(center * center, -1, keepdims=True) + EPS)
    return center * inv, inv


def norm_back(grad, gain, hat, inv):
    tilted = grad * gain
    first = jnp.mean(tilted, -1, keepdims=True)
    cross = jnp.mean(tilted * hat, -1, keepdims=True)
    return inv * (tilted - first - hat * cross)


def where_am_i():
    f = lax.axis_index("fsdp")
    z = lax.axis_index("seq")
    return f, z, f // 2, f % 2


def meet(peers):
    barrier = pltpu.get_barrier_semaphore()
    for peer in peers:
        pl.semaphore_signal(barrier, inc=1, device_id=peer, device_id_type=MESH)
    pl.semaphore_wait(barrier, len(peers))


def column_peers(seq):
    f, z, m, c = where_am_i()
    peers = []
    for dc in range(2):
        for dz in range(seq):
            if dc or dz:
                peers.append((m * 2 + (c + dc) % 2, (z + dz) % seq))
    return peers


class Ship:
    def __init__(self, src, dst, send, recv, target):
        f, z, _, _ = where_am_i()
        self.here = jnp.logical_and(target[0] == f, target[1] == z)
        self.local = pltpu.make_async_copy(src, dst, recv)
        self.remote = pltpu.make_async_remote_copy(
            src, dst, send, recv, device_id=target, device_id_type=MESH
        )

    def start(self):
        pl.when(self.here)(self.local.start)
        pl.when(jnp.logical_not(self.here))(self.remote.start)

    def wait_send(self):
        pl.when(jnp.logical_not(self.here))(self.remote.wait_send)


def remote(src, dst, send, recv, target):
    return pltpu.make_async_remote_copy(
        src, dst, send, recv, device_id=target, device_id_type=MESH
    )


class Gather:
    def __init__(self, send_ref, full_ref, send_sem, recv_sem, pass_send, pass_recv, seq):
        f, z, m, c = where_am_i()
        self.ships = []
        for i in range(2):
            for h in range(2):
                slot = 2 * c + i
                self.ships.append(
                    Ship(
                        send_ref.at[i, h],
                        full_ref.at[z, h],
                        send_sem.at[i, h],
                        recv_sem.at[z],
                        (m * 2 + h, slot),
                    )
                )
        other = (m * 2 + 1 - c, z)
        chips = [(z + d) % seq for d in range(seq)]
        self.arrivals = [
            remote(send_ref.at[0, 0], full_ref.at[k, c], send_sem.at[0, 0], recv_sem.at[k], other)
            for k in chips
        ]
        self.passes = [
            remote(full_ref.at[k, c], full_ref.at[k, c], pass_send.at[d], pass_recv.at[d], other)
            for d, k in enumerate(chips)
        ]
        self.handed = [
            remote(
                full_ref.at[k, c], full_ref.at[k, 1 - c], pass_send.at[d], pass_recv.at[d], other
            )
            for d, k in enumerate(chips)
        ]

    def start(self):
        for ship in self.ships:
            ship.start()

    def arrived(self):
        for item in self.arrivals:
            item.wait_recv()
        for ship in self.ships:
            ship.wait_send()

    def hand_on(self, k):
        self.arrivals[k].wait_recv()
        self.passes[k].start()

    def ready(self, k):
        self.handed[k].wait_recv()

    def finish(self):
        for ship in self.ships:
            ship.wait_send()
        for item in self.passes:
            item.wait_send()


GATHER_SEMS = lambda seq: [
    pltpu.SemaphoreType.DMA((2, 2)),
    pltpu.SemaphoreType.DMA((seq,)),
    pltpu.SemaphoreType.DMA((seq,)),
    pltpu.SemaphoreType.DMA((seq,)),
]


class Return:
    def __init__(self, own_ref, back_ref, send_sem, recv_sem, seq):
        f, z, m, c = where_am_i()
        home = z // 2
        self.ships = [
            Ship(
                own_ref.at[k],
                back_ref.at[z % 2, c],
                send_sem.at[k],
                recv_sem.at[z % 2, c],
                (m * 2 + home, k),
            )
            for k in range(seq)
        ]
        self.arrivals = [
            remote(
                own_ref.at[0],
                back_ref.at[i, h],
                send_sem.at[0],
                recv_sem.at[i, h],
                (m * 2 + 1 - c, z),
            )
            for i in range(2)
            for h in range(2)
        ]

    def start(self):
        for ship in self.ships:
            ship.start()

    def finish(self):
        for ship in self.ships:
            ship.wait_send()
        for item in self.arrivals:
            item.wait_recv()


RETURN_SEMS = lambda seq: [pltpu.SemaphoreType.DMA((seq,)), pltpu.SemaphoreType.DMA((2, 2))]


class Spread:
    def __init__(self, source, full_ref, send_sem, recv_sem, local_sem, stride):
        f, z, m, c = where_am_i()
        n_f = lax.axis_size("fsdp")
        steps = n_f // stride
        slot = f if stride == 1 else m
        self.local = pltpu.make_async_copy(source(f), full_ref.at[slot], local_sem)
        self.sends = []
        self.arrivals = []
        for d in range(1, steps):
            to = (f + d * stride) % n_f
            back = (f + n_f - d * stride) % n_f
            self.sends.append(
                remote(source(to), full_ref.at[slot], send_sem.at[d], recv_sem.at[d], (to, z))
            )
            place = back if stride == 1 else back // 2
            self.arrivals.append(
                remote(source(f), full_ref.at[place], send_sem.at[d], recv_sem.at[d], (to, z))
            )

    def start(self):
        self.local.start()
        for item in self.sends:
            item.start()

    def relay(self):
        pass

    def ready(self):
        self.local.wait()
        for item in self.arrivals:
            item.wait_recv()

    def finish(self):
        for item in self.sends:
            item.wait_send()


def square_chips():
    _, _, m, _ = where_am_i()
    x, y = m % 2, m // 2
    return y * 2 + 1 - x, (1 - y) * 2 + x, (1 - y) * 2 + 1 - x


class Near:
    def __init__(self, source, full_ref, send_sem, recv_sem, local_sem, stride):
        f, z, m, c = where_am_i()
        beside, above, _ = square_chips()

        def slot(chip, core):
            return chip * 2 + core if stride == 1 else chip

        mine = full_ref.at[slot(m, c)]
        self.local = pltpu.make_async_copy(source(f), mine, local_sem)
        self.sends, self.arrivals = [], []
        k = 0
        for dc in range(2 // stride):
            core = (c + dc) % 2
            for chip in [beside, above] + ([m] if dc else []):
                to = (chip * 2 + core, z)
                src = source(chip * 2 + core)
                theirs = full_ref.at[slot(chip, core)]
                self.sends.append(remote(src, mine, send_sem.at[k], recv_sem.at[k], to))
                self.arrivals.append(remote(src, theirs, send_sem.at[k], recv_sem.at[k], to))
                k += 1

    def start(self):
        self.local.start()
        for item in self.sends:
            item.start()

    def ready(self):
        self.local.wait()
        for item in self.arrivals:
            item.wait_recv()

    def finish(self):
        for item in self.sends:
            item.wait_send()


class Far:
    def __init__(self, have_ref, full_ref, send_sem, recv_sem, stride):
        f, z, m, c = where_am_i()
        beside, above, far = square_chips()

        def slot(chip, core):
            return chip * 2 + core if stride == 1 else chip

        rows = full_ref.shape[1] // 2
        halves = [pl.ds(0, rows), pl.ds(rows, rows)]
        self.sends, self.arrivals = [], []
        k = 5
        for dc in range(2 // stride):
            core = (c + dc) % 2
            for chip, onto, part in ((beside, above, halves[0]), (above, beside, halves[1])):
                to = (onto * 2 + c, z)
                src = have_ref.at[slot(chip, core), part]
                dst = full_ref.at[slot(chip, core), part]
                lands = full_ref.at[slot(far, core), part]
                self.sends.append(remote(src, dst, send_sem.at[k], recv_sem.at[k], to))
                self.arrivals.append(remote(src, lands, send_sem.at[k], recv_sem.at[k], to))
                k += 1

    def start(self):
        for item in self.sends:
            item.start()

    def ready(self):
        for item in self.arrivals:
            item.wait_recv()

    def finish(self):
        for item in self.sends:
            item.wait_send()


class Relay:
    def __init__(self, source, full_ref, send_sem, recv_sem, local_sem, stride):
        self.near = Near(source, full_ref, send_sem, recv_sem, local_sem, stride)
        self.far = Far(full_ref, full_ref, send_sem, recv_sem, stride)

    def start(self):
        self.near.start()

    def relay(self):
        self.near.ready()
        self.far.start()

    def ready(self):
        self.far.ready()

    def finish(self):
        self.near.finish()
        self.far.finish()


def squared():
    return lax.axis_size("fsdp") == 8


def spreading(source, full_ref, sems, stride):
    kind = Relay if squared() else Spread
    return kind(source, full_ref, *sems, stride)


def spread_sems(steps):
    steps = max(steps, 9)
    return [
        pltpu.SemaphoreType.DMA((steps,)),
        pltpu.SemaphoreType.DMA((steps,)),
        pltpu.SemaphoreType.DMA,
    ]


def fsdp_peers():
    f, z, _, _ = where_am_i()
    n_f = lax.axis_size("fsdp")
    return [((f + d) % n_f, z) for d in range(1, n_f)]


def all_peers(seq):
    f, z, m, c = where_am_i()
    other = m * 2 + 1 - c
    peers = fsdp_peers()
    for d in range(1, seq):
        peers.append((f, (z + d) % seq))
        peers.append((other, (z + d) % seq))
    return peers


class Scatter:
    def __init__(self, part, got_ref, send_sem, recv_sem):
        f, z, m, c = where_am_i()
        n_m = lax.axis_size("fsdp") // 2
        self.part, self.got, self.chip = part, got_ref, m
        self.copies = []
        for d in range(1, n_m):
            to = (m + d) % n_m
            self.copies.append(
                remote(
                    part(to),
                    got_ref.at[d - 1],
                    send_sem.at[d],
                    recv_sem.at[d],
                    (to * 2 + c, z),
                )
            )

    def start(self):
        for item in self.copies:
            item.start()

    def turn(self):
        pass

    def total(self, own):
        for item in self.copies:
            item.wait_recv()
        result = own.astype(F32)
        for k in range(len(self.copies)):
            result = result + self.got[k].astype(F32)
        return result

    def finish(self):
        for item in self.copies:
            item.wait_send()


class Fold:
    def __init__(self, part, got_ref, send_sem, recv_sem):
        f, z, m, c = where_am_i()
        beside, above, far = square_chips()
        self.chips = (beside, above, far)
        count = got_ref.shape[1] // 2

        def half(ref, n):
            return ref.at[pl.ds(n * count, count)]

        def sent(n, src, dst, chip):
            return remote(src, dst, send_sem.at[n], recv_sem.at[n], (chip * 2 + c, z))

        self.got = got_ref
        passing = [half(got_ref.at[2], 0), half(got_ref.at[2], 1)]
        adding = [half(part(beside), 0), half(part(above), 1)]
        self.joins = list(zip(passing, adding))
        self.copies = [
            sent(0, half(part(far), 0), passing[0], above),
            sent(1, half(part(far), 1), passing[1], beside),
            sent(2, half(part(beside), 1), half(got_ref.at[0], 1), beside),
            sent(3, half(part(above), 0), half(got_ref.at[1], 0), above),
            sent(4, passing[0], half(got_ref.at[0], 0), beside),
            sent(5, passing[1], half(got_ref.at[1], 1), above),
        ]

    def start(self):
        for item in self.copies[:4]:
            item.start()

    def turn(self):
        for n in range(2):
            passing, adding = self.joins[n]
            self.copies[n].wait_recv()
            joined = passing[...].astype(F32) + adding[...].astype(F32)
            passing[...] = joined.astype(passing.dtype)
            self.copies[4 + n].start()

    def total(self, own):
        for item in self.copies[2:]:
            item.wait_recv()
        return own.astype(F32) + self.got[0].astype(F32) + self.got[1].astype(F32)

    def finish(self):
        for item in self.copies:
            item.wait_send()


def folding(*args):
    return (Fold if squared() else Scatter)(*args)


def scatter_sems():
    n_m = lax.axis_size("fsdp") // 2
    return [pltpu.SemaphoreType.DMA((max(n_m, 6),)), pltpu.SemaphoreType.DMA((max(n_m, 6),))]


class Across:
    def __init__(self, own_ref, spare_ref, sems):
        f, z, _, _ = where_am_i()
        self.own, self.spare = own_ref, spare_ref
        self.edge = jnp.logical_or(z == 0, z == 3)
        self.inner = jnp.logical_not(self.edge)
        beside = jnp.where(z < 2, 1 - z, 5 - z)
        self.up = remote(own_ref, spare_ref.at[0], sems.at[0], sems.at[1], (f, beside))
        self.swap = remote(own_ref, spare_ref.at[1], sems.at[2], sems.at[3], (f, 3 - z))
        self.down = remote(own_ref, spare_ref.at[1], sems.at[4], sems.at[5], (f, beside))

    def add(self, k):
        total = self.own[...].astype(F32) + self.spare[k].astype(F32)
        self.own[...] = total.astype(self.own.dtype)

    def rise(self):
        pl.when(self.edge)(self.up.start)

    def risen(self):
        @pl.when(self.inner)
        def _():
            self.up.wait_recv()
            self.add(0)

        pl.when(self.edge)(self.up.wait_send)

    def cross(self):
        pl.when(self.inner)(self.swap.start)

    def crossed(self):
        @pl.when(self.inner)
        def _():
            self.swap.wait()
            self.add(1)

    def fall(self):
        pl.when(self.inner)(self.down.start)

    def fallen(self):
        @pl.when(self.edge)
        def _():
            self.down.wait_recv()
            self.own[...] = self.spare[1]

        pl.when(self.inner)(self.down.wait_send)


ACROSS_SEMS = pltpu.SemaphoreType.DMA((6,))


def front_kernel(seq, local, gathers, *refs):
    refs = list(refs)

    def take(n):
        got = refs[:n]
        del refs[:n]
        return got

    x_send, cot_send, wo_send, wu_send = take(4)
    if gathers:
        squares, wi = take(3), take(1)[0]
        given = take(9)
    else:
        wqkv, vecs_out = take(2)
    x_full, n1_out, q_out, k_out, v_out, e_out, o_out, linv_out = take(8)
    mixed_out, cot_full, wo_out, wu_out = take(4)
    if gathers:
        wqkv_out, wi_out, vecs_out, ibias_out = take(4)
    xsems, csems, osems, usems = take(4), take(4), take(3), take(3)
    xv, stage, qa, ka, va, ebuf, lsem, esem, nsem, msend, mrecv, mlocal, nbuf = take(13)
    q, k, v, obuf, lbuf, qkv_sem, osem = take(7)
    psems = take(2)
    if gathers:
        wqkv, wqkv_send, wi_send, small, smalls, wsem, tsem = take(7)
        qsems, isems, vsems = take(3), take(3), take(3)
    f, z, m, c = where_am_i()
    n_f = lax.axis_size("fsdp")
    half = xv.shape[2]
    chunk = 2 * half
    rows, mine = q.shape
    width = xv.shape[3]
    pairs = mine // 128
    other = (m * 2 + 1 - c, z)
    if gathers:
        share = given[0].shape[1]
        piece = given[8].shape[1]
        sorts = []
        for b in range(2):
            for t, ref in enumerate(squares):
                sorts.append(
                    (ref.at[:, pl.ds(b * mine, mine)], wqkv_send.at[b, :, pl.ds(t * mine, mine)])
                )
        for b in range(2):
            for t in range(n_f // 2):
                cols = pl.ds((2 * t + b) * piece, piece)
                sorts.append((wi.at[:, cols], wi_send.at[b, :, pl.ds(t * piece, piece)]))
        sorts = [
            pltpu.make_async_copy(src, dst, tsem.at[n]) for n, (src, dst) in enumerate(sorts)
        ]
        for item in sorts:
            item.start()
        small[...] = jnp.zeros_like(small)
        for r in range(8):
            small[r : r + 1, :share] = given[r][...].astype(F32)
        small[8:9, :piece] = given[8][...].astype(F32)
        vectors = Spread(lambda to: small, smalls, *vsems, 1)
        attn = spreading(lambda to: wqkv_send.at[to % 2], wqkv, qsems, 1)
        feed = spreading(lambda to: wi_send.at[to % 2], wi_out, isems, 1)
    meet(all_peers(seq))
    gather = Gather(x_send, xv, *xsems, seq)
    gather_cot = Gather(cot_send, cot_full, *csems, seq)
    out = spreading(lambda to: wo_send, wo_out.at[c], osems, 2)
    out_pass = remote(wo_out.at[c], wo_out.at[c], psems[0], psems[1], other)
    out_got = remote(wo_out.at[c], wo_out.at[1 - c], psems[0], psems[1], other)
    outer = (Near if squared() else Spread)(lambda to: wu_send, wu_out, *usems, 2)
    if gathers:
        gather.start()
        vectors.start()
        for item in sorts:
            item.wait()
        attn.start()
        vectors.ready()
        row = lax.broadcasted_iota(jnp.int32, (128, width), 0)
        col = lax.broadcasted_iota(jnp.int32, (128, width), 1)
        vecs = jnp.zeros((16, width), F32)
        for n in range(n_f):
            spot = jnp.logical_and(col - n * share == row, row < share)
            vecs = vecs + nn(
                smalls[n, :, :128].astype(BF16), jnp.where(spot, 1.0, 0.0).astype(BF16)
            )
        vecs_out[...] = vecs[:8]
        for n in range(n_f // 2):
            ibias_out[0:1, n * piece : (n + 1) * piece] = smalls[2 * n + c, 8:9, :piece]
        attn.relay()
        out.start()
        feed.start()
        attn.ready()
        keep_weights = pltpu.make_async_copy(wqkv, wqkv_out, wsem)
        keep_weights.start()
    else:
        gather.start()
        out.start()
    gain = vecs_out[0:1, :]
    shift = vecs_out[1:2, :]
    cols = pl.ds(pl.multiple_of(c * mine, 128), mine)
    qb = vecs_out[2:3, cols]
    vb = vecs_out[3:4, cols]
    keeps = []
    for n, d in enumerate(sorted(range(seq), key=lambda d: min(d, seq - d))):
        at = (z + d) % seq
        gather.hand_on(d)
        if n == seq - 1:
            gather_cot.start()
        gather.ready(d)
        sl = pl.ds(pl.multiple_of(at * chunk, 16), chunk)
        hat, _ = normalize(xv[at].reshape(chunk, width).astype(F32))
        normed = (hat * gain + shift).astype(BF16)
        nbuf[sl, :] = normed
        keeps.append(pltpu.make_async_copy(xv.at[at], x_full.at[at], lsem.at[d]))
        keeps.append(pltpu.make_async_copy(nbuf.at[sl], n1_out.at[sl], nsem.at[d]))
        for item in keeps[-2:]:
            item.start()
        qkv = nn(normed, wqkv[...].reshape(width, 3 * mine))
        q[sl, :] = (qkv[:, :mine] + qb).astype(BF16)
        k[sl, :] = qkv[:, mine : 2 * mine].astype(BF16)
        v[sl, :] = (qkv[:, 2 * mine :] + vb).astype(BF16)
    for n, (src, dst) in enumerate(((q, q_out), (k, k_out), (v, v_out))):
        keeps.append(pltpu.make_async_copy(src, dst, qkv_sem.at[n]))
        keeps[-1].start()
    lane = lax.broadcasted_iota(jnp.int32, (1, 128), 1)
    low = lane < HD
    factor = HD ** (-0.5) * math.log2(math.e)
    steps = [(i, a) for i in range(rows // QB) for a in range(2)]

    def block(i):
        return slice(i * QB, (i + 1) * QB)

    def e_copy(p, i):
        return pltpu.make_async_copy(
            ebuf.at[p % 2, i], e_out.at[p, i], esem.at[p % 2, i]
        )

    def o_copies(p):
        cols = pl.ds(pl.multiple_of(p * 128, 128), 128)
        return (
            pltpu.make_async_copy(obuf.at[p], o_out.at[:, cols], osem.at[0, p]),
            pltpu.make_async_copy(lbuf.at[p], linv_out.at[:, cols], osem.at[1, p]),
        )

    def mixed_copies(p):
        return (
            pltpu.make_async_copy(stage.at[p], mixed_out.at[c, p], mlocal.at[p]),
            remote(stage.at[p], mixed_out.at[c, p], msend.at[p], mrecv.at[p], other),
            remote(stage.at[p], mixed_out.at[1 - c, p], msend.at[p], mrecv.at[p], other),
        )

    def heads(pair, _):
        @pl.when(pair == 0)
        def _():
            out.relay()
            if gathers:
                feed.relay()
            outer.start()

        @pl.when(pair == 1)
        def _():
            out.ready()
            out_pass.start()


        @pl.when(pair >= 2)
        def _():
            for i in range(rows // QB):
                e_copy(pair - 2, i).wait()

        here = pl.ds(pl.multiple_of(pair * 128, 128), 128)
        place = lax.broadcasted_iota(jnp.int32, (rows, 1), 0) % (rows // seq)
        bar = jnp.where(place < local, 0.0, -1e38).astype(F32)
        qf, kf, vf = q[:, here].astype(F32), k[:, here].astype(F32), v[:, here].astype(F32)
        for a in range(2):
            own = low if a == 0 else jnp.logical_not(low)
            first = lane == HD * (1 - a)
            qa[a] = jnp.where(own, qf, jnp.where(first, 1.0, 0.0)).astype(BF16)
            ka[a] = jnp.where(own, kf, jnp.where(first, bar, 0.0)).astype(BF16)
            va[a] = jnp.where(own, vf, 1.0).astype(BF16)

        def scored(t):
            i, a = steps[t]
            return nt(qa[a, block(i), :], ka[a])

        raws = {}

        def finish(t, expo):
            i, a = steps[t]
            raws[a] = nn(expo, va[a])
            if a == 1:
                sl = block(i)
                total = pltpu.roll(jnp.where(low, raws[1], raws[0]), HD, 1)
                inv = 1.0 / total
                res = jnp.where(low, raws[0], raws[1]) * inv
                obuf[pair, sl, :] = res
                lbuf[pair, sl, :] = inv
                stage[pair, sl, :] = res.astype(BF16)

        scores, before = scored(0), None
        for t, (i, a) in enumerate(steps):
            peak = jnp.max(scores, -1, keepdims=True)
            upcoming = scored(t + 1) if t + 1 < len(steps) else None
            if before is not None:
                finish(t - 1, before)
            expo = jnp.exp2((scores - peak) * factor).astype(BF16)
            ebuf[pair % 2, i, a] = expo
            if a == 1:
                e_copy(pair, i).start()
            scores, before = upcoming, expo
        finish(len(steps) - 1, before)
        for item in o_copies(pair):
            item.start()
        to_self, to_other, _ = mixed_copies(pair)
        to_self.start()
        to_other.start()
        return 0

    lax.fori_loop(0, pairs, heads, 0)
    for item in keeps:
        item.wait()
    gather.finish()
    if gathers:
        keep_weights.wait()
        vectors.finish()
        attn.finish()
        feed.ready()
        feed.finish()
    out.finish()
    out_pass.wait_send()
    out_got.wait_recv()
    outer.ready()
    outer.finish()
    for p in range(pairs):
        to_self, to_other, back = mixed_copies(p)
        to_self.wait()
        to_other.wait_send()
        back.wait_recv()
        for item in o_copies(p):
            item.wait()
    for p in range(max(0, pairs - 2), pairs):
        for i in range(rows // QB):
            e_copy(p, i).wait()
    gather_cot.arrived()


def front(x_send, cot_send, wo_send, wu_send, rest, local, seq, gathers):
    _, _, half, width = x_send.shape
    n_f = lax.axis_size("fsdp")
    rows = seq * 2 * half
    share = wo_send.shape[0]
    mine = width // 2
    pairs = mine // 128
    frames = jax.ShapeDtypeStruct((seq, 2, half, width), BF16)
    heads = jax.ShapeDtypeStruct((rows, mine), BF16)
    wide = jax.ShapeDtypeStruct((rows, mine), F32)
    out_specs = [ANY] * 12
    out_shape = [
        frames,
        jax.ShapeDtypeStruct((rows, width), BF16),
        heads,
        heads,
        heads,
        jax.ShapeDtypeStruct((pairs, rows // QB, 2, QB, rows), BF16),
        wide,
        wide,
        jax.ShapeDtypeStruct((2, pairs, rows, 128), BF16),
        frames,
        jax.ShapeDtypeStruct((2, n_f // 2) + wo_send.shape, BF16),
        jax.ShapeDtypeStruct((n_f // 2,) + wu_send.shape, BF16),
    ]
    scratch = (
        GATHER_SEMS(seq)
        + GATHER_SEMS(seq)
        + spread_sems(n_f)
        + spread_sems(n_f // 2)
        + [
            pltpu.VMEM((seq, 2, half, width), BF16),
            pltpu.VMEM((pairs, rows, 128), BF16),
            pltpu.VMEM((2, rows, 128), BF16),
            pltpu.VMEM((2, rows, 128), BF16),
            pltpu.VMEM((2, rows, 128), BF16),
            pltpu.VMEM((2, rows // QB, 2, QB, rows), BF16),
            pltpu.SemaphoreType.DMA((seq,)),
            pltpu.SemaphoreType.DMA((2, rows // QB)),
            pltpu.SemaphoreType.DMA((seq,)),
            pltpu.SemaphoreType.DMA((pairs,)),
            pltpu.SemaphoreType.DMA((pairs,)),
            pltpu.SemaphoreType.DMA((pairs,)),
            pltpu.VMEM((rows, width), BF16),
            pltpu.VMEM((rows, mine), BF16),
            pltpu.VMEM((rows, mine), BF16),
            pltpu.VMEM((rows, mine), BF16),
            pltpu.VMEM((pairs, rows, 128), F32),
            pltpu.VMEM((pairs, rows, 128), F32),
            pltpu.SemaphoreType.DMA((3,)),
            pltpu.SemaphoreType.DMA((2, pairs)),
            pltpu.SemaphoreType.DMA,
            pltpu.SemaphoreType.DMA,
        ]
    )
    in_specs = [ANY] * 4 + [VMEM] * 2
    if gathers:
        piece = rest[-1].shape[1]
        hidden = rest[3].shape[1] // 2
        lanes = max(128, piece)
        in_specs = [ANY] * 8 + [VMEM] * 9
        out_specs += [ANY, ANY, VMEM, VMEM]
        out_shape += [
            jax.ShapeDtypeStruct((n_f, share, 3 * mine), BF16),
            jax.ShapeDtypeStruct((n_f, share, hidden), BF16),
            jax.ShapeDtypeStruct((8, width), F32),
            jax.ShapeDtypeStruct((1, hidden), F32),
        ]
        scratch += [
            pltpu.VMEM((n_f, share, 3 * mine), BF16),
            pltpu.VMEM((2, share, 3 * mine), BF16),
            pltpu.VMEM((2, share, hidden), BF16),
            pltpu.VMEM((16, lanes), F32),
            pltpu.VMEM((n_f, 16, lanes), F32),
            pltpu.SemaphoreType.DMA,
            pltpu.SemaphoreType.DMA((6 + n_f,)),
        ]
        scratch += spread_sems(n_f) + spread_sems(n_f) + spread_sems(n_f)
    return pl.pallas_call(
        lambda *refs: front_kernel(seq, local, gathers, *refs),
        in_specs=in_specs,
        out_specs=out_specs,
        out_shape=out_shape,
        scratch_shapes=scratch,
        compiler_params=pltpu.CompilerParams(
            collective_id=0, has_side_effects=True, vmem_limit_bytes=LIMIT
        ),
        name="front",
    )(x_send, cot_send, wo_send, wu_send, *rest)


def inverse(y):
    guess = pl.reciprocal(y, approx=True)
    return guess * (2.0 - y * guess)


def gelu_parts(u):
    t = inverse(1.0 + (0.3275911 / math.sqrt(2.0)) * jnp.abs(u))
    poly = t * (
        0.127414796
        + t * (-0.142248368 + t * (0.7107068705 + t * (-0.7265760135 + t * 0.5307027145)))
    )
    expo = jnp.exp2((u * u) * (-0.5 * math.log2(math.e)))
    tail = poly * expo
    phi = jnp.where(u >= 0, 1.0 - tail, tail)
    return phi, u * expo * (1.0 / math.sqrt(2.0 * math.pi))


def dense_kernel(
    seq, x, mixed_in, cot_in, wo_in, wi_in, wu_in, vecs, ibias,
    out_back, gres_own, gm_out, gwo_out, gwi_out, ru_out, gvec_out, gib_out,
    xv, mixed, cot, wo, wi, wu, n2, hat2, inv2, resid, active, slope, out_own,
    pstage, precv, grecv, ugot, upart,
    psem, prsem, gsem, grsem, bsend, brecv, usend, urecv, lsem, xsem, csend, crecv, fsend, frecv, osem,
):
    f, z, m, c = where_am_i()
    other = (m * 2 + 1 - c, z)
    half = x.shape[2]
    chunk = 2 * half
    width = x.shape[3]
    mine = gm_out.shape[1]
    hidden = wi.shape[1]
    n_m = gwi_out.shape[0]
    share = gwi_out.shape[2]
    piece = upart.shape[1]
    rows = seq * chunk
    tile = 512

    def block(i):
        return pl.ds(i * chunk, chunk)

    def fetch_x(i):
        return pltpu.make_async_copy(x.at[i], xv.at[i % 2], xsem.at[i % 2])

    def load(k, src, dst):
        return pltpu.make_async_copy(src, dst, lsem.at[k])

    loads = [load(0, mixed_in, mixed), load(2, wi_in, wi)]
    if len(wo_in.shape) == 2:
        loads.append(load(1, wo_in, wo))
    else:
        for a in range(2):
            for chip in range(n_m):
                at = pl.ds((2 * chip + a) * share, share)
                loads.append(
                    pltpu.make_async_copy(wo_in.at[a, chip], wo.at[at], osem.at[a, chip])
                )
    late = [load(3 + k, cot_in.at[k, c], cot.at[k, c]) for k in range(seq)]
    if squared():
        beside, above, _ = square_chips()
        late += [
            load(3 + seq + k, wu_in.at[chip], wu.at[chip])
            for k, chip in enumerate((m, beside, above))
        ]
    else:
        late.append(load(3 + seq, wu_in, wu))
    fetch_x(0).start()
    for item in loads + late:
        item.start()
    meet(all_peers(seq))
    if squared():
        tail = Far(wu_in, wu, fsend, frecv, 2)
        tail.start()
    passes = [
        remote(cot_in.at[k, c], cot.at[k, c], csend.at[k], crecv.at[k], other) for k in range(seq)
    ]
    handed = [
        remote(cot_in.at[k, c], cot.at[k, 1 - c], csend.at[k], crecv.at[k], other)
        for k in range(seq)
    ]
    for item in passes:
        item.start()
    obias, gain, shift, ubias = vecs[4:5, :], vecs[5:6, :], vecs[6:7, :], vecs[7:8, :]
    back = Return(out_own, out_back, bsend, brecv, seq)
    gstage = active.at[:, :width]
    branch = active.at[:, width : 2 * width]
    gown = resid

    def p_copy(i):
        return remote(pstage.at[i, 1 - c], precv.at[i], psem.at[i], prsem.at[i], other)

    def g_copy(i):
        return remote(gstage.at[block(i)], grecv.at[block(i)], gsem.at[i], grsem.at[i], other)

    def mixed_rows(sl):
        return jnp.concatenate(
            [mixed[a, p, sl, :] for a in range(2) for p in range(mixed.shape[1])], axis=1
        )

    def push(i):
        sl = block(i)
        pout = nn(active[sl, :], wu[...].reshape(hidden, width))
        resid[sl, :] += pout
        pstage[i] = pout.astype(BF16).reshape(2, half, width)
        p_copy(i).start()

    for item in loads:
        item.wait()
    for i in range(seq):
        sl = block(i)
        fetch_x(i).wait()
        if i + 1 < seq:
            fetch_x(i + 1).start()
        frames = xv[i % 2].reshape(chunk, width).astype(F32)
        res = frames + nn(mixed_rows(sl), wo[...]) + obias
        hat, inv = normalize(res)
        normed = (hat * gain + shift).astype(BF16)
        resid[sl, :] = res + ubias
        n2[sl, :] = normed
        hat2[sl, :] = hat
        inv2[sl, :] = jnp.broadcast_to(inv, (chunk, 128))
        for j in range(0, hidden, tile):
            cols = slice(j, j + tile)
            inner = nn(normed, wi[:, cols]) + ibias[:, cols]
            phi, bump = gelu_parts(inner)
            active[sl, cols] = (inner * phi).astype(BF16)
            slope[sl, cols] = (phi + bump).astype(BF16)
        if i == 1:
            for item in late:
                item.wait()
            if squared():
                tail.ready()
        if i:
            push(i - 1)
    push(seq - 1)
    for item in handed:
        item.wait_recv()
    cots = cot[...].reshape(rows, width)
    outer = folding(lambda to: upart.at[to], ugot, usend, urecv)

    def give_back():
        for i in range(seq):
            p_copy(i).wait_recv()
            out_own[i] = (
                resid[pl.ds(pl.multiple_of(i * chunk + c * half, 16), half), :]
                + precv[i].astype(F32)
            ).astype(BF16)
        back.start()

    if squared() and piece % 128 == 0:
        for n, chip in enumerate((outer.chips[2], outer.chips[0], outer.chips[1], m)):
            at = pl.ds(pl.multiple_of(chip * piece, 128), piece)
            upart[chip] = tn(active[:, at], cots).astype(BF16)
            for item in (outer.copies[0:2], outer.copies[2:3], outer.copies[3:4], [])[n]:
                item.start()
            if n == 0:
                give_back()
    else:
        for k in range(n_m):
            upart[k] = tn(active[:, k * piece : (k + 1) * piece], cots).astype(BF16)
        outer.start()
        give_back()
    gvec_out[0:1, :] = jnp.sum(cots.astype(F32), 0, keepdims=True)
    for i in range(seq):
        sl = block(i)
        g = cot[i].reshape(chunk, width)
        for j in range(0, hidden, piece):
            cols = slice(j, j + piece)
            gi = (nt(g, wu[j // piece]) * slope[sl, cols].astype(F32)).astype(BF16)
            slope[sl, cols] = gi
            line = jnp.sum(gi.astype(F32), 0, keepdims=True)
            if i == 0:
                gib_out[:, cols] = line
            else:
                gib_out[:, cols] += line
        gn2 = nt(slope[sl, :], wi[...])
        gown[sl, :] = gn2
        gstage[sl, :] = gn2.astype(BF16)
        g_copy(i).start()
        if i == 1:
            outer.turn()
    for j in range(0, hidden, tile):
        part = tn(n2[...], slope[:, j : j + tile])
        for k in range(n_m):
            for b in range(2):
                at = (2 * k + b) * share
                gwi_out[k, b, :, j : j + tile] = part[at : at + share, :].astype(BF16)
    wrows = pl.ds(pl.multiple_of(c * mine, 128), mine)
    for i in range(seq):
        sl = block(i)
        g_copy(i).wait_recv()
        gn2 = gown[sl, :] + grecv[sl, :].astype(F32)
        hat = hat2[sl, :]
        line = jnp.sum(gn2 * hat, 0, keepdims=True)
        flat = jnp.sum(gn2, 0, keepdims=True)
        g = cot[i].reshape(chunk, width).astype(F32)
        gres = g + norm_back(gn2, gain, hat, inv2[sl, 0:1])
        hat2[sl, :] = gres
        low = gres.astype(BF16)
        branch[sl, :] = low
        total = jnp.sum(low.astype(F32), 0, keepdims=True)
        if i == 0:
            lines, flats, totals = line, flat, total
        else:
            lines, flats, totals = lines + line, flats + flat, totals + total
        gm_out[sl, :] = nt(low, wo[wrows, :]).astype(BF16)
        gres_own[i] = hat2[pl.ds(pl.multiple_of(i * chunk + c * half, 16), half), :]
    gvec_out[1:2, :] = lines
    gvec_out[2:3, :] = flats
    gvec_out[3:4, :] = totals
    gvec_out[4:8, :] = jnp.zeros((4, width), F32)
    part = tn(
        mixed_rows(slice(None)),
        active[:, pl.ds(pl.multiple_of(width + c * mine, 128), mine)],
    )
    for k in range(n_m):
        for b in range(2):
            at = (2 * k + b) * share
            gwo_out[k, b] = part[at : at + share, :].astype(BF16)
    for i in range(seq):
        p_copy(i).wait_send()
        g_copy(i).wait_send()
        passes[i].wait_send()
    if squared():
        tail.finish()
    ru_out[...] = outer.total(upart[m]).astype(BF16).reshape(ru_out.shape)
    outer.finish()
    back.finish()


def dense(x, mixed, cot, wo, wi, wu, vecs, ibias):
    seq, _, half, width = x.shape
    rows = seq * 2 * half
    hidden = wi.shape[1]
    mine = width // 2
    n_f = lax.axis_size("fsdp")
    n_m = n_f // 2
    share = width // n_f
    piece = hidden // n_m
    return pl.pallas_call(
        lambda *refs: dense_kernel(seq, *refs),
        in_specs=[ANY] * 6 + [VMEM] * 2,
        out_specs=[ANY] + [VMEM] * 7,
        out_shape=[
            jax.ShapeDtypeStruct((2, 2, half, width), BF16),
            jax.ShapeDtypeStruct((seq, half, width), F32),
            jax.ShapeDtypeStruct((rows, mine), BF16),
            jax.ShapeDtypeStruct((n_m, 2, share, mine), BF16),
            jax.ShapeDtypeStruct((n_m, 2, share, hidden), BF16),
            jax.ShapeDtypeStruct((2, piece // 2, width), BF16),
            jax.ShapeDtypeStruct((8, width), F32),
            jax.ShapeDtypeStruct((1, hidden), F32),
        ],
        scratch_shapes=[
            pltpu.VMEM((2, 2, half, width), BF16),
            pltpu.VMEM(mixed.shape, BF16),
            pltpu.VMEM(cot.shape, BF16),
            pltpu.VMEM((width, width), BF16),
            pltpu.VMEM(wi.shape, BF16),
            pltpu.VMEM((n_m, piece, width), BF16),
            pltpu.VMEM((rows, width), BF16),
            pltpu.VMEM((rows, width), F32),
            pltpu.VMEM((rows, 128), F32),
            pltpu.VMEM((rows, width), F32),
            pltpu.VMEM((rows, hidden), BF16),
            pltpu.VMEM((rows, hidden), BF16),
            pltpu.VMEM((seq, half, width), BF16),
            pltpu.VMEM((seq, 2, half, width), BF16),
            pltpu.VMEM((seq, half, width), BF16),
            pltpu.VMEM((rows, width), BF16),
            pltpu.VMEM((n_m - 1, piece, width), BF16),
            pltpu.VMEM((n_m, piece, width), BF16),
            pltpu.SemaphoreType.DMA((seq,)),
            pltpu.SemaphoreType.DMA((seq,)),
            pltpu.SemaphoreType.DMA((seq,)),
            pltpu.SemaphoreType.DMA((seq,)),
        ]
        + RETURN_SEMS(seq)
        + scatter_sems()
        + [
            pltpu.SemaphoreType.DMA((6 + seq,)),
            pltpu.SemaphoreType.DMA((2,)),
            pltpu.SemaphoreType.DMA((seq,)),
            pltpu.SemaphoreType.DMA((seq,)),
            pltpu.SemaphoreType.DMA((7,)),
            pltpu.SemaphoreType.DMA((7,)),
            pltpu.SemaphoreType.DMA((2, n_m)),
        ],
        compiler_params=pltpu.CompilerParams(
            collective_id=2, has_side_effects=True, vmem_limit_bytes=LIMIT
        ),
        name="dense",
    )(x, mixed, cot, wo, wi, wu, vecs, ibias)


def back_kernel(seq, *refs):
    refs = list(refs)

    def take(n):
        got = refs[:n]
        del refs[:n]
        return got

    gwi, gwo, ru, q_in, k_in, v_in, gm_in, o_in, linv_in, e_in = take(10)
    n1_in, x_in, gres_in, wqkv_in, vecs, gvec, gib = take(7)
    gwu_out, w_out, gwi_out, vec_out, ib_out, ig_back = take(6)
    q, k, v, gm, o, linv, ebuf, n1, x, gres, wqkv, grads = take(12)
    do, dot_, qt, va, km, dvt, dkt = take(7)
    uown, uspare, ri, ispare, igot, ogot, ra, aspare, ito, ato = take(10)
    qpart, qgot, gstage, grecv, ig_own, vown, vspare, vgot, vto = take(9)
    isems, osems, qsems, vsems, gsems, bsems, pair_sems = [take(2) for _ in range(7)]
    zu, zi, za, zv, lsem, esem, wsem = take(7)
    gwiv, gwov = take(2)
    f, z, m, c = where_am_i()
    other = (m * 2 + 1 - c, z)
    rows, mine = q.shape
    half, width = gres.shape[1], gres.shape[2]
    chunk = 2 * half
    pairs = mine // 128
    n_m = gwi.shape[0]
    share, hidden = ri.shape[1], ri.shape[2]
    piece = hidden // n_m
    blocks = rows // QB

    def e_load(p, i):
        return pltpu.make_async_copy(e_in.at[p, i], ebuf.at[i], esem.at[i])

    first = [
        pltpu.make_async_copy(src, dst, lsem.at[n])
        for n, (src, dst) in enumerate(
            (
                (gwi, gwiv),
                (ru, uown),
                (gm_in, gm),
                (linv_in, linv),
                (o_in, o),
                (q_in, q),
                (k_in, k),
                (v_in, v),
                (gwo, gwov),
            )
        )
    ]
    later = [
        pltpu.make_async_copy(src, dst, lsem.at[len(first) + n])
        for n, (src, dst) in enumerate(((n1_in, n1), (gres_in, gres), (x_in.at[:, c], x)))
    ]
    for p in range(pairs):
        for t in range(3):
            later.append(
                pltpu.make_async_copy(
                    wqkv_in.at[:, pl.ds(t * mine + p * 128, 128)],
                    wqkv.at[:, pl.ds((3 * p + t) * 128, 128)],
                    wsem.at[p, t],
                )
            )
    for item in first:
        item.start()
    for i in range(blocks):
        e_load(0, i).start()
    for item in later:
        item.start()
    meet(all_peers(seq))

    outer = [Across(uown.at[n], uspare.at[n], zu.at[n]) for n in range(2)]
    inner = [Across(ri.at[n], ispare.at[n], zi.at[n]) for n in range(2)]
    parts = [Across(ra.at[n], aspare.at[n], za.at[n]) for n in range(4)]
    vectors = Across(vown, vspare, zv)
    inner_sums = [
        folding(lambda to, n=n: gwiv.at[to, n], igot.at[n], isems[0].at[n], isems[1].at[n])
        for n in range(2)
    ]
    out_sum = folding(lambda to: gwov.at[to], ogot, *osems)
    pair_sums = [
        folding(lambda to, n=n: qpart.at[n, to], qgot.at[n], qsems[0].at[n], qsems[1].at[n])
        for n in range(pairs)
    ]
    vector_sum = Scatter(lambda to: vown, vgot, *vsems)
    back = Return(ig_own, ig_back, *bsems, seq)

    def g_copy(i):
        return remote(
            gstage.at[i, 1 - c], grecv.at[i], gsems[0].at[i], gsems[1].at[i], other
        )

    def pass_on(n, src, dst):
        return remote(src, dst, pair_sems[0].at[n], pair_sems[1].at[n], other)

    def summed(n):
        ri[n] = inner_sums[n].total(gwiv[m, n]).astype(BF16)
        inner[n].rise()

    for item in first[:2]:
        item.wait()
    inner_sums[0].start()
    outer[0].rise()
    for item in first[2:]:
        item.wait()

    def part_sum(n):
        if n == 3:
            ra[3] = out_sum.total(gwov[m]).astype(BF16)
        else:
            ra[n] = pair_sums[n].total(qpart[n, m]).astype(BF16)
        parts[n].rise()

    def event_1():
        outer[0].risen()
        outer[0].cross()
        outer[1].rise()
        inner_sums[0].turn()
        inner_sums[1].start()

    def event_2():
        outer[0].crossed()
        outer[0].fall()
        outer[1].risen()
        outer[1].cross()
        summed(0)

    def event_3():
        inner[0].risen()
        inner[0].cross()
        outer[1].crossed()
        outer[1].fall()
        out_sum.start()

    def event_4():
        summed(1)
        out_sum.turn()
        pair_sums[0].start()

    def event_5():
        inner[0].crossed()
        inner[0].fall()
        part_sum(3)
        pair_sums[0].turn()
        pair_sums[1].start()

    def event_6():
        inner[1].risen()
        inner[1].cross()
        part_sum(0)
        pair_sums[1].turn()
        parts[3].risen()
        parts[3].cross()

    events = {
        0: [(2, event_4)],
        2: [(1, event_2)],
        4: [(1, inner_sums[1].turn), (2, event_5)],
        8: [(0, event_1), (1, event_3), (2, event_6)],
    }
    third = HD ** (-0.5)
    lane = lax.broadcasted_iota(jnp.int32, (1, 128), 1)
    low = lane < HD
    steps = [(i, a) for i in range(blocks) for a in range(2)]

    def block(i):
        return slice(i * QB, (i + 1) * QB)

    def sub(a):
        return slice(a * HD, (a + 1) * HD)

    for item in later:
        item.wait()

    def heads(pair, _):
        for when, action in events[0]:
            pl.when(pair == when)(action)
        here = pl.ds(pl.multiple_of(pair * 128, 128), 128)

        def spot(t):
            return pl.ds(pl.multiple_of((3 * pair + t) * 128, 128), 128)

        scaled = (gm[:, here].astype(F32) * linv[:, here]).astype(BF16).astype(F32)
        kf, vf = k[:, here].astype(F32), v[:, here].astype(F32)
        weighted = scaled * o[:, here]
        for a in range(2):
            own = low if a == 0 else jnp.logical_not(low)
            delta = jnp.sum(jnp.where(own, weighted, 0.0), -1, keepdims=True)
            high = delta.astype(BF16).astype(F32)
            middle = (delta - high).astype(BF16).astype(F32)
            last = delta - high - middle
            base = HD * (1 - a)
            extra = jnp.where(
                lane == base,
                high,
                jnp.where(lane == base + 1, middle, jnp.where(lane == base + 2, last, 0.0)),
            )
            do[a] = jnp.where(own, scaled, -extra).astype(BF16)
            va[a] = jnp.where(own, vf, 1.0).astype(BF16)
            km[a] = jnp.where(own, kf, 0.0).astype(BF16)
        dot_[...] = scaled.astype(BF16).T
        qt[...] = q[:, here].T

        def pushed(t):
            i, a = steps[t]
            return nt(do[a, block(i), :], va[a])

        dqs = {}
        upcoming = jnp.minimum(pair + 1, pairs - 1)
        push = pushed(0)
        for t, (i, a) in enumerate(steps):
            for when, action in events.get(t, []) if t else []:
                pl.when(pair == when)(action)
            if a == 0:
                e_load(pair, i).wait()
            sl = block(i)
            p = ebuf[i, a]
            ds = (p.astype(F32) * push).astype(BF16)
            push = pushed(t + 1) if t + 1 < len(steps) else None
            dv = nn(dot_[sub(a), sl], p)
            dk = nn(qt[sub(a), sl], ds)
            dqs[a] = nn(ds, km[a])
            if i == 0:
                dvt[sub(a), :] = dv
                dkt[sub(a), :] = dk
            else:
                dvt[sub(a), :] += dv
                dkt[sub(a), :] += dk
            if a == 1:
                e_load(upcoming, i).start()
                grads[sl, spot(0)] = ((dqs[0] + dqs[1]) * third).astype(BF16)
        grads[:, spot(1)] = (dkt[...] * third).astype(BF16).T
        grads[:, spot(2)] = dvt[...].astype(BF16).T
        cols = pl.ds(pl.multiple_of(3 * pair * 128, 128), 3 * 128)
        part = tn(n1[...], grads[:, cols])
        for j in range(n_m):
            for b in range(2):
                at = (2 * j + b) * share
                qpart[pair, j, b] = part[at : at + share, :].astype(BF16)
        return 0

    lax.fori_loop(0, pairs, heads, 0)
    pair_sums[2].start()
    part_sum(1)
    parts[0].risen()
    parts[0].cross()
    for i in range(blocks):
        e_load(pairs - 1, i).wait()
    for i in range(seq):
        sl = slice(i * chunk, (i + 1) * chunk)
        gn1 = nt(grads[sl, :], wqkv[...])
        o[sl, :] = gn1[:, :mine]
        linv[sl, :] = gn1[:, mine:]
        gstage[i] = gn1.astype(BF16).reshape(2, half, width)
        g_copy(i).start()
    pair_sums[2].turn()
    inner[1].crossed()
    inner[1].fall()
    parts[1].risen()
    parts[1].cross()
    parts[3].crossed()
    parts[3].fall()
    vown[...] = jnp.zeros_like(vown)
    for p in range(pairs):
        cols = pl.ds(pl.multiple_of(c * mine + p * 128, 128), 128)
        for r, t in ((2, 0), (3, 2)):
            at = (3 * p + t) * 128
            vown[r : r + 1, cols] = jnp.sum(
                grads[:, at : at + 128].astype(F32), 0, keepdims=True
            )
    for n, r in enumerate((3, 1, 2, 0)):
        vown[4 + n : 5 + n, :] = 0.5 * gvec[r : r + 1, :]
    lines = hidden // width
    for n in range(lines):
        vown[pl.ds(8 + lines * c + n, 1), :] = gib[:, n * width : (n + 1) * width]
    gain = vecs[0:1, :]
    for i in range(seq):
        g_copy(i).wait_recv()
        sl = pl.ds(pl.multiple_of(i * chunk + c * half, 16), half)
        gn1 = jnp.concatenate([o[sl, :], linv[sl, :]], axis=1) + grecv[i].astype(F32)
        hat, inv = normalize(x[i].astype(F32))
        line = jnp.sum(gn1 * hat, 0, keepdims=True)
        flat = jnp.sum(gn1, 0, keepdims=True)
        if i == 0:
            gain_sum, shift_sum = line, flat
        else:
            gain_sum, shift_sum = gain_sum + line, shift_sum + flat
        ig_own[i] = (gres[i] + norm_back(gn1, gain, hat, inv)).astype(BF16)
        back.ships[i].start()
        if i == seq // 2:
            part_sum(2)
            parts[0].crossed()
            parts[0].fall()
    parts[2].risen()
    parts[2].cross()
    parts[1].crossed()
    parts[1].fall()
    vown[0:1, :] = gain_sum
    vown[1:2, :] = shift_sum
    vector_sum.start()
    total = vector_sum.total(vown[...])
    vector_sum.finish()
    vown[...] = total
    vectors.rise()
    parts[2].crossed()
    parts[2].fall()
    vectors.risen()
    vectors.cross()
    outer[0].fallen()
    outer[1].fallen()
    gwu_out[...] = uown[...]
    inner[0].fallen()
    crosses = {}

    def hand_over(n, src, dst):
        crosses[n] = pass_on(n, src, dst)
        crosses[n].start()

    for n in range(2):
        if n:
            inner[n].fallen()
        pl.when(c != n)(pass_on(n, ri.at[n], ito).start)
    parts[3].fallen()
    hand_over(5, ra.at[3, 1 - c], ato.at[3])
    parts[0].fallen()
    hand_over(2, ra.at[0, 1 - c], ato.at[0])
    vectors.crossed()
    vectors.fall()
    for n in range(2):
        pl.when(c == n)(pass_on(n, ri.at[1 - n], ito).wait_recv)
        pl.when(c != n)(pass_on(n, ri.at[n], ito).wait_send)
    if piece % 128:
        gwi_out[c] = ri[c]
        gwi_out[1 - c] = ito[...]
    else:
        for n in range(n_m):
            cols = slice(n * piece, (n + 1) * piece)
            here = pl.ds(pl.multiple_of((2 * n + c) * piece, 128), piece)
            there = pl.ds(pl.multiple_of((2 * n + 1 - c) * piece, 128), piece)
            gwi_out[:, here] = ri[c, :, cols]
            gwi_out[:, there] = ito[:, cols]
    for p in (1, 2):
        parts[p].fallen()
        hand_over(2 + p, ra.at[p, 1 - c], ato.at[p])
    here = pl.ds(pl.multiple_of(c * mine, 128), mine)
    there = pl.ds(pl.multiple_of((1 - c) * mine, 128), mine)
    crosses[5].wait()
    w_out[3, :, here] = ra[3, c]
    w_out[3, :, there] = ato[3]
    for p in range(pairs):
        crosses[2 + p].wait()
        here = pl.ds(pl.multiple_of(c * mine + p * 128, 128), 128)
        there = pl.ds(pl.multiple_of((1 - c) * mine + p * 128, 128), 128)
        for t in range(3):
            w_out[t, :, here] = ra[p, c, :, t * 128 : (t + 1) * 128]
            w_out[t, :, there] = ato[p, :, t * 128 : (t + 1) * 128]
    vectors.fallen()
    hand_over(6, vown, vto)
    crosses[6].wait()
    vto[...] = vown[...] + vto[...]
    turned = pltpu.roll(vto[0:8, :], (width - f * share) % width, 1)
    vec_out[...] = turned[:, :share]
    per = width // piece
    line = jnp.broadcast_to(vto[pl.ds(8 + lines * c + m // per, 1), :], (8, width))
    ib_out[...] = pltpu.roll(line, (width - (m % per) * piece) % width, 1)[0:1, :piece]
    for i in range(seq):
        g_copy(i).wait_send()
    for item in inner_sums + [out_sum] + pair_sums:
        item.finish()
    back.finish()


def back(gwi, gwo, ru, q, k, v, gm, o, linv, e, n1, x, gres, wqkv, vecs, gvec, gib):
    seq, _, half, width = x.shape
    n_m, _, share, hidden = gwi.shape
    rows, mine = q.shape
    pairs = mine // 128
    piece = hidden // n_m
    block = (2, share, mine)
    assert pairs == 3 and seq == 4

    def sems(*shape):
        return pltpu.SemaphoreType.DMA(shape)

    def two(*shape):
        return [sems(*shape), sems(*shape)]

    return pl.pallas_call(
        lambda *refs: back_kernel(seq, *refs),
        in_specs=[ANY] * 14 + [VMEM] * 3,
        out_specs=[VMEM] * 5 + [ANY],
        out_shape=[
            jax.ShapeDtypeStruct(ru.shape, BF16),
            jax.ShapeDtypeStruct((4, share, width), BF16),
            jax.ShapeDtypeStruct(
                (2, share, hidden) if piece % 128 else (share, 2 * hidden), BF16
            ),
            jax.ShapeDtypeStruct((8, share), F32),
            jax.ShapeDtypeStruct((1, piece), F32),
            jax.ShapeDtypeStruct((2, 2, half, width), BF16),
        ],
        scratch_shapes=[
            pltpu.VMEM((rows, mine), BF16),
            pltpu.VMEM((rows, mine), BF16),
            pltpu.VMEM((rows, mine), BF16),
            pltpu.VMEM((rows, mine), BF16),
            pltpu.VMEM((rows, mine), F32),
            pltpu.VMEM((rows, mine), F32),
            pltpu.VMEM(e.shape[1:], BF16),
            pltpu.VMEM((rows, width), BF16),
            pltpu.VMEM((seq, half, width), BF16),
            pltpu.VMEM((seq, half, width), F32),
            pltpu.VMEM(wqkv.shape, BF16),
            pltpu.VMEM((rows, 3 * mine), BF16),
            pltpu.VMEM((2, rows, 128), BF16),
            pltpu.VMEM((128, rows), BF16),
            pltpu.VMEM((128, rows), BF16),
            pltpu.VMEM((2, rows, 128), BF16),
            pltpu.VMEM((2, rows, 128), BF16),
            pltpu.VMEM((128, rows), F32),
            pltpu.VMEM((128, rows), F32),
            pltpu.VMEM(ru.shape, BF16),
            pltpu.VMEM((2,) + ru.shape, BF16),
            pltpu.VMEM((2, share, hidden), BF16),
            pltpu.VMEM((2, 2, share, hidden), BF16),
            pltpu.VMEM((2, n_m - 1, share, hidden), BF16),
            pltpu.VMEM((n_m - 1,) + block, BF16),
            pltpu.VMEM((4,) + block, BF16),
            pltpu.VMEM((4, 2) + block, BF16),
            pltpu.VMEM((share, hidden), BF16),
            pltpu.VMEM((4, share, mine), BF16),
            pltpu.VMEM((pairs, n_m) + block, BF16),
            pltpu.VMEM((pairs, n_m - 1) + block, BF16),
            pltpu.VMEM((seq, 2, half, width), BF16),
            pltpu.VMEM((seq, half, width), BF16),
            pltpu.VMEM((seq, half, width), BF16),
            pltpu.VMEM((16, width), F32),
            pltpu.VMEM((2, 16, width), F32),
            pltpu.VMEM((n_m - 1, 16, width), F32),
            pltpu.VMEM((16, width), F32),
        ]
        + two(2, max(n_m, 6))
        + two(max(n_m, 6))
        + two(pairs, max(n_m, 6))
        + two(n_m)
        + two(seq)
        + RETURN_SEMS(seq)
        + two(7)
        + [sems(2, 6), sems(2, 6), sems(4, 6), sems(6), sems(12), sems(rows // QB)]
        + [sems(pairs, 3), pltpu.VMEM(gwi.shape, BF16), pltpu.VMEM(gwo.shape, BF16)],
        compiler_params=pltpu.CompilerParams(
            collective_id=3, has_side_effects=True, vmem_limit_bytes=LIMIT
        ),
        name="back",
    )(gwi, gwo, ru, q, k, v, gm, o, linv, e, n1, x, gres, wqkv, vecs, gvec, gib)


def widen_kernel(w, gwi, gwu, vec, ib, *outs):
    for k in range(4):
        outs[k][...] = w[k].astype(F32)
    outs[4][...] = gwi[...].astype(F32)
    outs[5][...] = gwu[...].astype(F32)
    outs[6][...] = ib[...]
    for k in range(8):
        outs[7 + k][...] = vec[k : k + 1, :]


def widen(w, gwi, gwu, vec, ib):
    square = jax.ShapeDtypeStruct(w.shape[1:], F32)
    return pl.pallas_call(
        widen_kernel,
        in_specs=[VMEM] * 5,
        out_specs=[VMEM] * 15,
        out_shape=[square] * 4
        + [jax.ShapeDtypeStruct(value.shape, F32) for value in (gwi, gwu, ib)]
        + [jax.ShapeDtypeStruct((1, vec.shape[1]), F32)] * 8,
        compiler_params=pltpu.CompilerParams(vmem_limit_bytes=LIMIT),
        name="widen",
    )(w, gwi, gwu, vec, ib)


def per_device(
    frames,
    cotangent,
    valid_slots,
    first_gain,
    first_shift,
    query_weight,
    query_bias,
    key_weight,
    value_weight,
    value_bias,
    output_weight,
    output_bias,
    second_gain,
    second_shift,
    inner_weight,
    inner_bias,
    outer_weight,
    outer_bias,
):
    seq = lax.axis_size("seq")
    n_f = lax.axis_size("fsdp")
    f = lax.axis_index("fsdp")
    m, c = f // 2, f % 2
    slots, local, width = frames.shape
    chunk = -(-local // 128) * 128
    half = chunk // 2
    mine = width // 2
    share = width // n_f
    piece = inner_bias.shape[0]
    hidden = piece * n_f // 2

    keep = valid_slots.astype(BF16)[:, None, None]
    pad = ((0, 0), (0, chunk - local), (0, 0))
    x_send = jnp.pad(frames, pad).reshape(slots, 2, half, width)
    cot_send = jnp.pad(cotangent * keep, pad).reshape(slots, 2, half, width)
    vectors = (
        first_gain,
        first_shift,
        query_bias,
        value_bias,
        output_bias,
        second_gain,
        second_shift,
        outer_bias,
    )
    if share % 16 == 0 and piece % 128 == 0:
        rest = [query_weight, key_weight, value_weight, inner_weight]
        rest += [value[None] for value in vectors] + [inner_bias.astype(F32)[None]]
        *kept, wqkv, wi, vecs, ibias = front(
            x_send, cot_send, output_weight, outer_weight, rest, local, seq, True
        )
        wqkv = wqkv.reshape(width, 3 * mine)
        wi = wi.reshape(width, hidden)
    else:

        def gathered(value, axis=0):
            return lax.all_gather(value, "fsdp", axis=axis, tiled=True)

        def my_columns(value):
            return lax.dynamic_slice_in_dim(value, c * mine, mine, axis=1)

        wqkv = jnp.concatenate(
            [my_columns(gathered(w)) for w in (query_weight, key_weight, value_weight)], axis=1
        )
        wi = gathered(inner_weight).reshape(width, n_f // 2, 2, piece)
        wi = lax.dynamic_index_in_dim(wi, c, 2, keepdims=False).reshape(width, hidden)
        vecs = gathered(jnp.stack(vectors), 1).astype(F32)
        ibias = gathered(inner_bias).astype(F32).reshape(n_f // 2, 2, piece)
        ibias = lax.dynamic_index_in_dim(ibias, c, 1, keepdims=False).reshape(1, hidden)
        kept = front(
            x_send, cot_send, output_weight, outer_weight, [wqkv, vecs], local, seq, False
        )

    x, n1, q, k, v, e, o, linv, mixed, cot, wo, wu = kept
    if share % 16:
        wo = wo.transpose(1, 0, 2, 3).reshape(width, width)
    out_back, gres, gm, gwo, gwi, ru, gvec, gib = dense(x, mixed, cot, wo, wi, wu, vecs, ibias)
    gwu, w, gwi, vec, ib, ig_back = back(
        gwi, gwo, ru, q, k, v, gm, o, linv, e, n1, x, gres, wqkv, vecs, gvec, gib
    )
    if gwi.ndim == 3:
        gwi = gwi.reshape(2, share, n_f // 2, piece).transpose(1, 2, 0, 3)
        gwi = gwi.reshape(share, 2 * hidden)
    gwq, gwk, gwv, gwo, gwi, gwu, ib, fg, fs, qb, vb, ob, sg, ss, ub = widen(
        w, gwi, gwu.reshape(piece, width), vec, ib
    )
    keep32 = valid_slots.astype(F32)[:, None, None]
    outputs = (out_back.reshape(slots, chunk, width)[:, :local].astype(F32) * keep32).astype(BF16)
    input_grad = ig_back.reshape(slots, chunk, width)[:, :local]
    return (
        outputs,
        input_grad,
        fg[0],
        fs[0],
        gwq,
        qb[0],
        gwk,
        gwv,
        vb[0],
        gwo,
        ob[0],
        sg[0],
        ss[0],
        gwi,
        ib.reshape(piece),
        gwu,
        ub[0],
    )


def solution(mesh):
    rows = P("fsdp", "seq", None)
    vector, matrix = P("fsdp"), P("fsdp", None)
    weights = (
        vector,
        vector,
        matrix,
        vector,
        matrix,
        matrix,
        vector,
        matrix,
        vector,
        vector,
        vector,
        matrix,
        vector,
        matrix,
        vector,
    )
    return jax.shard_map(
        per_device,
        mesh=mesh,
        in_specs=(rows, rows, vector) + weights,
        out_specs=(rows, rows) + weights,
        check_vma=False,
    )
```

```python
import math

import jax
import jax.numpy as jnp
from jax import lax
from jax.experimental import pallas as pl
from jax.experimental.pallas import tpu as pltpu
from jax.sharding import PartitionSpec as P

H = 12
HD = 64
EPS = 1e-05
MESH = pl.DeviceIdType.MESH
F32 = jnp.float32
BF16 = jnp.bfloat16
ANY = pl.BlockSpec(memory_space=pl.ANY)
VMEM = pl.BlockSpec(memory_space=pltpu.VMEM)
LIMIT = 62 << 20
QB = 256


def nn(a, b):
    return lax.dot_general(a, b, (((1,), (0,)), ((), ())), preferred_element_type=F32)


def nt(a, b):
    return lax.dot_general(a, b, (((1,), (1,)), ((), ())), preferred_element_type=F32)


def tn(a, b):
    return lax.dot_general(a, b, (((0,), (0,)), ((), ())), preferred_element_type=F32)


def normalize(rows):
    center = rows - jnp.mean(rows, -1, keepdims=True)
    inv = lax.rsqrt(jnp.mean(center * center, -1, keepdims=True) + EPS)
    return center * inv, inv


def norm_back(grad, gain, hat, inv):
    tilted = grad * gain
    first = jnp.mean(tilted, -1, keepdims=True)
    cross = jnp.mean(tilted * hat, -1, keepdims=True)
    return inv * (tilted - first - hat * cross)


def where_am_i():
    f = lax.axis_index("fsdp")
    z = lax.axis_index("seq")
    return f, z, f // 2, f % 2


def meet(peers):
    barrier = pltpu.get_barrier_semaphore()
    for peer in peers:
        pl.semaphore_signal(barrier, inc=1, device_id=peer, device_id_type=MESH)
    pl.semaphore_wait(barrier, len(peers))


def column_peers(seq):
    f, z, m, c = where_am_i()
    peers = []
    for dc in range(2):
        for dz in range(seq):
            if dc or dz:
                peers.append((m * 2 + (c + dc) % 2, (z + dz) % seq))
    return peers


class Ship:
    def __init__(self, src, dst, send, recv, target):
        f, z, _, _ = where_am_i()
        self.here = jnp.logical_and(target[0] == f, target[1] == z)
        self.local = pltpu.make_async_copy(src, dst, recv)
        self.remote = pltpu.make_async_remote_copy(
            src, dst, send, recv, device_id=target, device_id_type=MESH
        )

    def start(self):
        pl.when(self.here)(self.local.start)
        pl.when(jnp.logical_not(self.here))(self.remote.start)

    def wait_send(self):
        pl.when(jnp.logical_not(self.here))(self.remote.wait_send)


def remote(src, dst, send, recv, target):
    return pltpu.make_async_remote_copy(
        src, dst, send, recv, device_id=target, device_id_type=MESH
    )


class Gather:
    def __init__(self, send_ref, full_ref, send_sem, recv_sem, pass_send, pass_recv, seq):
        f, z, m, c = where_am_i()
        self.ships = []
        for i in range(2):
            for h in range(2):
                slot = 2 * c + i
                self.ships.append(
                    Ship(
                        send_ref.at[i, h],
                        full_ref.at[z, h],
                        send_sem.at[i, h],
                        recv_sem.at[z],
                        (m * 2 + h, slot),
                    )
                )
        other = (m * 2 + 1 - c, z)
        chips = [(z + d) % seq for d in range(seq)]
        self.arrivals = [
            remote(send_ref.at[0, 0], full_ref.at[k, c], send_sem.at[0, 0], recv_sem.at[k], other)
            for k in chips
        ]
        self.passes = [
            remote(full_ref.at[k, c], full_ref.at[k, c], pass_send.at[d], pass_recv.at[d], other)
            for d, k in enumerate(chips)
        ]
        self.handed = [
            remote(
                full_ref.at[k, c], full_ref.at[k, 1 - c], pass_send.at[d], pass_recv.at[d], other
            )
            for d, k in enumerate(chips)
        ]

    def start(self):
        for ship in self.ships:
            ship.start()

    def arrived(self):
        for item in self.arrivals:
            item.wait_recv()
        for ship in self.ships:
            ship.wait_send()

    def hand_on(self, k):
        self.arrivals[k].wait_recv()
        self.passes[k].start()

    def ready(self, k):
        self.handed[k].wait_recv()

    def finish(self):
        for ship in self.ships:
            ship.wait_send()
        for item in self.passes:
            item.wait_send()


GATHER_SEMS = lambda seq: [
    pltpu.SemaphoreType.DMA((2, 2)),
    pltpu.SemaphoreType.DMA((seq,)),
    pltpu.SemaphoreType.DMA((seq,)),
    pltpu.SemaphoreType.DMA((seq,)),
]


class Return:
    def __init__(self, own_ref, back_ref, send_sem, recv_sem, seq):
        f, z, m, c = where_am_i()
        home = z // 2
        self.ships = [
            Ship(
                own_ref.at[k],
                back_ref.at[z % 2, c],
                send_sem.at[k],
                recv_sem.at[z % 2, c],
                (m * 2 + home, k),
            )
            for k in range(seq)
        ]
        self.arrivals = [
            remote(
                own_ref.at[0],
                back_ref.at[i, h],
                send_sem.at[0],
                recv_sem.at[i, h],
                (m * 2 + 1 - c, z),
            )
            for i in range(2)
            for h in range(2)
        ]

    def start(self):
        for ship in self.ships:
            ship.start()

    def finish(self):
        for ship in self.ships:
            ship.wait_send()
        for item in self.arrivals:
            item.wait_recv()


RETURN_SEMS = lambda seq: [pltpu.SemaphoreType.DMA((seq,)), pltpu.SemaphoreType.DMA((2, 2))]


class Spread:
    def __init__(self, source, full_ref, send_sem, recv_sem, local_sem, stride):
        f, z, m, c = where_am_i()
        n_f = lax.axis_size("fsdp")
        steps = n_f // stride
        slot = f if stride == 1 else m
        self.local = pltpu.make_async_copy(source(f), full_ref.at[slot], local_sem)
        self.sends = []
        self.arrivals = []
        for d in range(1, steps):
            to = (f + d * stride) % n_f
            back = (f + n_f - d * stride) % n_f
            self.sends.append(
                remote(source(to), full_ref.at[slot], send_sem.at[d], recv_sem.at[d], (to, z))
            )
            place = back if stride == 1 else back // 2
            self.arrivals.append(
                remote(source(f), full_ref.at[place], send_sem.at[d], recv_sem.at[d], (to, z))
            )

    def start(self):
        self.local.start()
        for item in self.sends:
            item.start()

    def relay(self):
        pass

    def ready(self):
        self.local.wait()
        for item in self.arrivals:
            item.wait_recv()

    def finish(self):
        for item in self.sends:
            item.wait_send()


def square_chips():
    _, _, m, _ = where_am_i()
    x, y = m % 2, m // 2
    return y * 2 + 1 - x, (1 - y) * 2 + x, (1 - y) * 2 + 1 - x


class Near:
    def __init__(self, source, full_ref, send_sem, recv_sem, local_sem, stride):
        f, z, m, c = where_am_i()
        beside, above, _ = square_chips()

        def slot(chip, core):
            return chip * 2 + core if stride == 1 else chip

        mine = full_ref.at[slot(m, c)]
        self.local = pltpu.make_async_copy(source(f), mine, local_sem)
        self.sends, self.arrivals = [], []
        k = 0
        for dc in range(2 // stride):
            core = (c + dc) % 2
            for chip in [beside, above] + ([m] if dc else []):
                to = (chip * 2 + core, z)
                src = source(chip * 2 + core)
                theirs = full_ref.at[slot(chip, core)]
                self.sends.append(remote(src, mine, send_sem.at[k], recv_sem.at[k], to))
                self.arrivals.append(remote(src, theirs, send_sem.at[k], recv_sem.at[k], to))
                k += 1

    def start(self):
        self.local.start()
        for item in self.sends:
            item.start()

    def ready(self):
        self.local.wait()
        for item in self.arrivals:
            item.wait_recv()

    def finish(self):
        for item in self.sends:
            item.wait_send()


class Far:
    def __init__(self, have_ref, full_ref, send_sem, recv_sem, stride):
        f, z, m, c = where_am_i()
        beside, above, far = square_chips()

        def slot(chip, core):
            return chip * 2 + core if stride == 1 else chip

        rows = full_ref.shape[1] // 2
        halves = [pl.ds(0, rows), pl.ds(rows, rows)]
        self.sends, self.arrivals = [], []
        k = 5
        for dc in range(2 // stride):
            core = (c + dc) % 2
            for chip, onto, part in ((beside, above, halves[0]), (above, beside, halves[1])):
                to = (onto * 2 + c, z)
                src = have_ref.at[slot(chip, core), part]
                dst = full_ref.at[slot(chip, core), part]
                lands = full_ref.at[slot(far, core), part]
                self.sends.append(remote(src, dst, send_sem.at[k], recv_sem.at[k], to))
                self.arrivals.append(remote(src, lands, send_sem.at[k], recv_sem.at[k], to))
                k += 1

    def start(self):
        for item in self.sends:
            item.start()

    def ready(self):
        for item in self.arrivals:
            item.wait_recv()

    def finish(self):
        for item in self.sends:
            item.wait_send()


class Relay:
    def __init__(self, source, full_ref, send_sem, recv_sem, local_sem, stride):
        self.near = Near(source, full_ref, send_sem, recv_sem, local_sem, stride)
        self.far = Far(full_ref, full_ref, send_sem, recv_sem, stride)

    def start(self):
        self.near.start()

    def relay(self):
        self.near.ready()
        self.far.start()

    def ready(self):
        self.far.ready()

    def finish(self):
        self.near.finish()
        self.far.finish()


def squared():
    return lax.axis_size("fsdp") == 8


def spreading(source, full_ref, sems, stride):
    kind = Relay if squared() else Spread
    return kind(source, full_ref, *sems, stride)


def spread_sems(steps):
    steps = max(steps, 9)
    return [
        pltpu.SemaphoreType.DMA((steps,)),
        pltpu.SemaphoreType.DMA((steps,)),
        pltpu.SemaphoreType.DMA,
    ]


def fsdp_peers():
    f, z, _, _ = where_am_i()
    n_f = lax.axis_size("fsdp")
    return [((f + d) % n_f, z) for d in range(1, n_f)]


def all_peers(seq):
    f, z, m, c = where_am_i()
    other = m * 2 + 1 - c
    peers = fsdp_peers()
    for d in range(1, seq):
        peers.append((f, (z + d) % seq))
        peers.append((other, (z + d) % seq))
    return peers


class Scatter:
    def __init__(self, part, got_ref, send_sem, recv_sem):
        f, z, m, c = where_am_i()
        n_m = lax.axis_size("fsdp") // 2
        self.part, self.got, self.chip = part, got_ref, m
        self.copies = []
        for d in range(1, n_m):
            to = (m + d) % n_m
            self.copies.append(
                remote(
                    part(to),
                    got_ref.at[d - 1],
                    send_sem.at[d],
                    recv_sem.at[d],
                    (to * 2 + c, z),
                )
            )

    def start(self):
        for item in self.copies:
            item.start()

    def turn(self):
        pass

    def total(self, own):
        for item in self.copies:
            item.wait_recv()
        result = own.astype(F32)
        for k in range(len(self.copies)):
            result = result + self.got[k].astype(F32)
        return result

    def finish(self):
        for item in self.copies:
            item.wait_send()


class Fold:
    def __init__(self, part, got_ref, send_sem, recv_sem):
        f, z, m, c = where_am_i()
        beside, above, far = square_chips()
        self.chips = (beside, above, far)
        count = got_ref.shape[1] // 2

        def half(ref, n):
            return ref.at[pl.ds(n * count, count)]

        def sent(n, src, dst, chip):
            return remote(src, dst, send_sem.at[n], recv_sem.at[n], (chip * 2 + c, z))

        self.got = got_ref
        passing = [half(got_ref.at[2], 0), half(got_ref.at[2], 1)]
        adding = [half(part(beside), 0), half(part(above), 1)]
        self.joins = list(zip(passing, adding))
        self.copies = [
            sent(0, half(part(far), 0), passing[0], above),
            sent(1, half(part(far), 1), passing[1], beside),
            sent(2, half(part(beside), 1), half(got_ref.at[0], 1), beside),
            sent(3, half(part(above), 0), half(got_ref.at[1], 0), above),
            sent(4, passing[0], half(got_ref.at[0], 0), beside),
            sent(5, passing[1], half(got_ref.at[1], 1), above),
        ]

    def start(self):
        for item in self.copies[:4]:
            item.start()

    def turn(self):
        for n in range(2):
            passing, adding = self.joins[n]
            self.copies[n].wait_recv()
            joined = passing[...].astype(F32) + adding[...].astype(F32)
            passing[...] = joined.astype(passing.dtype)
            self.copies[4 + n].start()

    def total(self, own):
        for item in self.copies[2:]:
            item.wait_recv()
        return own.astype(F32) + self.got[0].astype(F32) + self.got[1].astype(F32)

    def finish(self):
        for item in self.copies:
            item.wait_send()


def folding(*args):
    return (Fold if squared() else Scatter)(*args)


def scatter_sems():
    n_m = lax.axis_size("fsdp") // 2
    return [pltpu.SemaphoreType.DMA((max(n_m, 6),)), pltpu.SemaphoreType.DMA((max(n_m, 6),))]


class Across:
    def __init__(self, own_ref, spare_ref, sems):
        f, z, _, _ = where_am_i()
        self.own, self.spare = own_ref, spare_ref
        self.edge = jnp.logical_or(z == 0, z == 3)
        self.inner = jnp.logical_not(self.edge)
        beside = jnp.where(z < 2, 1 - z, 5 - z)
        self.up = remote(own_ref, spare_ref.at[0], sems.at[0], sems.at[1], (f, beside))
        self.swap = remote(own_ref, spare_ref.at[1], sems.at[2], sems.at[3], (f, 3 - z))
        self.down = remote(own_ref, spare_ref.at[1], sems.at[4], sems.at[5], (f, beside))

    def add(self, k):
        total = self.own[...].astype(F32) + self.spare[k].astype(F32)
        self.own[...] = total.astype(self.own.dtype)

    def rise(self):
        pl.when(self.edge)(self.up.start)

    def risen(self):
        @pl.when(self.inner)
        def _():
            self.up.wait_recv()
            self.add(0)

        pl.when(self.edge)(self.up.wait_send)

    def cross(self):
        pl.when(self.inner)(self.swap.start)

    def crossed(self):
        @pl.when(self.inner)
        def _():
            self.swap.wait()
            self.add(1)

    def fall(self):
        pl.when(self.inner)(self.down.start)

    def fallen(self):
        @pl.when(self.edge)
        def _():
            self.down.wait_recv()
            self.own[...] = self.spare[1]

        pl.when(self.inner)(self.down.wait_send)


ACROSS_SEMS = pltpu.SemaphoreType.DMA((6,))


def front_kernel(seq, local, gathers, *refs):
    refs = list(refs)

    def take(n):
        got = refs[:n]
        del refs[:n]
        return got

    x_send, cot_send, wo_send, wu_send = take(4)
    if gathers:
        squares, wi = take(3), take(1)[0]
        given = take(9)
    else:
        wqkv, vecs_out = take(2)
    x_full, n1_out, q_out, k_out, v_out, e_out, o_out, linv_out = take(8)
    mixed_out, cot_full, wo_out, wu_out = take(4)
    if gathers:
        wqkv_out, wi_out, vecs_out, ibias_out = take(4)
    xsems, csems, osems, usems = take(4), take(4), take(3), take(3)
    xv, stage, qa, ka, va, ebuf, lsem, esem, nsem, msend, mrecv, mlocal, nbuf = take(13)
    q, k, v, obuf, lbuf, qkv_sem, osem = take(7)
    psems = take(2)
    if gathers:
        wqkv, wqkv_send, wi_send, small, smalls, wsem, tsem = take(7)
        qsems, isems, vsems = take(3), take(3), take(3)
    f, z, m, c = where_am_i()
    n_f = lax.axis_size("fsdp")
    half = xv.shape[2]
    chunk = 2 * half
    rows, mine = q.shape
    width = xv.shape[3]
    pairs = mine // 128
    other = (m * 2 + 1 - c, z)
    if gathers:
        share = given[0].shape[1]
        piece = given[8].shape[1]
        sorts = []
        for b in range(2):
            for t, ref in enumerate(squares):
                sorts.append(
                    (ref.at[:, pl.ds(b * mine, mine)], wqkv_send.at[b, :, pl.ds(t * mine, mine)])
                )
        for b in range(2):
            for t in range(n_f // 2):
                cols = pl.ds((2 * t + b) * piece, piece)
                sorts.append((wi.at[:, cols], wi_send.at[b, :, pl.ds(t * piece, piece)]))
        sorts = [
            pltpu.make_async_copy(src, dst, tsem.at[n]) for n, (src, dst) in enumerate(sorts)
        ]
        for item in sorts:
            item.start()
        small[...] = jnp.zeros_like(small)
        for r in range(8):
            small[r : r + 1, :share] = given[r][...].astype(F32)
        small[8:9, :piece] = given[8][...].astype(F32)
        vectors = Spread(lambda to: small, smalls, *vsems, 1)
        attn = spreading(lambda to: wqkv_send.at[to % 2], wqkv, qsems, 1)
        feed = spreading(lambda to: wi_send.at[to % 2], wi_out, isems, 1)
    meet(all_peers(seq))
    gather = Gather(x_send, xv, *xsems, seq)
    gather_cot = Gather(cot_send, cot_full, *csems, seq)
    out = spreading(lambda to: wo_send, wo_out.at[c], osems, 2)
    out_pass = remote(wo_out.at[c], wo_out.at[c], psems[0], psems[1], other)
    out_got = remote(wo_out.at[c], wo_out.at[1 - c], psems[0], psems[1], other)
    outer = (Near if squared() else Spread)(lambda to: wu_send, wu_out, *usems, 2)
    if gathers:
        gather.start()
        vectors.start()
        for item in sorts:
            item.wait()
        attn.start()
        vectors.ready()
        row = lax.broadcasted_iota(jnp.int32, (128, width), 0)
        col = lax.broadcasted_iota(jnp.int32, (128, width), 1)
        vecs = jnp.zeros((16, width), F32)
        for n in range(n_f):
            spot = jnp.logical_and(col - n * share == row, row < share)
            vecs = vecs + nn(
                smalls[n, :, :128].astype(BF16), jnp.where(spot, 1.0, 0.0).astype(BF16)
            )
        vecs_out[...] = vecs[:8]
        for n in range(n_f // 2):
            ibias_out[0:1, n * piece : (n + 1) * piece] = smalls[2 * n + c, 8:9, :piece]
        attn.relay()
        out.start()
        feed.start()
        attn.ready()
        keep_weights = pltpu.make_async_copy(wqkv, wqkv_out, wsem)
        keep_weights.start()
    else:
        gather.start()
        out.start()
    gain = vecs_out[0:1, :]
    shift = vecs_out[1:2, :]
    cols = pl.ds(pl.multiple_of(c * mine, 128), mine)
    qb = vecs_out[2:3, cols]
    vb = vecs_out[3:4, cols]
    keeps = []
    for n, d in enumerate(sorted(range(seq), key=lambda d: min(d, seq - d))):
        at = (z + d) % seq
        gather.hand_on(d)
        if n == seq - 1:
            gather_cot.start()
        gather.ready(d)
        sl = pl.ds(pl.multiple_of(at * chunk, 16), chunk)
        hat, _ = normalize(xv[at].reshape(chunk, width).astype(F32))
        normed = (hat * gain + shift).astype(BF16)
        nbuf[sl, :] = normed
        keeps.append(pltpu.make_async_copy(xv.at[at], x_full.at[at], lsem.at[d]))
        keeps.append(pltpu.make_async_copy(nbuf.at[sl], n1_out.at[sl], nsem.at[d]))
        for item in keeps[-2:]:
            item.start()
        qkv = nn(normed, wqkv[...].reshape(width, 3 * mine))
        q[sl, :] = (qkv[:, :mine] + qb).astype(BF16)
        k[sl, :] = qkv[:, mine : 2 * mine].astype(BF16)
        v[sl, :] = (qkv[:, 2 * mine :] + vb).astype(BF16)
    for n, (src, dst) in enumerate(((q, q_out), (k, k_out), (v, v_out))):
        keeps.append(pltpu.make_async_copy(src, dst, qkv_sem.at[n]))
        keeps[-1].start()
    lane = lax.broadcasted_iota(jnp.int32, (1, 128), 1)
    low = lane < HD
    factor = HD ** (-0.5) * math.log2(math.e)
    steps = [(i, a) for i in range(rows // QB) for a in range(2)]

    def block(i):
        return slice(i * QB, (i + 1) * QB)

    def e_copy(p, i):
        return pltpu.make_async_copy(
            ebuf.at[p % 2, i], e_out.at[p, i], esem.at[p % 2, i]
        )

    def o_copies(p):
        cols = pl.ds(pl.multiple_of(p * 128, 128), 128)
        return (
            pltpu.make_async_copy(obuf.at[p], o_out.at[:, cols], osem.at[0, p]),
            pltpu.make_async_copy(lbuf.at[p], linv_out.at[:, cols], osem.at[1, p]),
        )

    def mixed_copies(p):
        return (
            pltpu.make_async_copy(stage.at[p], mixed_out.at[c, p], mlocal.at[p]),
            remote(stage.at[p], mixed_out.at[c, p], msend.at[p], mrecv.at[p], other),
            remote(stage.at[p], mixed_out.at[1 - c, p], msend.at[p], mrecv.at[p], other),
        )

    def heads(pair, _):
        @pl.when(pair == 0)
        def _():
            out.relay()
            if gathers:
                feed.relay()
            outer.start()

        @pl.when(pair == 1)
        def _():
            out.ready()
            out_pass.start()


        @pl.when(pair >= 2)
        def _():
            for i in range(rows // QB):
                e_copy(pair - 2, i).wait()

        here = pl.ds(pl.multiple_of(pair * 128, 128), 128)
        place = lax.broadcasted_iota(jnp.int32, (rows, 1), 0) % (rows // seq)
        bar = jnp.where(place < local, 0.0, -1e38).astype(F32)
        qf, kf, vf = q[:, here].astype(F32), k[:, here].astype(F32), v[:, here].astype(F32)
        for a in range(2):
            own = low if a == 0 else jnp.logical_not(low)
            first = lane == HD * (1 - a)
            qa[a] = jnp.where(own, qf, jnp.where(first, 1.0, 0.0)).astype(BF16)
            ka[a] = jnp.where(own, kf, jnp.where(first, bar, 0.0)).astype(BF16)
            va[a] = jnp.where(own, vf, 1.0).astype(BF16)

        def scored(t):
            i, a = steps[t]
            return nt(qa[a, block(i), :], ka[a])

        raws = {}

        def finish(t, expo):
            i, a = steps[t]
            raws[a] = nn(expo, va[a])
            if a == 1:
                sl = block(i)
                total = pltpu.roll(jnp.where(low, raws[1], raws[0]), HD, 1)
                inv = 1.0 / total
                res = jnp.where(low, raws[0], raws[1]) * inv
                obuf[pair, sl, :] = res
                lbuf[pair, sl, :] = inv
                stage[pair, sl, :] = res.astype(BF16)

        scores, before = scored(0), None
        for t, (i, a) in enumerate(steps):
            peak = jnp.max(scores, -1, keepdims=True)
            upcoming = scored(t + 1) if t + 1 < len(steps) else None
            if before is not None:
                finish(t - 1, before)
            expo = jnp.exp2((scores - peak) * factor).astype(BF16)
            ebuf[pair % 2, i, a] = expo
            if a == 1:
                e_copy(pair, i).start()
            scores, before = upcoming, expo
        finish(len(steps) - 1, before)
        for item in o_copies(pair):
            item.start()
        to_self, to_other, _ = mixed_copies(pair)
        to_self.start()
        to_other.start()
        return 0

    lax.fori_loop(0, pairs, heads, 0)
    for item in keeps:
        item.wait()
    gather.finish()
    if gathers:
        keep_weights.wait()
        vectors.finish()
        attn.finish()
        feed.ready()
        feed.finish()
    out.finish()
    out_pass.wait_send()
    out_got.wait_recv()
    outer.ready()
    outer.finish()
    for p in range(pairs):
        to_self, to_other, back = mixed_copies(p)
        to_self.wait()
        to_other.wait_send()
        back.wait_recv()
        for item in o_copies(p):
            item.wait()
    for p in range(max(0, pairs - 2), pairs):
        for i in range(rows // QB):
            e_copy(p, i).wait()
    gather_cot.arrived()


def front(x_send, cot_send, wo_send, wu_send, rest, local, seq, gathers):
    _, _, half, width = x_send.shape
    n_f = lax.axis_size("fsdp")
    rows = seq * 2 * half
    share = wo_send.shape[0]
    mine = width // 2
    pairs = mine // 128
    frames = jax.ShapeDtypeStruct((seq, 2, half, width), BF16)
    heads = jax.ShapeDtypeStruct((rows, mine), BF16)
    wide = jax.ShapeDtypeStruct((rows, mine), F32)
    out_specs = [ANY] * 12
    out_shape = [
        frames,
        jax.ShapeDtypeStruct((rows, width), BF16),
        heads,
        heads,
        heads,
        jax.ShapeDtypeStruct((pairs, rows // QB, 2, QB, rows), BF16),
        wide,
        wide,
        jax.ShapeDtypeStruct((2, pairs, rows, 128), BF16),
        frames,
        jax.ShapeDtypeStruct((2, n_f // 2) + wo_send.shape, BF16),
        jax.ShapeDtypeStruct((n_f // 2,) + wu_send.shape, BF16),
    ]
    scratch = (
        GATHER_SEMS(seq)
        + GATHER_SEMS(seq)
        + spread_sems(n_f)
        + spread_sems(n_f // 2)
        + [
            pltpu.VMEM((seq, 2, half, width), BF16),
            pltpu.VMEM((pairs, rows, 128), BF16),
            pltpu.VMEM((2, rows, 128), BF16),
            pltpu.VMEM((2, rows, 128), BF16),
            pltpu.VMEM((2, rows, 128), BF16),
            pltpu.VMEM((2, rows // QB, 2, QB, rows), BF16),
            pltpu.SemaphoreType.DMA((seq,)),
            pltpu.SemaphoreType.DMA((2, rows // QB)),
            pltpu.SemaphoreType.DMA((seq,)),
            pltpu.SemaphoreType.DMA((pairs,)),
            pltpu.SemaphoreType.DMA((pairs,)),
            pltpu.SemaphoreType.DMA((pairs,)),
            pltpu.VMEM((rows, width), BF16),
            pltpu.VMEM((rows, mine), BF16),
            pltpu.VMEM((rows, mine), BF16),
            pltpu.VMEM((rows, mine), BF16),
            pltpu.VMEM((pairs, rows, 128), F32),
            pltpu.VMEM((pairs, rows, 128), F32),
            pltpu.SemaphoreType.DMA((3,)),
            pltpu.SemaphoreType.DMA((2, pairs)),
            pltpu.SemaphoreType.DMA,
            pltpu.SemaphoreType.DMA,
        ]
    )
    in_specs = [ANY] * 4 + [VMEM] * 2
    if gathers:
        piece = rest[-1].shape[1]
        hidden = rest[3].shape[1] // 2
        lanes = max(128, piece)
        in_specs = [ANY] * 8 + [VMEM] * 9
        out_specs += [ANY, ANY, VMEM, VMEM]
        out_shape += [
            jax.ShapeDtypeStruct((n_f, share, 3 * mine), BF16),
            jax.ShapeDtypeStruct((n_f, share, hidden), BF16),
            jax.ShapeDtypeStruct((8, width), F32),
            jax.ShapeDtypeStruct((1, hidden), F32),
        ]
        scratch += [
            pltpu.VMEM((n_f, share, 3 * mine), BF16),
            pltpu.VMEM((2, share, 3 * mine), BF16),
            pltpu.VMEM((2, share, hidden), BF16),
            pltpu.VMEM((16, lanes), F32),
            pltpu.VMEM((n_f, 16, lanes), F32),
            pltpu.SemaphoreType.DMA,
            pltpu.SemaphoreType.DMA((6 + n_f,)),
        ]
        scratch += spread_sems(n_f) + spread_sems(n_f) + spread_sems(n_f)
    return pl.pallas_call(
        lambda *refs: front_kernel(seq, local, gathers, *refs),
        in_specs=in_specs,
        out_specs=out_specs,
        out_shape=out_shape,
        scratch_shapes=scratch,
        compiler_params=pltpu.CompilerParams(
            collective_id=0, has_side_effects=True, vmem_limit_bytes=LIMIT
        ),
        name="front",
    )(x_send, cot_send, wo_send, wu_send, *rest)


def inverse(y):
    guess = pl.reciprocal(y, approx=True)
    return guess * (2.0 - y * guess)


def gelu_parts(u):
    t = inverse(1.0 + (0.3275911 / math.sqrt(2.0)) * jnp.abs(u))
    poly = t * (
        0.127414796
        + t * (-0.142248368 + t * (0.7107068705 + t * (-0.7265760135 + t * 0.5307027145)))
    )
    expo = jnp.exp2((u * u) * (-0.5 * math.log2(math.e)))
    tail = poly * expo
    phi = jnp.where(u >= 0, 1.0 - tail, tail)
    return phi, u * expo * (1.0 / math.sqrt(2.0 * math.pi))


def dense_kernel(
    seq, x, mixed_in, cot_in, wo_in, wi_in, wu_in, vecs, ibias,
    out_back, gres_own, gm_out, gwo_out, gwi_out, ru_out, gvec_out, gib_out,
    xv, mixed, cot, wo, wi, wu, n2, hat2, inv2, resid, active, slope, out_own,
    pstage, precv, grecv, ugot, upart,
    psem, prsem, gsem, grsem, bsend, brecv, usend, urecv, lsem, xsem, csend, crecv, fsend, frecv, osem,
):
    f, z, m, c = where_am_i()
    other = (m * 2 + 1 - c, z)
    half = x.shape[2]
    chunk = 2 * half
    width = x.shape[3]
    mine = gm_out.shape[1]
    hidden = wi.shape[1]
    n_m = gwi_out.shape[0]
    share = gwi_out.shape[2]
    piece = upart.shape[1]
    rows = seq * chunk
    tile = 512

    def block(i):
        return pl.ds(i * chunk, chunk)

    def fetch_x(i):
        return pltpu.make_async_copy(x.at[i], xv.at[i % 2], xsem.at[i % 2])

    def load(k, src, dst):
        return pltpu.make_async_copy(src, dst, lsem.at[k])

    loads = [load(0, mixed_in, mixed), load(2, wi_in, wi)]
    if len(wo_in.shape) == 2:
        loads.append(load(1, wo_in, wo))
    else:
        for a in range(2):
            for chip in range(n_m):
                at = pl.ds((2 * chip + a) * share, share)
                loads.append(
                    pltpu.make_async_copy(wo_in.at[a, chip], wo.at[at], osem.at[a, chip])
                )
    late = [load(3 + k, cot_in.at[k, c], cot.at[k, c]) for k in range(seq)]
    if squared():
        beside, above, _ = square_chips()
        late += [
            load(3 + seq + k, wu_in.at[chip], wu.at[chip])
            for k, chip in enumerate((m, beside, above))
        ]
    else:
        late.append(load(3 + seq, wu_in, wu))
    fetch_x(0).start()
    for item in loads + late:
        item.start()
    meet(all_peers(seq))
    if squared():
        tail = Far(wu_in, wu, fsend, frecv, 2)
        tail.start()
    passes = [
        remote(cot_in.at[k, c], cot.at[k, c], csend.at[k], crecv.at[k], other) for k in range(seq)
    ]
    handed = [
        remote(cot_in.at[k, c], cot.at[k, 1 - c], csend.at[k], crecv.at[k], other)
        for k in range(seq)
    ]
    for item in passes:
        item.start()
    obias, gain, shift, ubias = vecs[4:5, :], vecs[5:6, :], vecs[6:7, :], vecs[7:8, :]
    back = Return(out_own, out_back, bsend, brecv, seq)
    gstage = active.at[:, :width]
    branch = active.at[:, width : 2 * width]
    gown = resid

    def p_copy(i):
        return remote(pstage.at[i, 1 - c], precv.at[i], psem.at[i], prsem.at[i], other)

    def g_copy(i):
        return remote(gstage.at[block(i)], grecv.at[block(i)], gsem.at[i], grsem.at[i], other)

    def mixed_rows(sl):
        return jnp.concatenate(
            [mixed[a, p, sl, :] for a in range(2) for p in range(mixed.shape[1])], axis=1
        )

    def push(i):
        sl = block(i)
        pout = nn(active[sl, :], wu[...].reshape(hidden, width))
        resid[sl, :] += pout
        pstage[i] = pout.astype(BF16).reshape(2, half, width)
        p_copy(i).start()

    for item in loads:
        item.wait()
    for i in range(seq):
        sl = block(i)
        fetch_x(i).wait()
        if i + 1 < seq:
            fetch_x(i + 1).start()
        frames = xv[i % 2].reshape(chunk, width).astype(F32)
        res = frames + nn(mixed_rows(sl), wo[...]) + obias
        hat, inv = normalize(res)
        normed = (hat * gain + shift).astype(BF16)
        resid[sl, :] = res + ubias
        n2[sl, :] = normed
        hat2[sl, :] = hat
        inv2[sl, :] = jnp.broadcast_to(inv, (chunk, 128))
        for j in range(0, hidden, tile):
            cols = slice(j, j + tile)
            inner = nn(normed, wi[:, cols]) + ibias[:, cols]
            phi, bump = gelu_parts(inner)
            active[sl, cols] = (inner * phi).astype(BF16)
            slope[sl, cols] = (phi + bump).astype(BF16)
        if i == 1:
            for item in late:
                item.wait()
            if squared():
                tail.ready()
        if i:
            push(i - 1)
    push(seq - 1)
    for item in handed:
        item.wait_recv()
    cots = cot[...].reshape(rows, width)
    outer = folding(lambda to: upart.at[to], ugot, usend, urecv)

    def give_back():
        for i in range(seq):
            p_copy(i).wait_recv()
            out_own[i] = (
                resid[pl.ds(pl.multiple_of(i * chunk + c * half, 16), half), :]
                + precv[i].astype(F32)
            ).astype(BF16)
        back.start()

    if squared() and piece % 128 == 0:
        for n, chip in enumerate((outer.chips[2], outer.chips[0], outer.chips[1], m)):
            at = pl.ds(pl.multiple_of(chip * piece, 128), piece)
            upart[chip] = tn(active[:, at], cots).astype(BF16)
            for item in (outer.copies[0:2], outer.copies[2:3], outer.copies[3:4], [])[n]:
                item.start()
            if n == 0:
                give_back()
    else:
        for k in range(n_m):
            upart[k] = tn(active[:, k * piece : (k + 1) * piece], cots).astype(BF16)
        outer.start()
        give_back()
    gvec_out[0:1, :] = jnp.sum(cots.astype(F32), 0, keepdims=True)
    for i in range(seq):
        sl = block(i)
        g = cot[i].reshape(chunk, width)
        for j in range(0, hidden, piece):
            cols = slice(j, j + piece)
            gi = (nt(g, wu[j // piece]) * slope[sl, cols].astype(F32)).astype(BF16)
            slope[sl, cols] = gi
            line = jnp.sum(gi.astype(F32), 0, keepdims=True)
            if i == 0:
                gib_out[:, cols] = line
            else:
                gib_out[:, cols] += line
        gn2 = nt(slope[sl, :], wi[...])
        gown[sl, :] = gn2
        gstage[sl, :] = gn2.astype(BF16)
        g_copy(i).start()
        if i == 1:
            outer.turn()
    for j in range(0, hidden, tile):
        part = tn(n2[...], slope[:, j : j + tile])
        for k in range(n_m):
            for b in range(2):
                at = (2 * k + b) * share
                gwi_out[k, b, :, j : j + tile] = part[at : at + share, :].astype(BF16)
    wrows = pl.ds(pl.multiple_of(c * mine, 128), mine)
    for i in range(seq):
        sl = block(i)
        g_copy(i).wait_recv()
        gn2 = gown[sl, :] + grecv[sl, :].astype(F32)
        hat = hat2[sl, :]
        line = jnp.sum(gn2 * hat, 0, keepdims=True)
        flat = jnp.sum(gn2, 0, keepdims=True)
        g = cot[i].reshape(chunk, width).astype(F32)
        gres = g + norm_back(gn2, gain, hat, inv2[sl, 0:1])
        hat2[sl, :] = gres
        low = gres.astype(BF16)
        branch[sl, :] = low
        total = jnp.sum(low.astype(F32), 0, keepdims=True)
        if i == 0:
            lines, flats, totals = line, flat, total
        else:
            lines, flats, totals = lines + line, flats + flat, totals + total
        gm_out[sl, :] = nt(low, wo[wrows, :]).astype(BF16)
        gres_own[i] = hat2[pl.ds(pl.multiple_of(i * chunk + c * half, 16), half), :]
    gvec_out[1:2, :] = lines
    gvec_out[2:3, :] = flats
    gvec_out[3:4, :] = totals
    gvec_out[4:8, :] = jnp.zeros((4, width), F32)
    part = tn(
        mixed_rows(slice(None)),
        active[:, pl.ds(pl.multiple_of(width + c * mine, 128), mine)],
    )
    for k in range(n_m):
        for b in range(2):
            at = (2 * k + b) * share
            gwo_out[k, b] = part[at : at + share, :].astype(BF16)
    for i in range(seq):
        p_copy(i).wait_send()
        g_copy(i).wait_send()
        passes[i].wait_send()
    if squared():
        tail.finish()
    ru_out[...] = outer.total(upart[m]).astype(BF16).reshape(ru_out.shape)
    outer.finish()
    back.finish()


def dense(x, mixed, cot, wo, wi, wu, vecs, ibias):
    seq, _, half, width = x.shape
    rows = seq * 2 * half
    hidden = wi.shape[1]
    mine = width // 2
    n_f = lax.axis_size("fsdp")
    n_m = n_f // 2
    share = width // n_f
    piece = hidden // n_m
    return pl.pallas_call(
        lambda *refs: dense_kernel(seq, *refs),
        in_specs=[ANY] * 6 + [VMEM] * 2,
        out_specs=[ANY] + [VMEM] * 7,
        out_shape=[
            jax.ShapeDtypeStruct((2, 2, half, width), BF16),
            jax.ShapeDtypeStruct((seq, half, width), F32),
            jax.ShapeDtypeStruct((rows, mine), BF16),
            jax.ShapeDtypeStruct((n_m, 2, share, mine), BF16),
            jax.ShapeDtypeStruct((n_m, 2, share, hidden), BF16),
            jax.ShapeDtypeStruct((2, piece // 2, width), BF16),
            jax.ShapeDtypeStruct((8, width), F32),
            jax.ShapeDtypeStruct((1, hidden), F32),
        ],
        scratch_shapes=[
            pltpu.VMEM((2, 2, half, width), BF16),
            pltpu.VMEM(mixed.shape, BF16),
            pltpu.VMEM(cot.shape, BF16),
            pltpu.VMEM((width, width), BF16),
            pltpu.VMEM(wi.shape, BF16),
            pltpu.VMEM((n_m, piece, width), BF16),
            pltpu.VMEM((rows, width), BF16),
            pltpu.VMEM((rows, width), F32),
            pltpu.VMEM((rows, 128), F32),
            pltpu.VMEM((rows, width), F32),
            pltpu.VMEM((rows, hidden), BF16),
            pltpu.VMEM((rows, hidden), BF16),
            pltpu.VMEM((seq, half, width), BF16),
            pltpu.VMEM((seq, 2, half, width), BF16),
            pltpu.VMEM((seq, half, width), BF16),
            pltpu.VMEM((rows, width), BF16),
            pltpu.VMEM((n_m - 1, piece, width), BF16),
            pltpu.VMEM((n_m, piece, width), BF16),
            pltpu.SemaphoreType.DMA((seq,)),
            pltpu.SemaphoreType.DMA((seq,)),
            pltpu.SemaphoreType.DMA((seq,)),
            pltpu.SemaphoreType.DMA((seq,)),
        ]
        + RETURN_SEMS(seq)
        + scatter_sems()
        + [
            pltpu.SemaphoreType.DMA((6 + seq,)),
            pltpu.SemaphoreType.DMA((2,)),
            pltpu.SemaphoreType.DMA((seq,)),
            pltpu.SemaphoreType.DMA((seq,)),
            pltpu.SemaphoreType.DMA((7,)),
            pltpu.SemaphoreType.DMA((7,)),
            pltpu.SemaphoreType.DMA((2, n_m)),
        ],
        compiler_params=pltpu.CompilerParams(
            collective_id=2, has_side_effects=True, vmem_limit_bytes=LIMIT
        ),
        name="dense",
    )(x, mixed, cot, wo, wi, wu, vecs, ibias)


def back_kernel(seq, *refs):
    refs = list(refs)

    def take(n):
        got = refs[:n]
        del refs[:n]
        return got

    gwi, gwo, ru, q_in, k_in, v_in, gm_in, o_in, linv_in, e_in = take(10)
    n1_in, x_in, gres_in, wqkv_in, vecs, gvec, gib = take(7)
    gwu_out, w_out, gwi_out, vec_out, ib_out, ig_back = take(6)
    q, k, v, gm, o, linv, ebuf, n1, x, gres, wqkv, grads = take(12)
    do, dot_, qt, va, km, dvt, dkt = take(7)
    uown, uspare, ri, ispare, igot, ogot, ra, aspare, ito, ato = take(10)
    qpart, qgot, gstage, grecv, ig_own, vown, vspare, vgot, vto = take(9)
    isems, osems, qsems, vsems, gsems, bsems, pair_sems = [take(2) for _ in range(7)]
    zu, zi, za, zv, lsem, esem, wsem = take(7)
    gwiv, gwov = take(2)
    f, z, m, c = where_am_i()
    other = (m * 2 + 1 - c, z)
    rows, mine = q.shape
    half, width = gres.shape[1], gres.shape[2]
    chunk = 2 * half
    pairs = mine // 128
    n_m = gwi.shape[0]
    share, hidden = ri.shape[1], ri.shape[2]
    piece = hidden // n_m
    blocks = rows // QB

    def e_load(p, i):
        return pltpu.make_async_copy(e_in.at[p, i], ebuf.at[i], esem.at[i])

    first = [
        pltpu.make_async_copy(src, dst, lsem.at[n])
        for n, (src, dst) in enumerate(
            (
                (gwi, gwiv),
                (ru, uown),
                (gm_in, gm),
                (linv_in, linv),
                (o_in, o),
                (q_in, q),
                (k_in, k),
                (v_in, v),
                (gwo, gwov),
            )
        )
    ]
    later = [
        pltpu.make_async_copy(src, dst, lsem.at[len(first) + n])
        for n, (src, dst) in enumerate(((n1_in, n1), (gres_in, gres), (x_in.at[:, c], x)))
    ]
    for p in range(pairs):
        for t in range(3):
            later.append(
                pltpu.make_async_copy(
                    wqkv_in.at[:, pl.ds(t * mine + p * 128, 128)],
                    wqkv.at[:, pl.ds((3 * p + t) * 128, 128)],
                    wsem.at[p, t],
                )
            )
    for item in first:
        item.start()
    for i in range(blocks):
        e_load(0, i).start()
    for item in later:
        item.start()
    meet(all_peers(seq))

    outer = [Across(uown.at[n], uspare.at[n], zu.at[n]) for n in range(2)]
    inner = [Across(ri.at[n], ispare.at[n], zi.at[n]) for n in range(2)]
    parts = [Across(ra.at[n], aspare.at[n], za.at[n]) for n in range(4)]
    vectors = Across(vown, vspare, zv)
    inner_sums = [
        folding(lambda to, n=n: gwiv.at[to, n], igot.at[n], isems[0].at[n], isems[1].at[n])
        for n in range(2)
    ]
    out_sum = folding(lambda to: gwov.at[to], ogot, *osems)
    pair_sums = [
        folding(lambda to, n=n: qpart.at[n, to], qgot.at[n], qsems[0].at[n], qsems[1].at[n])
        for n in range(pairs)
    ]
    vector_sum = Scatter(lambda to: vown, vgot, *vsems)
    back = Return(ig_own, ig_back, *bsems, seq)

    def g_copy(i):
        return remote(
            gstage.at[i, 1 - c], grecv.at[i], gsems[0].at[i], gsems[1].at[i], other
        )

    def pass_on(n, src, dst):
        return remote(src, dst, pair_sems[0].at[n], pair_sems[1].at[n], other)

    def summed(n):
        ri[n] = inner_sums[n].total(gwiv[m, n]).astype(BF16)
        inner[n].rise()

    for item in first[:2]:
        item.wait()
    inner_sums[0].start()
    outer[0].rise()
    for item in first[2:]:
        item.wait()

    def part_sum(n):
        if n == 3:
            ra[3] = out_sum.total(gwov[m]).astype(BF16)
        else:
            ra[n] = pair_sums[n].total(qpart[n, m]).astype(BF16)
        parts[n].rise()

    def event_1():
        for item in later:
            item.wait()
        outer[0].risen()
        outer[0].cross()
        outer[1].rise()
        inner_sums[0].turn()
        inner_sums[1].start()

    def event_2():
        outer[0].crossed()
        outer[0].fall()
        outer[1].risen()
        outer[1].cross()
        summed(0)

    def event_3():
        inner[0].risen()
        inner[0].cross()
        outer[1].crossed()
        outer[1].fall()
        out_sum.start()

    def event_4():
        summed(1)
        out_sum.turn()
        pair_sums[0].start()

    def event_5():
        inner[0].crossed()
        inner[0].fall()
        part_sum(3)
        pair_sums[0].turn()
        pair_sums[1].start()

    def event_6():
        inner[1].risen()
        inner[1].cross()
        part_sum(0)
        pair_sums[1].turn()
        parts[3].risen()
        parts[3].cross()

    events = {
        0: [(2, event_4)],
        2: [(1, event_2)],
        4: [(1, inner_sums[1].turn), (2, event_5)],
        8: [(0, event_1), (1, event_3), (2, event_6)],
    }
    third = HD ** (-0.5)
    lane = lax.broadcasted_iota(jnp.int32, (1, 128), 1)
    low = lane < HD
    steps = [(i, a) for i in range(blocks) for a in range(2)]

    def block(i):
        return slice(i * QB, (i + 1) * QB)

    def sub(a):
        return slice(a * HD, (a + 1) * HD)

    def heads(pair, _):
        for when, action in events[0]:
            pl.when(pair == when)(action)
        here = pl.ds(pl.multiple_of(pair * 128, 128), 128)

        def spot(t):
            return pl.ds(pl.multiple_of((3 * pair + t) * 128, 128), 128)

        scaled = (gm[:, here].astype(F32) * linv[:, here]).astype(BF16).astype(F32)
        kf, vf = k[:, here].astype(F32), v[:, here].astype(F32)
        weighted = scaled * o[:, here]
        for a in range(2):
            own = low if a == 0 else jnp.logical_not(low)
            delta = jnp.sum(jnp.where(own, weighted, 0.0), -1, keepdims=True)
            high = delta.astype(BF16).astype(F32)
            middle = (delta - high).astype(BF16).astype(F32)
            last = delta - high - middle
            base = HD * (1 - a)
            extra = jnp.where(
                lane == base,
                high,
                jnp.where(lane == base + 1, middle, jnp.where(lane == base + 2, last, 0.0)),
            )
            do[a] = jnp.where(own, scaled, -extra).astype(BF16)
            va[a] = jnp.where(own, vf, 1.0).astype(BF16)
            km[a] = jnp.where(own, kf, 0.0).astype(BF16)
        dot_[...] = scaled.astype(BF16).T
        qt[...] = q[:, here].T

        def pushed(t):
            i, a = steps[t]
            return nt(do[a, block(i), :], va[a])

        dqs = {}
        upcoming = jnp.minimum(pair + 1, pairs - 1)
        push = pushed(0)
        for t, (i, a) in enumerate(steps):
            for when, action in events.get(t, []) if t else []:
                pl.when(pair == when)(action)
            if a == 0:
                e_load(pair, i).wait()
            sl = block(i)
            p = ebuf[i, a]
            ds = (p.astype(F32) * push).astype(BF16)
            push = pushed(t + 1) if t + 1 < len(steps) else None
            dv = nn(dot_[sub(a), sl], p)
            dk = nn(qt[sub(a), sl], ds)
            dqs[a] = nn(ds, km[a])
            if i == 0:
                dvt[sub(a), :] = dv
                dkt[sub(a), :] = dk
            else:
                dvt[sub(a), :] += dv
                dkt[sub(a), :] += dk
            if a == 1:
                e_load(upcoming, i).start()
                grads[sl, spot(0)] = ((dqs[0] + dqs[1]) * third).astype(BF16)
        grads[:, spot(1)] = (dkt[...] * third).astype(BF16).T
        grads[:, spot(2)] = dvt[...].astype(BF16).T
        cols = pl.ds(pl.multiple_of(3 * pair * 128, 128), 3 * 128)
        part = tn(n1[...], grads[:, cols])
        for j in range(n_m):
            for b in range(2):
                at = (2 * j + b) * share
                qpart[pair, j, b] = part[at : at + share, :].astype(BF16)
        return 0

    lax.fori_loop(0, pairs, heads, 0)
    pair_sums[2].start()
    part_sum(1)
    parts[0].risen()
    parts[0].cross()
    for i in range(blocks):
        e_load(pairs - 1, i).wait()
    for i in range(seq):
        sl = slice(i * chunk, (i + 1) * chunk)
        gn1 = nt(grads[sl, :], wqkv[...])
        o[sl, :] = gn1[:, :mine]
        linv[sl, :] = gn1[:, mine:]
        gstage[i] = gn1.astype(BF16).reshape(2, half, width)
        g_copy(i).start()
    pair_sums[2].turn()
    inner[1].crossed()
    inner[1].fall()
    parts[1].risen()
    parts[1].cross()
    parts[3].crossed()
    parts[3].fall()
    vown[...] = jnp.zeros_like(vown)
    for p in range(pairs):
        cols = pl.ds(pl.multiple_of(c * mine + p * 128, 128), 128)
        for r, t in ((2, 0), (3, 2)):
            at = (3 * p + t) * 128
            vown[r : r + 1, cols] = jnp.sum(
                grads[:, at : at + 128].astype(F32), 0, keepdims=True
            )
    for n, r in enumerate((3, 1, 2, 0)):
        vown[4 + n : 5 + n, :] = 0.5 * gvec[r : r + 1, :]
    lines = hidden // width
    for n in range(lines):
        vown[pl.ds(8 + lines * c + n, 1), :] = gib[:, n * width : (n + 1) * width]
    gain = vecs[0:1, :]
    for i in range(seq):
        g_copy(i).wait_recv()
        sl = pl.ds(pl.multiple_of(i * chunk + c * half, 16), half)
        gn1 = jnp.concatenate([o[sl, :], linv[sl, :]], axis=1) + grecv[i].astype(F32)
        hat, inv = normalize(x[i].astype(F32))
        line = jnp.sum(gn1 * hat, 0, keepdims=True)
        flat = jnp.sum(gn1, 0, keepdims=True)
        if i == 0:
            gain_sum, shift_sum = line, flat
        else:
            gain_sum, shift_sum = gain_sum + line, shift_sum + flat
        ig_own[i] = (gres[i] + norm_back(gn1, gain, hat, inv)).astype(BF16)
        back.ships[i].start()
        if i == seq // 2:
            part_sum(2)
            parts[0].crossed()
            parts[0].fall()
    parts[2].risen()
    parts[2].cross()
    parts[1].crossed()
    parts[1].fall()
    vown[0:1, :] = gain_sum
    vown[1:2, :] = shift_sum
    vector_sum.start()
    total = vector_sum.total(vown[...])
    vector_sum.finish()
    vown[...] = total
    vectors.rise()
    parts[2].crossed()
    parts[2].fall()
    vectors.risen()
    vectors.cross()
    outer[0].fallen()
    outer[1].fallen()
    gwu_out[...] = uown[...]
    inner[0].fallen()
    crosses = {}

    def hand_over(n, src, dst):
        crosses[n] = pass_on(n, src, dst)
        crosses[n].start()

    for n in range(2):
        if n:
            inner[n].fallen()
        pl.when(c != n)(pass_on(n, ri.at[n], ito).start)
    parts[3].fallen()
    hand_over(5, ra.at[3, 1 - c], ato.at[3])
    parts[0].fallen()
    hand_over(2, ra.at[0, 1 - c], ato.at[0])
    vectors.crossed()
    vectors.fall()
    for n in range(2):
        pl.when(c == n)(pass_on(n, ri.at[1 - n], ito).wait_recv)
        pl.when(c != n)(pass_on(n, ri.at[n], ito).wait_send)
    if piece % 128:
        gwi_out[c] = ri[c]
        gwi_out[1 - c] = ito[...]
    else:
        for n in range(n_m):
            cols = slice(n * piece, (n + 1) * piece)
            here = pl.ds(pl.multiple_of((2 * n + c) * piece, 128), piece)
            there = pl.ds(pl.multiple_of((2 * n + 1 - c) * piece, 128), piece)
            gwi_out[:, here] = ri[c, :, cols]
            gwi_out[:, there] = ito[:, cols]
    for p in (1, 2):
        parts[p].fallen()
        hand_over(2 + p, ra.at[p, 1 - c], ato.at[p])
    here = pl.ds(pl.multiple_of(c * mine, 128), mine)
    there = pl.ds(pl.multiple_of((1 - c) * mine, 128), mine)
    crosses[5].wait()
    w_out[3, :, here] = ra[3, c]
    w_out[3, :, there] = ato[3]
    for p in range(pairs):
        crosses[2 + p].wait()
        here = pl.ds(pl.multiple_of(c * mine + p * 128, 128), 128)
        there = pl.ds(pl.multiple_of((1 - c) * mine + p * 128, 128), 128)
        for t in range(3):
            w_out[t, :, here] = ra[p, c, :, t * 128 : (t + 1) * 128]
            w_out[t, :, there] = ato[p, :, t * 128 : (t + 1) * 128]
    vectors.fallen()
    hand_over(6, vown, vto)
    crosses[6].wait()
    vto[...] = vown[...] + vto[...]
    turned = pltpu.roll(vto[0:8, :], (width - f * share) % width, 1)
    vec_out[...] = turned[:, :share]
    per = width // piece
    line = jnp.broadcast_to(vto[pl.ds(8 + lines * c + m // per, 1), :], (8, width))
    ib_out[...] = pltpu.roll(line, (width - (m % per) * piece) % width, 1)[0:1, :piece]
    for i in range(seq):
        g_copy(i).wait_send()
    for item in inner_sums + [out_sum] + pair_sums:
        item.finish()
    back.finish()


def back(gwi, gwo, ru, q, k, v, gm, o, linv, e, n1, x, gres, wqkv, vecs, gvec, gib):
    seq, _, half, width = x.shape
    n_m, _, share, hidden = gwi.shape
    rows, mine = q.shape
    pairs = mine // 128
    piece = hidden // n_m
    block = (2, share, mine)
    assert pairs == 3 and seq == 4

    def sems(*shape):
        return pltpu.SemaphoreType.DMA(shape)

    def two(*shape):
        return [sems(*shape), sems(*shape)]

    return pl.pallas_call(
        lambda *refs: back_kernel(seq, *refs),
        in_specs=[ANY] * 14 + [VMEM] * 3,
        out_specs=[VMEM] * 5 + [ANY],
        out_shape=[
            jax.ShapeDtypeStruct(ru.shape, BF16),
            jax.ShapeDtypeStruct((4, share, width), BF16),
            jax.ShapeDtypeStruct(
                (2, share, hidden) if piece % 128 else (share, 2 * hidden), BF16
            ),
            jax.ShapeDtypeStruct((8, share), F32),
            jax.ShapeDtypeStruct((1, piece), F32),
            jax.ShapeDtypeStruct((2, 2, half, width), BF16),
        ],
        scratch_shapes=[
            pltpu.VMEM((rows, mine), BF16),
            pltpu.VMEM((rows, mine), BF16),
            pltpu.VMEM((rows, mine), BF16),
            pltpu.VMEM((rows, mine), BF16),
            pltpu.VMEM((rows, mine), F32),
            pltpu.VMEM((rows, mine), F32),
            pltpu.VMEM(e.shape[1:], BF16),
            pltpu.VMEM((rows, width), BF16),
            pltpu.VMEM((seq, half, width), BF16),
            pltpu.VMEM((seq, half, width), F32),
            pltpu.VMEM(wqkv.shape, BF16),
            pltpu.VMEM((rows, 3 * mine), BF16),
            pltpu.VMEM((2, rows, 128), BF16),
            pltpu.VMEM((128, rows), BF16),
            pltpu.VMEM((128, rows), BF16),
            pltpu.VMEM((2, rows, 128), BF16),
            pltpu.VMEM((2, rows, 128), BF16),
            pltpu.VMEM((128, rows), F32),
            pltpu.VMEM((128, rows), F32),
            pltpu.VMEM(ru.shape, BF16),
            pltpu.VMEM((2,) + ru.shape, BF16),
            pltpu.VMEM((2, share, hidden), BF16),
            pltpu.VMEM((2, 2, share, hidden), BF16),
            pltpu.VMEM((2, n_m - 1, share, hidden), BF16),
            pltpu.VMEM((n_m - 1,) + block, BF16),
            pltpu.VMEM((4,) + block, BF16),
            pltpu.VMEM((4, 2) + block, BF16),
            pltpu.VMEM((share, hidden), BF16),
            pltpu.VMEM((4, share, mine), BF16),
            pltpu.VMEM((pairs, n_m) + block, BF16),
            pltpu.VMEM((pairs, n_m - 1) + block, BF16),
            pltpu.VMEM((seq, 2, half, width), BF16),
            pltpu.VMEM((seq, half, width), BF16),
            pltpu.VMEM((seq, half, width), BF16),
            pltpu.VMEM((16, width), F32),
            pltpu.VMEM((2, 16, width), F32),
            pltpu.VMEM((n_m - 1, 16, width), F32),
            pltpu.VMEM((16, width), F32),
        ]
        + two(2, max(n_m, 6))
        + two(max(n_m, 6))
        + two(pairs, max(n_m, 6))
        + two(n_m)
        + two(seq)
        + RETURN_SEMS(seq)
        + two(7)
        + [sems(2, 6), sems(2, 6), sems(4, 6), sems(6), sems(12), sems(rows // QB)]
        + [sems(pairs, 3), pltpu.VMEM(gwi.shape, BF16), pltpu.VMEM(gwo.shape, BF16)],
        compiler_params=pltpu.CompilerParams(
            collective_id=3, has_side_effects=True, vmem_limit_bytes=LIMIT
        ),
        name="back",
    )(gwi, gwo, ru, q, k, v, gm, o, linv, e, n1, x, gres, wqkv, vecs, gvec, gib)


def widen_kernel(w, gwi, gwu, vec, ib, *outs):
    for k in range(4):
        outs[k][...] = w[k].astype(F32)
    outs[4][...] = gwi[...].astype(F32)
    outs[5][...] = gwu[...].astype(F32)
    outs[6][...] = ib[...]
    for k in range(8):
        outs[7 + k][...] = vec[k : k + 1, :]


def widen(w, gwi, gwu, vec, ib):
    square = jax.ShapeDtypeStruct(w.shape[1:], F32)
    return pl.pallas_call(
        widen_kernel,
        in_specs=[VMEM] * 5,
        out_specs=[VMEM] * 15,
        out_shape=[square] * 4
        + [jax.ShapeDtypeStruct(value.shape, F32) for value in (gwi, gwu, ib)]
        + [jax.ShapeDtypeStruct((1, vec.shape[1]), F32)] * 8,
        compiler_params=pltpu.CompilerParams(vmem_limit_bytes=LIMIT),
        name="widen",
    )(w, gwi, gwu, vec, ib)


def per_device(
    frames,
    cotangent,
    valid_slots,
    first_gain,
    first_shift,
    query_weight,
    query_bias,
    key_weight,
    value_weight,
    value_bias,
    output_weight,
    output_bias,
    second_gain,
    second_shift,
    inner_weight,
    inner_bias,
    outer_weight,
    outer_bias,
):
    seq = lax.axis_size("seq")
    n_f = lax.axis_size("fsdp")
    f = lax.axis_index("fsdp")
    m, c = f // 2, f % 2
    slots, local, width = frames.shape
    chunk = -(-local // 128) * 128
    half = chunk // 2
    mine = width // 2
    share = width // n_f
    piece = inner_bias.shape[0]
    hidden = piece * n_f // 2

    keep = valid_slots.astype(BF16)[:, None, None]
    pad = ((0, 0), (0, chunk - local), (0, 0))
    x_send = jnp.pad(frames, pad).reshape(slots, 2, half, width)
    cot_send = jnp.pad(cotangent * keep, pad).reshape(slots, 2, half, width)
    vectors = (
        first_gain,
        first_shift,
        query_bias,
        value_bias,
        output_bias,
        second_gain,
        second_shift,
        outer_bias,
    )
    if share % 16 == 0 and piece % 128 == 0:
        rest = [query_weight, key_weight, value_weight, inner_weight]
        rest += [value[None] for value in vectors] + [inner_bias.astype(F32)[None]]
        *kept, wqkv, wi, vecs, ibias = front(
            x_send, cot_send, output_weight, outer_weight, rest, local, seq, True
        )
        wqkv = wqkv.reshape(width, 3 * mine)
        wi = wi.reshape(width, hidden)
    else:

        def gathered(value, axis=0):
            return lax.all_gather(value, "fsdp", axis=axis, tiled=True)

        def my_columns(value):
            return lax.dynamic_slice_in_dim(value, c * mine, mine, axis=1)

        wqkv = jnp.concatenate(
            [my_columns(gathered(w)) for w in (query_weight, key_weight, value_weight)], axis=1
        )
        wi = gathered(inner_weight).reshape(width, n_f // 2, 2, piece)
        wi = lax.dynamic_index_in_dim(wi, c, 2, keepdims=False).reshape(width, hidden)
        vecs = gathered(jnp.stack(vectors), 1).astype(F32)
        ibias = gathered(inner_bias).astype(F32).reshape(n_f // 2, 2, piece)
        ibias = lax.dynamic_index_in_dim(ibias, c, 1, keepdims=False).reshape(1, hidden)
        kept = front(
            x_send, cot_send, output_weight, outer_weight, [wqkv, vecs], local, seq, False
        )

    x, n1, q, k, v, e, o, linv, mixed, cot, wo, wu = kept
    if share % 16:
        wo = wo.transpose(1, 0, 2, 3).reshape(width, width)
    out_back, gres, gm, gwo, gwi, ru, gvec, gib = dense(x, mixed, cot, wo, wi, wu, vecs, ibias)
    gwu, w, gwi, vec, ib, ig_back = back(
        gwi, gwo, ru, q, k, v, gm, o, linv, e, n1, x, gres, wqkv, vecs, gvec, gib
    )
    if gwi.ndim == 3:
        gwi = gwi.reshape(2, share, n_f // 2, piece).transpose(1, 2, 0, 3)
        gwi = gwi.reshape(share, 2 * hidden)
    gwq, gwk, gwv, gwo, gwi, gwu, ib, fg, fs, qb, vb, ob, sg, ss, ub = widen(
        w, gwi, gwu.reshape(piece, width), vec, ib
    )
    keep32 = valid_slots.astype(F32)[:, None, None]
    outputs = (out_back.reshape(slots, chunk, width)[:, :local].astype(F32) * keep32).astype(BF16)
    input_grad = ig_back.reshape(slots, chunk, width)[:, :local]
    return (
        outputs,
        input_grad,
        fg[0],
        fs[0],
        gwq,
        qb[0],
        gwk,
        gwv,
        vb[0],
        gwo,
        ob[0],
        sg[0],
        ss[0],
        gwi,
        ib.reshape(piece),
        gwu,
        ub[0],
    )


def solution(mesh):
    rows = P("fsdp", "seq", None)
    vector, matrix = P("fsdp"), P("fsdp", None)
    weights = (
        vector,
        vector,
        matrix,
        vector,
        matrix,
        matrix,
        vector,
        matrix,
        vector,
        vector,
        vector,
        matrix,
        vector,
        matrix,
        vector,
    )
    return jax.shard_map(
        per_device,
        mesh=mesh,
        in_specs=(rows, rows, vector) + weights,
        out_specs=(rows, rows) + weights,
        check_vma=False,
    )
```
